32 devices in a mesh: gx: 4 (over y, x), gy: 8 (over z, core).
Axes of the slice: x: 2, y: 2, z: 4, core: 2. Of those that a mesh axis runs over, the one named last changes fastest.
Arguments:
- velocity: float32 [3, 1536, 32, 512], P(None, 'gy', None, 'gx'), may hold values from -6 to 6
- old_advection: float32 [3, 1536, 32, 512], P(None, 'gy', None, 'gx'), may hold values from -12 to 12
- lower_gap: float32 [1536], P('gy'), may hold values from 0.35 to 1.4
- upper_gap: float32 [1536], P('gy'), may hold values from 0.35 to 1.4, as said below
Outputs:
- new_velocity: float32 [3, 1536, 32, 512], P(None, 'gy', None, 'gx')
- advection: float32 [3, 1536, 32, 512], P(None, 'gy', None, 'gx')
The draws below stay inside these ranges and needn't reach their ends.
Inputs may be any that keep to these rules, and one draw needn't show every extreme that they name: upper_gap of every point equals lower_gap of the next point.
All inputs are finite; a program needn't handle non-finite values.
Results may differ from the reference program's by a relative error of at most 0.0075.
Values sent between devices are 32-bit elements; how exact they have to be, the bound alone decides.
No kernel may reach another device: no remote copies, remote signals or barrier semaphores. Data moves between devices by JAX's collectives and lax.ppermute only.
A program may use at most 256 MiB of HBM per device.

```python
import jax
import jax.numpy as jnp
from jax import lax

NY = 1536
NZ = 32
NX = 512
STIFF = 1024


def gap_table(key):
    sub_key = jax.random.fold_in(key, 7)
    points = NY + 1
    position = jnp.arange(points, dtype=jnp.float32)
    profile = jnp.sin(jnp.pi * (position + 0.5) / points)
    roughness = jnp.exp(jax.random.uniform(sub_key, (points,), jnp.float32, jnp.log(0.7), jnp.log(1.4)))
    return (0.5 * jnp.exp(profile * jnp.log(2.0)) * roughness).astype(jnp.float32)


def draw_lower_gap(key, part):
    return gap_table(key)[:NY]


def draw_upper_gap(key, part):
    return gap_table(key)[1:]


def draw_velocity(key, part):
    shape = (3, NY, NZ, NX)
    values = jnp.clip(jax.random.normal(key, shape, jnp.float32), -6.0, 6.0)
    return values.astype(jnp.float32)


def steps_of(key, dims, cuts, least, high):
    def one(dim, blocks):
        draws = jax.random.uniform(jax.random.fold_in(jax.random.fold_in(key, 6), dim), (blocks,), jnp.float32, least / len(cuts), high / len(cuts))
        return jnp.repeat(jnp.exp(draws), dims[dim] // blocks).reshape((-1,) + (1,) * (len(dims) - dim - 1))

    gain = one(*cuts[0])
    for cut in cuts[1:]:
        gain = gain * one(*cut)
    return gain


def noise(key, shape, deviation, bound, cuts=(), kind=jnp.bfloat16):
    loudness = steps_of(key, shape, cuts, -0.22, 0.18) if cuts else 1.0
    result = jax.random.normal(key, shape, jnp.float32) * deviation * loudness
    return jnp.minimum(jnp.maximum(result, -bound), bound).astype(kind)


def setup_inputs(seed: int = 0) -> dict:
    splits = jax.random.split(jax.random.key(seed), 5)
    return {
        "velocity": draw_velocity(jax.random.fold_in(splits[4], 71), 0),
        "old_advection": noise(splits[1], (3, NY, NZ, NX), 2.0, 12.0, ((1, 8), (3, 4)), jnp.float32),
        "lower_gap": draw_lower_gap(jax.random.fold_in(splits[4], 71), 0),
        "upper_gap": draw_upper_gap(jax.random.fold_in(splits[4], 71), 0),
    }


STENCIL = (0.8, -0.2, 4.0 / 105.0, -1.0 / 280.0)
GAMMA = 5.0 / 12.0
ZETA = -17.0 / 60.0

def roll_slope(values, along_axis):
    summed = STENCIL[0] * (jnp.roll(values, -1, along_axis) - jnp.roll(values, 1, along_axis))
    for offset in range(2, 5):
        summed = summed + STENCIL[offset - 1] * (jnp.roll(values, -offset, along_axis) - jnp.roll(values, offset, along_axis))
    return summed

def reference(velocity, old_advection, lower_gap, upper_gap):
    gap_sum = lower_gap + upper_gap

    def advect(component):
        stream = roll_slope(component, 2)
        spanwise = roll_slope(component, 1)
        padded = jnp.pad(component, ((1, 1), (0, 0), (0, 0)))
        normal_slope = (padded[2:] - padded[:-2]) / gap_sum[:, None, None]
        return -(velocity[0] * stream + velocity[1] * normal_slope + velocity[2] * spanwise)
    advection = lax.map(advect, velocity)
    forcing = velocity + GAMMA * advection + ZETA * old_advection
    lower_coef = -2.0 * STIFF / (gap_sum * lower_gap)
    upper_coef = -2.0 * STIFF / (gap_sum * upper_gap)
    diagonal = 1.0 - lower_coef - upper_coef
    below_band = lower_coef.at[0].set(0.0)
    above_band = upper_coef.at[-1].set(0.0)
    stacked = forcing.reshape(3, NY, -1)
    solved = lax.linalg.tridiagonal_solve(jnp.stack([below_band] * 3), jnp.stack([diagonal] * 3), jnp.stack([above_band] * 3), stacked)
    new_velocity = solved.reshape(forcing.shape)
    return (new_velocity, advection)
```

```python
import functools
import math

import jax
import jax.numpy as jnp
import numpy as np
from jax import lax
from jax.experimental import pallas as pl
from jax.experimental.pallas import tpu as pltpu
from jax.sharding import PartitionSpec as P

STIFF = 1024
GAMMA = 5.0 / 12.0
ZETA = -17.0 / 60.0
WEIGHTS = (672.0, -168.0, 32.0, -3.0)
UNIT = 1.0 / 840.0
F32 = jnp.float32
BF16 = jnp.bfloat16
MIB = 1 << 20

INV_GAP, FORWARD, BACKWARD, PSI, PHI = range(5)


def shift_matrix(size, periodic):
    m = np.zeros((size, size), np.float32)
    for j in range(size):
        for k, w in enumerate(WEIGHTS, 1):
            for i, s in ((j + k, w), (j - k, -w)):
                if periodic:
                    m[i % size, j] += s
                elif 0 <= i < size:
                    m[i, j] += s
    return m


def edge_matrices():
    left, right = np.zeros((4, 4), np.float32), np.zeros((4, 4), np.float32)
    for l in range(4):
        for m in range(4):
            if m >= l:
                left[m, l] = -WEIGHTS[l + 3 - m]
            if m <= l:
                right[m, l] = WEIGHTS[m + 3 - l]
    return np.kron(np.eye(32), left), np.kron(np.eye(32), right)


def lanes(shape):
    return lax.broadcasted_iota(jnp.int32, shape, len(shape) - 1)


def split(values):
    hi = values.astype(BF16)
    return hi, (values - hi.astype(F32)).astype(BF16)


def pack_kernel(group, v_ref, left_ref, right_ref):
    lane = lanes((8, 128))
    low = (lane & 7) < 4
    slot = lane >> 3
    for c in range(3):
        for g in range(v_ref.shape[1] // group):
            halves = [jnp.zeros((8, 128), F32), jnp.zeros((8, 128), F32)]
            for yl in range(group):
                for zt in range(4):
                    s = zt * 4 + yl // 2
                    tile = v_ref[c, g * group + yl, 8 * zt : 8 * zt + 8, :]
                    turned = pltpu.roll(tile, (8 * s + 4) % 128, 1)
                    halves[yl % 2] = jnp.where(slot == s, turned, halves[yl % 2])
            even, odd = halves
            right_ref[c, g] = jnp.where(low, even, pltpu.roll(odd, 4, 1))
            left_ref[c, g] = jnp.where(low, pltpu.roll(even, 124, 1), odd)


def interleave(left, right):
    low = (lanes((8, 128)) & 7) < 4
    even = jnp.where(low, right, pltpu.roll(left, 4, 1))
    odd = jnp.where(low, pltpu.roll(right, 124, 1), left)
    return even, odd


def pack(velocity, group, block):
    n = velocity.shape[1]
    packed = jax.ShapeDtypeStruct((3, n // group, 8, 128), F32)
    out = pl.BlockSpec((3, block // group, 8, 128), lambda i: (0, i, 0, 0))
    return pl.pallas_call(
        functools.partial(pack_kernel, group),
        grid=(n // block,),
        in_specs=[pl.BlockSpec((3, block, 32, 128), lambda i: (0, i, 0, 0))],
        out_specs=[out, out],
        out_shape=[packed, packed],
        name="pack_edges",
    )(velocity)


def coef_kernel(n, lower_ref, upper_ref, kappa_ref, inv_ref, out_ref):
    def up(i, state):
        phi, flux = state
        out_ref[PHI, i] = phi
        out_ref[FORWARD, i] = phi * kappa_ref[i]
        out_ref[INV_GAP, i] = inv_ref[i]
        flux = flux + kappa_ref[i] * phi
        return phi + upper_ref[i] * flux, flux

    def down(k, state):
        i = n - 1 - k
        psi, flux = state
        out_ref[PSI, i] = psi
        out_ref[BACKWARD, i] = psi * kappa_ref[i]
        flux = flux + kappa_ref[i] * psi
        return psi + lower_ref[i] * flux, flux

    def both(i, state):
        return up(i, state[0]), down(i, state[1])

    start = ((lower_ref[0], jnp.float32(1.0)), (upper_ref[n - 1], jnp.float32(1.0)))
    (wronskian, _), _ = lax.fori_loop(0, n, both, start, unroll=4)
    scale = (1.0 / jnp.full((8, 128), wronskian, F32))[0, 0]

    def norm(i, _):
        out_ref[PHI, i] = out_ref[PHI, i] * scale
        out_ref[PSI, i] = out_ref[PSI, i] * scale
        return 0

    lax.fori_loop(0, n, norm, 0, unroll=4)


def smem():
    return pl.BlockSpec(memory_space=pltpu.SMEM)


def vmem():
    return pl.BlockSpec(memory_space=pltpu.VMEM)


def coefs(lower_gap, upper_gap):
    n = lower_gap.shape[0]
    gap_sum = lower_gap + upper_gap
    return pl.pallas_call(
        functools.partial(coef_kernel, n),
        in_specs=[smem()] * 4,
        out_specs=smem(),
        out_shape=jax.ShapeDtypeStruct((5, n), F32),
        name="coefficients",
    )(lower_gap, upper_gap, gap_sum * (0.5 / STIFF), 1.0 / gap_sum)


def main_kernel(n, block, group, co, v_ref, before_ref, after_ref, below_ref, above_ref, old_ref,
                dx_ref, dz_ref, adv_ref, u_ref, a_ref, b_ref, f_ref):
    step = pl.program_id(0)
    steps = pl.num_programs(0)

    @pl.when(step == 0)
    def _():
        a_ref[...] = jnp.zeros_like(a_ref)

    rows = group * 32

    def chunk(k, _):
        y0 = k * group
        first = jnp.logical_and(step == 0, k == 0)
        last = jnp.logical_and(step == steps - 1, k == block // group - 1)
        inner = pl.ds(y0, group)
        vel = [v_ref[c, inner].reshape(rows, 128) for c in range(3)]
        for c in range(3):
            f = vel[c]
            pair = jnp.concatenate(split(f), axis=1)
            along_x = jnp.dot(pair, dx_ref[...], preferred_element_type=F32)
            both = jnp.dot(dz_ref[...], pair, preferred_element_type=F32)
            along_z = both[:, :128] + both[:, 128:]
            below = jnp.where(k == 0, before_ref[c, 0], v_ref[c, jnp.maximum(y0 - 1, 0)])
            below = jnp.where(first, below_ref[c, 0], below)
            above = jnp.where(k == block // group - 1, after_ref[c, 0],
                              v_ref[c, jnp.minimum(y0 + group, block - 1)])
            above = jnp.where(last, above_ref[c, 0], above)
            acc = a_ref[c]
            for y in range(group):
                here = slice(32 * y, 32 * y + 32)
                i = step * block + y0 + y
                under = below if y == 0 else f[32 * y - 32 : 32 * y]
                over = above if y == group - 1 else f[32 * y + 32 : 32 * y + 64]
                flat = (vel[0][here] * along_x[here] + vel[2][here] * along_z[here]) * (-UNIT)
                adv = flat - vel[1][here] * ((over - under) * co[INV_GAP, i])
                force = f[here] + GAMMA * adv + ZETA * old_ref[c, y0 + y]
                acc = acc + co[FORWARD, i] * force
                adv_ref[c, i] = adv
                f_ref[c, i] = force
                u_ref[c, i] = co[PSI, i] * acc
            a_ref[c] = acc
        return 0

    lax.fori_loop(0, block // group, chunk, 0)

    @pl.when(step == steps - 1)
    def _():
        b_ref[...] = jnp.zeros_like(b_ref)

        def back(k, _):
            for c in range(3):
                acc = b_ref[c]
                for y in range(group):
                    i = n - 1 - k * group - y
                    u_ref[c, i] = u_ref[c, i] + co[PHI, i] * acc
                    acc = acc + co[BACKWARD, i] * f_ref[c, i]
                b_ref[c] = acc
            return 0

        lax.fori_loop(0, n // group, back, 0)


def main_part(velocity, below, above, old, table, group, block):
    n = velocity.shape[1]
    dx = shift_matrix(128, False)
    dx = jnp.asarray(np.concatenate([dx, dx]), BF16)
    dz = jnp.asarray(np.kron(np.eye(group), shift_matrix(32, True).T), BF16)
    tile = pl.BlockSpec((3, block, 32, 128), lambda i: (0, i, 0, 0))
    kernel = functools.partial(main_kernel, n, block, group)

    def body(v, before, after, lo, hi, old, co, dx, dz, *rest):
        kernel(co, v, before, after, lo, hi, old, dx, dz, *rest)

    return pl.pallas_call(
        body,
        grid=(n // block,),
        in_specs=[
            tile,
            pl.BlockSpec((3, 1, 32, 128), lambda i: (0, jnp.maximum(i * block - 1, 0), 0, 0)),
            pl.BlockSpec((3, 1, 32, 128), lambda i: (0, jnp.minimum(i * block + block, n - 1), 0, 0)),
            pl.BlockSpec((3, 1, 32, 128), lambda i: (0, 0, 0, 0)),
            pl.BlockSpec((3, 1, 32, 128), lambda i: (0, 0, 0, 0)),
            tile,
            smem(),
            pl.BlockSpec(dx.shape, lambda i: (0, 0)),
            pl.BlockSpec(dz.shape, lambda i: (0, 0)),
        ],
        out_specs=[vmem()] * 4,
        out_shape=[
            pltpu.VMEM((3, n, 32, 128), F32),
            pltpu.VMEM((3, n, 32, 128), F32),
            pltpu.VMEM((3, 32, 128), F32),
            pltpu.VMEM((3, 32, 128), F32),
        ],
        scratch_shapes=[pltpu.VMEM((3, n, 32, 128), F32)],
        compiler_params=pltpu.CompilerParams(vmem_limit_bytes=24 * MIB),
        name="inner_part",
    )(velocity, velocity, velocity, below, above, old, table, dx, dz)


def edge_kernel(groups, group, co, from_left, from_right, left_ref, right_ref, a_ref, b_ref,
                ml_ref, mr_ref, adv_l, adv_r, u_l, u_r, load_ref, table_ref):
    n = groups * group
    lane = lanes((8, 128))
    place = (lane & 31) >> 2

    def weights(g, _):
        for t, row in enumerate((FORWARD, BACKWARD, PSI, PHI)):
            value = jnp.zeros((8, 128), F32)
            for yl in range(group):
                value = jnp.where(place == yl, co[row, g * group + yl], value)
            table_ref[t, g] = value
        return 0

    lax.fori_loop(0, groups, weights, 0)

    sides = (
        (from_left, ml_ref, left_ref, adv_l, u_l),
        (from_right, mr_ref, right_ref, adv_r, u_r),
    )
    totals = []
    for halo, matrix, own, adv, u in sides:
        for c in range(3):
            hi, lo = split(halo[c].reshape(groups * 8, 128))
            slope = jnp.dot(hi, matrix[...], preferred_element_type=F32)
            slope = slope + jnp.dot(lo, matrix[...], preferred_element_type=F32)
            adv[c] = (own[0].reshape(groups * 8, 128) * slope * (-UNIT)).reshape(groups, 8, 128)

            def forward(g, carry):
                part = table_ref[0, g] * (GAMMA * adv[c, g])
                for s in (1, 2, 4):
                    part = part + jnp.where(place >= s, pltpu.roll(part, 4 * s, 1), 0.0)
                u[c, g] = table_ref[2, g] * (part + carry)
                total = jnp.where(place == 7, part, 0.0)
                for s in (1, 2, 4):
                    total = total + pltpu.roll(total, 128 - 4 * s, 1)
                return carry + total

            def backward(k, carry):
                g = groups - 1 - k
                own_part = table_ref[1, g] * (GAMMA * adv[c, g])
                part = own_part
                for s in (1, 2, 4):
                    part = part + jnp.where(place < 8 - s, pltpu.roll(part, 128 - 4 * s, 1), 0.0)
                u[c, g] = u[c, g] + table_ref[3, g] * (part - own_part + carry)
                total = jnp.where(place == 0, part, 0.0)
                for s in (1, 2, 4):
                    total = total + pltpu.roll(total, 4 * s, 1)
                return carry + total

            zero = jnp.zeros((8, 128), F32)
            totals.append(
                (lax.fori_loop(0, groups, forward, zero), lax.fori_loop(0, groups, backward, zero))
            )

    for c in range(3):
        for t, (main, row, i) in enumerate(((b_ref, PHI, 0), (a_ref, PSI, n - 1))):
            at_left, at_right = totals[c][1 - t], totals[3 + c][1 - t]
            for zt in range(4):
                value = main[c, 8 * zt : 8 * zt + 8, :]
                value = value + jnp.where(lane < 4, pltpu.roll(at_left, (128 - 32 * zt) % 128, 1), 0.0)
                value = value + jnp.where(lane >= 124, pltpu.roll(at_right, 96 - 32 * zt, 1), 0.0)
                load_ref[pl.ds(t * 96 + c * 32 + zt * 8, 8), :] = value * co[row, i]
    row = lax.broadcasted_iota(jnp.int32, (8, 128), 0)
    ends = jnp.where(row == 0, co[PSI, 0], co[PSI, n - 1])
    ends = jnp.where(row == 2, co[PHI, 0], ends)
    load_ref[192:200, :] = jnp.where(row == 3, co[PHI, n - 1], ends)


def edge_part(from_left, from_right, left, right, a_sum, b_sum, table, group):
    groups = left.shape[1]
    ml, mr = edge_matrices()
    packed = pltpu.VMEM(left.shape, F32)

    def body(fl, fr, lo, hi, a, b, co, ml, mr, *rest):
        edge_kernel(groups, group, co, fl, fr, lo, hi, a, b, ml, mr, *rest)

    return pl.pallas_call(
        body,
        in_specs=[vmem()] * 6 + [smem()] + [vmem()] * 2,
        out_specs=[vmem()] * 5,
        out_shape=[packed] * 4 + [jax.ShapeDtypeStruct((200, 128), F32)],
        scratch_shapes=[pltpu.VMEM((4, groups, 8, 128), F32)],
        name="edge_part",
    )(from_left, from_right, left, right, a_sum, b_sum, table, jnp.asarray(ml, BF16), jnp.asarray(mr, BF16))


def couple(parts, mine, loads, below_ref, above_ref):
    def read(i):
        first, last = loads[i, 0:96, :], loads[i, 96:192, :]
        return (first, last) + tuple(loads[i, 192 + t : 193 + t, :] for t in range(4))

    def up(i, state):
        a, r = state
        first, last, psi_f, psi_l, phi_f, phi_l = read(i)
        share = psi_l * r / (1.0 - psi_f * r)
        return last + psi_l * a + share * (first + psi_f * a), phi_l + share * phi_f

    def down(k, state):
        b, q = state
        first, last, psi_f, psi_l, phi_f, phi_l = read(parts - 1 - k)
        share = phi_f * q / (1.0 - phi_l * q)
        return first + phi_f * b + share * (last + phi_l * b), psi_f + share * psi_l

    zero = (jnp.zeros((96, 128), F32), jnp.zeros((1, 128), F32))
    a, r = lax.fori_loop(0, mine, up, zero)
    b, q = lax.fori_loop(0, parts - 1 - mine, down, zero)
    first, last, psi_f, psi_l, phi_f, phi_l = read(mine)
    a_next, r_next = up(mine, (a, r))
    above = (b + q * a_next) / (1.0 - q * r_next)
    u_first = (first + psi_f * a + phi_f * above) / (1.0 - psi_f * r)
    above_ref[...] = above
    below_ref[...] = a + r * u_first


def final_kernel(parts, block, group, me, co, loads, adv_part, u_part, adv_l, adv_r, u_l, u_r,
                 u_ref, adv_ref, below_ref, above_ref):
    step = pl.program_id(0)

    @pl.when(step == 0)
    def _():
        couple(parts, me[0], loads, below_ref, above_ref)

    lane = lanes((8, 128))
    rim = jnp.logical_or(lane < 4, lane >= 124)
    for c in range(3):
        for k in range(block // group):
            g = step * (block // group) + k
            u_halves = interleave(u_l[c, g], u_r[c, g])
            adv_halves = interleave(adv_l[c, g], adv_r[c, g])
            for yl in range(group):
                i = g * group + yl
                psi, phi = co[PSI, i], co[PHI, i]
                for zt in range(4):
                    s = zt * 4 + yl // 2
                    turn = (124 - 8 * s) % 128
                    z = slice(8 * zt, 8 * zt + 8)
                    lines = slice(c * 32 + 8 * zt, c * 32 + 8 * zt + 8)
                    value = u_part[c, i, z, :] + psi * below_ref[lines, :] + phi * above_ref[lines, :]
                    extra = jnp.where(rim, pltpu.roll(u_halves[yl % 2], turn, 1), 0.0)
                    u_ref[c, k * group + yl, z, :] = value + extra
                    extra = jnp.where(rim, pltpu.roll(adv_halves[yl % 2], turn, 1), 0.0)
                    adv_ref[c, k * group + yl, z, :] = adv_part[c, i, z, :] + extra


def final_part(loads, me, table, adv_part, u_part, edges, group, block):
    parts = loads.shape[0]
    n = adv_part.shape[1]
    whole = jax.ShapeDtypeStruct((3, n, 32, 128), F32)
    tile = pl.BlockSpec((3, block, 32, 128), lambda i: (0, i, 0, 0))
    return pl.pallas_call(
        functools.partial(final_kernel, parts, block, group),
        grid=(n // block,),
        in_specs=[smem(), smem()] + [vmem()] * 7,
        out_specs=[tile, tile],
        out_shape=[whole, whole],
        scratch_shapes=[pltpu.VMEM((96, 128), F32), pltpu.VMEM((96, 128), F32)],
        compiler_params=pltpu.CompilerParams(vmem_limit_bytes=24 * MIB),
        name="final_part",
    )(me, table, loads, adv_part, u_part, *edges)


def shards(velocity, old_advection, lower_gap, upper_gap):
    n = velocity.shape[1]
    group = math.gcd(n, 8)
    block = 2 * group if n % (2 * group) == 0 else group
    wide = 3 * group if n % (3 * group) == 0 else group
    nx, ny = lax.axis_size("gx"), lax.axis_size("gy")
    ring = [(i, (i + 1) % nx) for i in range(nx)]
    line = [(i, i + 1) for i in range(ny - 1)]

    left, right = pack(velocity, group, block)
    from_left = lax.ppermute(right, "gx", ring)
    from_right = lax.ppermute(left, "gx", [(j, i) for i, j in ring])
    below = lax.ppermute(velocity[:, n - 1 :], "gy", line)
    above = lax.ppermute(velocity[:, :1], "gy", [(j, i) for i, j in line])
    table = coefs(lower_gap, upper_gap)
    adv_part, u_part, a_sum, b_sum = main_part(velocity, below, above, old_advection, table, group, wide)
    *edges, load = edge_part(from_left, from_right, left, right, a_sum, b_sum, table, group)
    loads = lax.all_gather(load, "gy")
    me = lax.axis_index("gy").astype(jnp.int32).reshape(1)
    u, adv = final_part(loads, me, table, adv_part, u_part, edges, group, block)
    return u, adv


def solution(mesh):
    spec = P(None, "gy", None, "gx")
    return jax.shard_map(
        shards,
        mesh=mesh,
        in_specs=(spec, spec, P("gy"), P("gy")),
        out_specs=(spec, spec),
        check_vma=False,
    )
```

```python
import functools

import jax
import jax.numpy as jnp
import numpy as np
from jax import lax
from jax.experimental import pallas as pl
from jax.experimental.pallas import tpu as pltpu
from jax.sharding import PartitionSpec as P

STIFF = 1024
GAMMA = 5.0 / 12.0
ZETA = -17.0 / 60.0
WEIGHTS = (672.0, -168.0, 32.0, -3.0)
UNIT = 1.0 / 840.0
F32 = jnp.float32
BF16 = jnp.bfloat16
MIB = 1 << 20

INV_GAP, FORWARD, BACKWARD, PSI, PHI = range(5)


def shift_matrix(size, periodic):
    m = np.zeros((size, size), np.float32)
    for j in range(size):
        for k, w in enumerate(WEIGHTS, 1):
            for i, s in ((j + k, w), (j - k, -w)):
                if periodic:
                    m[i % size, j] += s
                elif 0 <= i < size:
                    m[i, j] += s
    return m


def split(values):
    hi = values.astype(BF16)
    return hi, (values - hi.astype(F32)).astype(BF16)


def sublanes(shape):
    return lax.broadcasted_iota(jnp.int32, shape, len(shape) - 2)


def smem():
    return pl.BlockSpec(memory_space=pltpu.SMEM)


def vmem():
    return pl.BlockSpec(memory_space=pltpu.VMEM)


def limit(mib):
    return pltpu.CompilerParams(vmem_limit_bytes=mib * MIB)


def held(shape):
    return pltpu.VMEM(shape, F32)


def pack_kernel(group, v_hbm, pick_ref, vel, left_ref, right_ref, bottom_ref, top_ref, sems):
    n = vel.shape[1]
    pairs = n // (2 * group)

    def copy(p):
        rows = pl.ds(p * 2 * group, 2 * group)
        return pltpu.make_async_copy(v_hbm.at[:, rows], vel.at[:, rows], sems.at[p])

    for p in range(pairs):
        copy(p).start()
    rows = group * 32
    low = sublanes((8, rows)) < 4
    for p in range(pairs):
        copy(p).wait()
        for c in range(3):
            picked = []
            for h in range(2):
                f = vel[c, pl.ds((2 * p + h) * group, group)].reshape(rows, 128)
                pair = jnp.concatenate(split(f), axis=1)
                picked.append(
                    lax.dot_general(pick_ref[...], pair, (((1,), (1,)), ((), ())),
                                    preferred_element_type=F32)
                )
            one, two = picked
            right_ref[c, p] = jnp.where(low, one[:8], two[8:])
            left_ref[c, p] = jnp.where(low, one[8:], two[:8])
    for c in range(3):
        bottom_ref[c, 0] = vel[c, 0]
        top_ref[c, 0] = vel[c, n - 1]


def pack(velocity, group):
    n = velocity.shape[1]
    pick = np.zeros((16, 256), np.float32)
    edge = [124, 125, 126, 127, 0, 1, 2, 3]
    for r, lane in enumerate(edge + edge[4:] + edge[:4]):
        pick[r, lane] = pick[r, 128 + lane] = 1.0
    pairs = n // (2 * group)
    packed = jax.ShapeDtypeStruct((3, pairs, 8, group * 32), F32)
    row = jax.ShapeDtypeStruct((3, 1, 32, 128), F32)
    return pl.pallas_call(
        functools.partial(pack_kernel, group),
        in_specs=[pl.BlockSpec(memory_space=pltpu.HBM), vmem()],
        out_specs=[vmem()] * 5,
        out_shape=[held(velocity.shape), packed, packed, row, row],
        scratch_shapes=[pltpu.SemaphoreType.DMA((pairs,))],
        compiler_params=limit(8),
        name="pack_edges",
    )(pltpu.with_memory_space_constraint(velocity, pltpu.HBM), jnp.asarray(pick, BF16))


def coef_kernel(n, group, lower_ref, upper_ref, kappa_ref, inv_ref, out_ref, wide_ref):
    def up(i, state):
        phi, flux = state
        out_ref[PHI, i] = phi
        out_ref[FORWARD, i] = phi * kappa_ref[i]
        out_ref[INV_GAP, i] = inv_ref[i]
        flux = flux + kappa_ref[i] * phi
        return phi + upper_ref[i] * flux, flux

    def down(k, state):
        i = n - 1 - k
        psi, flux = state
        out_ref[PSI, i] = psi
        out_ref[BACKWARD, i] = psi * kappa_ref[i]
        flux = flux + kappa_ref[i] * psi
        return psi + lower_ref[i] * flux, flux

    def both(i, state):
        return up(i, state[0]), down(i, state[1])

    start = ((lower_ref[0], jnp.float32(1.0)), (upper_ref[n - 1], jnp.float32(1.0)))
    (wronskian, _), _ = lax.fori_loop(0, n, both, start, unroll=4)
    scale = (1.0 / jnp.full((8, 128), wronskian, F32))[0, 0]

    def norm(i, _):
        out_ref[PHI, i] = out_ref[PHI, i] * scale
        out_ref[PSI, i] = out_ref[PSI, i] * scale
        return 0

    lax.fori_loop(0, n, norm, 0, unroll=4)

    shape = (8, group * 32)
    place = lax.broadcasted_iota(jnp.int32, shape, 1) // 32
    low = sublanes(shape) < 4

    def widen(p, _):
        for t, row in enumerate((FORWARD, BACKWARD, PSI, PHI)):
            halves = []
            for h in range(2):
                value = jnp.zeros(shape, F32)
                for y in range(group):
                    value = jnp.where(place == y, out_ref[row, (2 * p + h) * group + y], value)
                halves.append(value)
            wide_ref[t, p] = jnp.where(low, *halves)
        return 0

    lax.fori_loop(0, n // (2 * group), widen, 0)


def coefs(lower_gap, upper_gap, group):
    n = lower_gap.shape[0]
    gap_sum = lower_gap + upper_gap
    return pl.pallas_call(
        functools.partial(coef_kernel, n, group),
        in_specs=[smem()] * 4,
        out_specs=[smem(), vmem()],
        out_shape=[jax.ShapeDtypeStruct((5, n), F32), held((4, n // (2 * group), 8, group * 32))],
        compiler_params=limit(2),
        name="coefficients",
    )(lower_gap, upper_gap, gap_sum * (0.5 / STIFF), 1.0 / gap_sum)


def main_kernel(n, block, group, co, vel_ref, below_ref, above_ref, old_ref, dx_ref, dz_ref,
                adv_ref, u_ref, a_ref, b_ref, f_ref):
    step = pl.program_id(0)
    steps = pl.num_programs(0)

    @pl.when(step == 0)
    def _():
        a_ref[...] = jnp.zeros_like(a_ref)

    rows = group * 32

    def chunk(k, _):
        y0 = k * group
        i0 = step * block + y0
        vel = [vel_ref[c, pl.ds(i0, group)].reshape(rows, 128) for c in range(3)]
        for c in range(3):
            f = vel[c]
            pair = jnp.concatenate(split(f), axis=1)
            along_x = jnp.dot(pair, dx_ref[...], preferred_element_type=F32)
            both = jnp.dot(dz_ref[...], pair, preferred_element_type=F32)
            along_z = both[:, :128] + both[:, 128:]
            below = jnp.where(i0 == 0, below_ref[c, 0], vel_ref[c, jnp.maximum(i0 - 1, 0)])
            above = jnp.where(i0 == n - group, above_ref[c, 0], vel_ref[c, jnp.minimum(i0 + group, n - 1)])
            acc = a_ref[c]
            for y in range(group):
                here = slice(32 * y, 32 * y + 32)
                i = i0 + y
                under = below if y == 0 else f[32 * y - 32 : 32 * y]
                over = above if y == group - 1 else f[32 * y + 32 : 32 * y + 64]
                flat = (vel[0][here] * along_x[here] + vel[2][here] * along_z[here]) * (-UNIT)
                adv = flat - vel[1][here] * ((over - under) * co[INV_GAP, i])
                force = f[here] + GAMMA * adv + ZETA * old_ref[c, y0 + y]
                acc = acc + co[FORWARD, i] * force
                adv_ref[c, i] = adv
                f_ref[c, i] = force
                u_ref[c, i] = co[PSI, i] * acc
            a_ref[c] = acc
        return 0

    lax.fori_loop(0, block // group, chunk, 0)

    @pl.when(step == steps - 1)
    def _():
        b_ref[...] = jnp.zeros_like(b_ref)

        def back(k, _):
            for c in range(3):
                acc = b_ref[c]
                for y in range(group):
                    i = n - 1 - k * group - y
                    u_ref[c, i] = u_ref[c, i] + co[PHI, i] * acc
                    acc = acc + co[BACKWARD, i] * f_ref[c, i]
                b_ref[c] = acc
            return 0

        lax.fori_loop(0, n // group, back, 0)


def main_part(vel, below, above, old, table, group, block):
    n = vel.shape[1]
    dx = shift_matrix(128, False)
    dx = jnp.asarray(np.concatenate([dx, dx]), BF16)
    dz = jnp.asarray(np.kron(np.eye(group), shift_matrix(32, True).T), BF16)
    return pl.pallas_call(
        functools.partial(main_kernel, n, block, group),
        grid=(n // block,),
        in_specs=[smem(), vmem(), vmem(), vmem(),
                  pl.BlockSpec((3, block, 32, 128), lambda i: (0, i, 0, 0)), vmem(), vmem()],
        out_specs=[vmem()] * 4,
        out_shape=[held(vel.shape), held(vel.shape), held((3, 32, 128)), held((3, 32, 128))],
        scratch_shapes=[held(vel.shape)],
        compiler_params=limit(18),
        name="inner_part",
    )(table, vel, below, above, pltpu.with_memory_space_constraint(old, pltpu.HBM), dx, dz)


def edge_kernel(pairs, group, co, from_left, from_right, left_ref, right_ref, a_ref, b_ref, wide_ref,
                sums_ref, place_ref, extra_ref, load_ref):
    n = 2 * pairs * group
    rows = group * 32
    shape = (pairs, 8, rows)
    sub = sublanes((1, 8, rows))
    low = sub < 4
    quarter = sub & 3

    def swap(x):
        return pltpu.roll(x, 4, x.ndim - 2)

    adv, u, a_total, b_total = {}, {}, {}, {}
    for side, halo, own in ((0, from_left, left_ref), (1, from_right, right_ref)):
        for c in range(3):
            h = halo[c]
            slope = jnp.zeros(shape, F32)
            for d in range(4):
                w = WEIGHTS[3 - d] * UNIT
                if side == 0:
                    weight = jnp.where(quarter + d < 4, -w, 0.0)
                    turned = pltpu.roll(h, 8 - d, 1) if d else h
                else:
                    weight = jnp.where(quarter >= d, w, 0.0)
                    turned = pltpu.roll(h, d, 1) if d else h
                slope = slope + weight * turned
            adv[side, c] = -own[0] * slope
            force = GAMMA * adv[side, c]

            def sums(weighted, which):
                hi, lo = split(weighted.reshape(pairs * 8, rows))
                both = []
                for m in (sums_ref[which], sums_ref[2]):
                    both.append(
                        (jnp.dot(hi, m, preferred_element_type=F32)
                         + jnp.dot(lo, m, preferred_element_type=F32)).reshape(shape)
                    )
                return both

            part, total = sums(wide_ref[0] * force, 0)
            carry = jnp.zeros((8, rows), F32)
            first = []
            for p in range(pairs):
                other = swap(total[p])
                first.append(part[p] + carry + jnp.where(low[0], 0.0, other))
                carry = carry + total[p] + other
            a_total[side, c] = carry
            part, total = sums(wide_ref[1] * force, 1)
            carry = jnp.zeros((8, rows), F32)
            values = [None] * pairs
            for p in reversed(range(pairs)):
                other = swap(total[p])
                second = part[p] + carry + jnp.where(low[0], other, 0.0)
                values[p] = wide_ref[2, p] * first[p] + wide_ref[3, p] * second
                carry = carry + total[p] + other
            b_total[side, c] = carry
            u[side, c] = values

    low = low[0]
    for c in range(3):
        for p in range(pairs):
            for t, (l, r) in enumerate(((u[0, c][p], u[1, c][p]), (adv[0, c][p], adv[1, c][p]))):
                for h, value in ((0, jnp.where(low, l, swap(r))), (1, jnp.where(low, swap(l), r))):
                    extra_ref[c, 2 * p + h, pl.ds(16 * t, 16)] = jnp.concatenate(split(value), axis=0)
        for t, (main, extra, row, i) in enumerate(
            ((b_ref, b_total, PHI, 0), (a_ref, a_total, PSI, n - 1))
        ):
            value = jnp.where(low, extra[0, c], extra[1, c])[:, :32]
            value = jnp.concatenate(split(value), axis=0)
            spread = lax.dot_general(value, place_ref[...], (((0,), (0,)), ((), ())),
                                     preferred_element_type=F32)
            load_ref[pl.ds(t * 96 + c * 32, 32), :] = (main[c] + spread) * co[row, i]
    row = sublanes((8, 128))
    ends = jnp.where(row == 0, co[PSI, 0], co[PSI, n - 1])
    ends = jnp.where(row == 2, co[PHI, 0], ends)
    load_ref[192:200, :] = jnp.where(row == 3, co[PHI, n - 1], ends)


def place_matrix():
    m = np.zeros((16, 128), np.float32)
    for r, lane in enumerate([0, 1, 2, 3, 124, 125, 126, 127]):
        m[r, lane] = m[r + 8, lane] = 1.0
    return m


def edge_part(from_left, from_right, left, right, a_sum, b_sum, table, wide, group):
    pairs = left.shape[1]
    each = np.eye(32)
    ones = np.ones((group, group))
    sums = np.stack([np.kron(np.triu(ones), each), np.kron(np.tril(ones, -1), each), np.kron(ones, each)])
    return pl.pallas_call(
        functools.partial(edge_kernel, pairs, group),
        in_specs=[smem()] + [vmem()] * 9,
        out_specs=[vmem()] * 2,
        out_shape=[pltpu.VMEM((3, 2 * pairs, 32, group * 32), BF16), jax.ShapeDtypeStruct((200, 128), F32)],
        compiler_params=limit(12),
        name="edge_part",
    )(table, from_left, from_right, left, right, a_sum, b_sum, wide, jnp.asarray(sums, BF16),
      jnp.asarray(place_matrix(), BF16))


def couple(parts, mine, loads, below_ref, above_ref):
    def read(i):
        first, last = loads[i, 0:96, :], loads[i, 96:192, :]
        return (first, last) + tuple(loads[i, 192 + t : 193 + t, :] for t in range(4))

    def up(i, state):
        a, r = state
        first, last, psi_f, psi_l, phi_f, phi_l = read(i)
        share = psi_l * r / (1.0 - psi_f * r)
        return last + psi_l * a + share * (first + psi_f * a), phi_l + share * phi_f

    def down(k, state):
        b, q = state
        first, last, psi_f, psi_l, phi_f, phi_l = read(parts - 1 - k)
        share = phi_f * q / (1.0 - phi_l * q)
        return first + phi_f * b + share * (last + phi_l * b), psi_f + share * psi_l

    zero = (jnp.zeros((96, 128), F32), jnp.zeros((1, 128), F32))
    a, r = lax.fori_loop(0, mine, up, zero)
    b, q = lax.fori_loop(0, parts - 1 - mine, down, zero)
    first, last, psi_f, psi_l, phi_f, phi_l = read(mine)
    a_next, r_next = up(mine, (a, r))
    above = (b + q * a_next) / (1.0 - q * r_next)
    u_first = (first + psi_f * a + phi_f * above) / (1.0 - psi_f * r)
    above_ref[...] = above
    below_ref[...] = a + r * u_first


def final_kernel(parts, block, group, me, co, loads, adv_part, u_part, extra_ref, place_ref,
                 u_ref, adv_ref, below_ref, above_ref):
    step = pl.program_id(0)

    @pl.when(step == 0)
    def _():
        couple(parts, me[0], loads, below_ref, above_ref)

    for c in range(3):
        below = below_ref[32 * c : 32 * c + 32, :]
        above = above_ref[32 * c : 32 * c + 32, :]
        for k in range(block // group):
            g = step * (block // group) + k
            spread = lax.dot_general(extra_ref[c, g], place_ref[...], (((0,), (0,)), ((), ())),
                                     preferred_element_type=F32)
            for y in range(group):
                i = g * group + y
                here = slice(32 * y, 32 * y + 32)
                value = u_part[c, i] + co[PSI, i] * below + co[PHI, i] * above
                u_ref[c, k * group + y] = value + spread[here, :128]
                adv_ref[c, k * group + y] = adv_part[c, i] + spread[here, 128:]


def final_part(loads, me, table, adv_part, u_part, extra, group, block):
    parts = loads.shape[0]
    n = adv_part.shape[1]
    whole = jax.ShapeDtypeStruct((3, n, 32, 128), F32)
    tile = pl.BlockSpec((3, block, 32, 128), lambda i: (0, i, 0, 0))
    place = jnp.asarray(np.kron(np.eye(2), place_matrix()), BF16)
    return pl.pallas_call(
        functools.partial(final_kernel, parts, block, group),
        grid=(n // block,),
        in_specs=[smem(), smem()] + [vmem()] * 5,
        out_specs=[tile, tile],
        out_shape=[whole, whole],
        scratch_shapes=[held((96, 128)), held((96, 128))],
        compiler_params=limit(12),
        name="final_part",
    )(me, table, loads, adv_part, u_part, extra, place)


def shards(velocity, old_advection, lower_gap, upper_gap):
    n = velocity.shape[1]
    group = max(d for d in range(1, 9) if n % (2 * d) == 0)
    nx, ny = lax.axis_size("gx"), lax.axis_size("gy")
    ring = [(i, (i + 1) % nx) for i in range(nx)]
    line = [(i, i + 1) for i in range(ny - 1)]

    vel, left, right, bottom, top = pack(velocity, group)
    from_left = lax.ppermute(right, "gx", ring)
    from_right = lax.ppermute(left, "gx", [(j, i) for i, j in ring])
    below = lax.ppermute(top, "gy", line)
    above = lax.ppermute(bottom, "gy", [(j, i) for i, j in line])
    table, wide = coefs(lower_gap, upper_gap, group)
    adv_part, u_part, a_sum, b_sum = main_part(vel, below, above, old_advection, table, group, 2 * group)
    extra, load = edge_part(from_left, from_right, left, right, a_sum, b_sum, table, wide, group)
    loads = lax.all_gather(load, "gy")
    me = lax.axis_index("gy").astype(jnp.int32).reshape(1)
    return final_part(loads, me, table, adv_part, u_part, extra, group, 2 * group)


def solution(mesh):
    spec = P(None, "gy", None, "gx")
    return jax.shard_map(
        shards,
        mesh=mesh,
        in_specs=(spec, spec, P("gy"), P("gy")),
        out_specs=(spec, spec),
        check_vma=False,
    )
```

```python
import functools

import jax
import jax.numpy as jnp
import numpy as np
from jax import lax
from jax.experimental import pallas as pl
from jax.experimental.pallas import tpu as pltpu
from jax.sharding import PartitionSpec as P

STIFF = 1024
GAMMA = 5.0 / 12.0
ZETA = -17.0 / 60.0
WEIGHTS = (672.0, -168.0, 32.0, -3.0)
UNIT = 1.0 / 840.0
F32 = jnp.float32
BF16 = jnp.bfloat16
MIB = 1 << 20

INV_GAP, FORWARD, BACKWARD, PSI, PHI, OWN, NEXT = range(7)


def shift_matrix(size, periodic):
    m = np.zeros((size, size), np.float32)
    for j in range(size):
        for k, w in enumerate(WEIGHTS, 1):
            for i, s in ((j + k, w), (j - k, -w)):
                if periodic:
                    m[i % size, j] += s
                elif 0 <= i < size:
                    m[i, j] += s
    return m


def split(values):
    hi = values.astype(BF16)
    return hi, (values - hi.astype(F32)).astype(BF16)


def sublanes(shape):
    return lax.broadcasted_iota(jnp.int32, shape, len(shape) - 2)


def smem():
    return pl.BlockSpec(memory_space=pltpu.SMEM)


def vmem():
    return pl.BlockSpec(memory_space=pltpu.VMEM)


def limit(mib):
    return pltpu.CompilerParams(vmem_limit_bytes=mib * MIB)


def cost(flops, moved=0):
    return pl.CostEstimate(flops=int(flops), bytes_accessed=int(moved), transcendentals=0)


def held(shape):
    return pltpu.VMEM(shape, F32)


def pack_kernel(group, v_hbm, vel, left_ref, right_ref, bottom_ref, top_ref, sems):
    n = vel.shape[1]
    pairs = n // (2 * group)

    def copy(p):
        rows = pl.ds(p * 2 * group, 2 * group)
        return pltpu.make_async_copy(v_hbm.at[:, rows], vel.at[:, rows], sems.at[p])

    for p in range(pairs):
        copy(p).start()
    rows = group * 32
    low = sublanes((8, rows)) < 4
    r = lax.broadcasted_iota(jnp.int32, (16, 256), 0)
    lane = lax.broadcasted_iota(jnp.int32, (16, 256), 1) & 127
    inside = jnp.logical_or(r < 4, r >= 12)
    pick = jnp.where(lane == jnp.where(inside, 124, 0) + (r & 3), 1.0, 0.0).astype(BF16)
    for p in range(pairs):
        copy(p).wait()
        for c in range(3):
            picked = []
            for h in range(2):
                f = vel[c, pl.ds((2 * p + h) * group, group)].reshape(rows, 128)
                pair = jnp.concatenate(split(f), axis=1)
                picked.append(
                    lax.dot_general(pick, pair, (((1,), (1,)), ((), ())), preferred_element_type=F32)
                )
            one, two = picked
            right_ref[c, p] = jnp.where(low, one[:8], two[8:])
            left_ref[c, p] = jnp.where(low, one[8:], two[:8])
    for c in range(3):
        bottom_ref[c, 0] = vel[c, 0]
        top_ref[c, 0] = vel[c, n - 1]


def pack(velocity, group):
    n = velocity.shape[1]
    pairs = n // (2 * group)
    packed = jax.ShapeDtypeStruct((3, pairs, 8, group * 32), F32)
    row = jax.ShapeDtypeStruct((3, 1, 32, 128), F32)
    return pl.pallas_call(
        functools.partial(pack_kernel, group),
        in_specs=[pl.BlockSpec(memory_space=pltpu.HBM)],
        out_specs=[vmem()] * 5,
        out_shape=[held(velocity.shape), packed, packed, row, row],
        scratch_shapes=[pltpu.SemaphoreType.DMA((pairs,))],
        compiler_params=limit(8),
        cost_estimate=cost(velocity.size, 4 * velocity.size),
        name="pack_edges",
    )(pltpu.with_memory_space_constraint(velocity, pltpu.HBM))


def coef_kernel(n, group, lower_ref, upper_ref, out_ref, wide_ref, gap_ref):
    width = out_ref.shape[1]
    shape = (8, width)
    lane = lax.broadcasted_iota(jnp.int32, shape, 1)
    gap_ref[...] = jnp.ones_like(gap_ref)
    gap_ref[0:8, 0:n] = jnp.broadcast_to(lower_ref[...].reshape(1, n), (8, n))
    gap_ref[8:16, 0:n] = jnp.broadcast_to(upper_ref[...].reshape(1, n), (8, n))
    lower, upper = gap_ref[0:8, :], gap_ref[8:16, :]
    gap_sum = lower + upper
    kappa = gap_sum * (0.5 / STIFF)
    live = lane < n

    def at(values, place):
        return jnp.sum(jnp.where(lane == place, values, 0.0), axis=1, keepdims=True)

    def sweep(gap, start, backward):
        one, zero = jnp.ones(shape, F32), jnp.zeros(shape, F32)
        m = [jnp.where(live, v, w) for v, w in
             ((1.0 + gap * kappa, one), (gap, zero), (kappa, zero), (one, one))]
        s = 1
        while s < n:
            inside = lane < width - s if backward else lane >= s
            turn = width - s if backward else s
            a, b, c, d = (jnp.where(inside, pltpu.roll(v, turn, 1), w)
                          for v, w in zip(m, (one, zero, zero, one)))
            m = [m[0] * a + m[1] * c, m[0] * b + m[1] * d, m[2] * a + m[3] * c, m[2] * b + m[3] * d]
            s *= 2
        return m[0] * start + m[1]

    first, last = at(lower, 0), at(upper, n - 1)
    phi_next = sweep(upper, first, False)
    psi_next = sweep(lower, last, True)
    phi = jnp.where(lane == 0, first, pltpu.roll(phi_next, 1, 1))
    psi = jnp.where(lane == n - 1, last, pltpu.roll(psi_next, width - 1, 1))
    scale = 1.0 / at(phi_next, n - 1)
    forward, backward = phi * kappa, psi * kappa
    out_ref[...] = jnp.zeros_like(out_ref)
    for row, value in ((INV_GAP, 1.0 / gap_sum), (FORWARD, forward), (BACKWARD, backward),
                       (PSI, psi * scale), (PHI, phi * scale), (OWN, upper / phi_next), (NEXT, phi / phi_next)):
        out_ref[row : row + 1, :] = value[0:1]

    pairs, rows = wide_ref.shape[1], wide_ref.shape[3]
    y = lax.broadcasted_iota(jnp.int32, (pairs * 8, width), 1)
    r = lax.broadcasted_iota(jnp.int32, (pairs * 8, width), 0)
    mine = y // group == (r // 8) * 2 + (r & 7) // 4
    fold = (lax.broadcasted_iota(jnp.int32, (width, rows), 0) % group
            == lax.broadcasted_iota(jnp.int32, (width, rows), 1) // 32)
    fold = jnp.where(fold, 1.0, 0.0).astype(BF16)
    for t, value in enumerate((forward, backward)):
        value = jnp.where(live, value, 0.0)
        hi, lo = split(jnp.where(mine, jnp.broadcast_to(value[0:1], mine.shape), 0.0))
        spread = jnp.dot(hi, fold, preferred_element_type=F32) + jnp.dot(lo, fold, preferred_element_type=F32)
        wide_ref[t] = spread.reshape(pairs, 8, rows)


def coefs(lower_gap, upper_gap, group):
    n = lower_gap.shape[0]
    width = -(-n // 128) * 128
    return pl.pallas_call(
        functools.partial(coef_kernel, n, group),
        in_specs=[vmem(), vmem()],
        out_specs=[vmem(), vmem()],
        out_shape=[jax.ShapeDtypeStruct((8, width), F32), held((2, n // (2 * group), 8, group * 32))],
        scratch_shapes=[held((16, width))],
        compiler_params=limit(8),
        cost_estimate=cost(1e5),
        name="coefficients",
    )(lower_gap, upper_gap)


def main_kernel(n, block, group, co, vel_ref, old_ref, dx_ref, dz_ref, adv_ref, sum_ref, b_ref, a_ref):
    step = pl.program_id(0)

    @pl.when(step == 0)
    def _():
        a_ref[...] = jnp.zeros_like(a_ref)
        b_ref[...] = jnp.zeros_like(b_ref)

    rows = group * 32
    nothing = jnp.zeros((32, 128), F32)

    for k in range(block // group):
        y0 = k * group
        i0 = step * block + y0
        vel = [vel_ref[c, pl.ds(i0, group)].reshape(rows, 128) for c in range(3)]
        for c in range(3):
            f = vel[c]
            pair = jnp.concatenate(split(f), axis=1)
            along_x = jnp.dot(pair, dx_ref[...], preferred_element_type=F32)
            both = jnp.dot(dz_ref[...], pair, preferred_element_type=F32)
            along_z = both[:, :128] + both[:, 128:]
            below = jnp.where(i0 == 0, nothing, vel_ref[c, jnp.maximum(i0 - 1, 0)])
            above = jnp.where(i0 == n - group, nothing, vel_ref[c, jnp.minimum(i0 + group, n - 1)])
            up, down = a_ref[c], b_ref[c]
            for y in range(group):
                here = slice(32 * y, 32 * y + 32)
                i = i0 + y
                under = below if y == 0 else f[32 * y - 32 : 32 * y]
                over = above if y == group - 1 else f[32 * y + 32 : 32 * y + 64]
                flat = (vel[0][here] * along_x[here] + vel[2][here] * along_z[here]) * (-UNIT)
                adv = flat - vel[1][here] * ((over - under) * co[INV_GAP, i])
                force = f[here] + GAMMA * adv + ZETA * old_ref[c, y0 + y]
                up = up + co[FORWARD, i] * force
                down = down + co[BACKWARD, i] * force
                adv_ref[c, i] = adv
                sum_ref[c, i] = up
            a_ref[c] = up
            b_ref[c] = down


def main_part(vel, old, table, group, block):
    n = vel.shape[1]
    dx = shift_matrix(128, False)
    dx = jnp.asarray(np.concatenate([dx, dx]), BF16)
    dz = jnp.asarray(np.kron(np.eye(group), shift_matrix(32, True).T), BF16)
    return pl.pallas_call(
        functools.partial(main_kernel, n, block, group),
        grid=(n // block,),
        in_specs=[smem(), vmem(), pl.BlockSpec((3, block, 32, 128), lambda i: (0, i, 0, 0)), vmem(), vmem()],
        out_specs=[vmem()] * 3,
        out_shape=[held(vel.shape), held(vel.shape), held((3, 32, 128))],
        scratch_shapes=[held((3, 32, 128))],
        compiler_params=limit(8),
        cost_estimate=cost(25 * old.size, 4 * old.size),
        name="inner_part",
    )(table, vel, pltpu.with_memory_space_constraint(old, pltpu.HBM), dx, dz)


def place_matrix():
    r = lax.broadcasted_iota(jnp.int32, (16, 128), 0) & 7
    lane = lax.broadcasted_iota(jnp.int32, (16, 128), 1)
    return jnp.where(lane == jnp.where(r < 4, r, r + 120), 1.0, 0.0).astype(BF16)


def spread_planes(value):
    return lax.dot_general(value, place_matrix(), (((0,), (0,)), ((), ())), preferred_element_type=F32)


def edge_kernel(pairs, group, co, from_left, from_right, left_ref, right_ref, sum_ref, b_ref, wide_ref,
                low_ref, high_ref, vel_ref, extra_ref, rim_ref, load_ref):
    n = 2 * pairs * group
    rows = group * 32
    shape = (pairs, 8, rows)
    sub = sublanes((1, 8, rows))
    low = sub[0] < 4
    quarter = sub & 3

    def swap(x):
        return pltpu.roll(x, 4, 0)

    def total(x):
        t = x[0]
        for p in range(1, pairs):
            t = t + x[p]
        t = t + swap(t)
        parts = t[:, 0:32]
        for y in range(1, group):
            parts = parts + t[:, 32 * y : 32 * y + 32]
        return parts

    for c in range(3):
        rims = (vel_ref[1, 0] * low_ref[c, 0] * co[INV_GAP, 0],
                -vel_ref[1, n - 1] * high_ref[c, 0] * co[INV_GAP, n - 1])
        rim_ref[0, c], rim_ref[1, c] = rims
        adv, totals = [], []
        for side, halo, own in ((0, from_left, left_ref), (1, from_right, right_ref)):
            h = halo[c]
            slope = jnp.zeros(shape, F32)
            for d in range(4):
                w = WEIGHTS[3 - d] * UNIT
                if side == 0:
                    weight = jnp.where(quarter + d < 4, -w, 0.0)
                    turned = pltpu.roll(h, 8 - d, 1) if d else h
                else:
                    weight = jnp.where(quarter >= d, w, 0.0)
                    turned = pltpu.roll(h, d, 1) if d else h
                slope = slope + weight * turned
            adv.append(-own[0] * slope)
            force = GAMMA * adv[side]
            totals.append([total(wide_ref[t] * force) for t in range(2)])
        for p in range(pairs):
            l, r = adv[0][p], adv[1][p]
            for h, value in ((0, jnp.where(low, l, swap(r))), (1, jnp.where(low, swap(l), r))):
                extra_ref[c, 2 * p + h] = jnp.concatenate(split(value), axis=0)
        for t, (main, weight, row, i) in enumerate(
            ((b_ref[c], BACKWARD, PHI, 0), (sum_ref[c, n - 1], FORWARD, PSI, n - 1))
        ):
            main = main + (GAMMA * co[weight, 0]) * rims[0] + (GAMMA * co[weight, n - 1]) * rims[1]
            value = jnp.where(low[:, :32], totals[0][1 - t], totals[1][1 - t])
            spread = spread_planes(jnp.concatenate(split(value), axis=0))
            load_ref[pl.ds(t * 96 + c * 32, 32), :] = (main + spread) * co[row, i]
    row = sublanes((8, 128))
    ends = jnp.where(row == 0, co[PSI, 0], co[PSI, n - 1])
    ends = jnp.where(row == 2, co[PHI, 0], ends)
    load_ref[192:200, :] = jnp.where(row == 3, co[PHI, n - 1], ends)


def edge_part(from_left, from_right, left, right, sums, b_sum, wide, low, high, vel, table, group):
    pairs = left.shape[1]
    return pl.pallas_call(
        functools.partial(edge_kernel, pairs, group),
        in_specs=[smem()] + [vmem()] * 10,
        out_specs=[vmem()] * 3,
        out_shape=[pltpu.VMEM((3, 2 * pairs, 16, group * 32), BF16), held((2, 3, 32, 128)),
                   jax.ShapeDtypeStruct((200, 128), F32)],
        compiler_params=limit(8),
        cost_estimate=cost(40 * left.size),
        name="edge_part",
    )(table, from_left, from_right, left, right, sums, b_sum, wide, low, high, vel)


def read(ref):
    return (ref[0:96, :], ref[96:192, :]) + tuple(ref[192 + t : 193 + t, :] for t in range(4))


def write(ref, run):
    ref[0:96, :] = run[0]
    ref[96:192, :] = run[1]
    for t in range(4):
        ref[192 + t : 193 + t, :] = run[2 + t]
    ref[196:200, :] = jnp.zeros((4, 128), F32)


def join(lower, upper):
    f1, l1, pf1, pl1, qf1, ql1 = lower
    f2, l2, pf2, pl2, qf2, ql2 = upper
    inverse = 1.0 / (1.0 - pf2 * ql1)
    over, under = qf1 * inverse, pl2 * inverse
    return (
        f1 + over * (f2 + pf2 * l1),
        l2 + under * (l1 + ql1 * f2),
        pf1 + over * pf2 * pl1,
        under * pl1,
        over * qf2,
        ql2 + under * ql1 * qf2,
    )


def empty():
    zero, one, none = (jnp.zeros((1, 128), F32), jnp.ones((1, 128), F32), jnp.zeros((96, 128), F32))
    return (none, none, zero, one, one, zero)


def join_kernel(bit, opening, closing, all_ref, other_ref, *refs):
    me = lax.axis_index("gy")
    if opening:
        lower_in = upper_in = None
        all_out, lower_out, upper_out = refs[:3]
    else:
        lower_in, upper_in, all_out, lower_out, upper_out = refs[:5]
    lower = empty() if opening else read(lower_in)
    upper = empty() if opening else read(upper_in)
    whole, other = read(all_ref), read(other_ref)

    def send(run):
        if closing:
            above_me = (me & (2 * bit)) != 0
            all_out[0:96, :] = jnp.where(above_me, run[0], run[1])
            all_out[96:104, :] = jnp.broadcast_to(jnp.where(above_me, run[2], run[5]), (8, 128))
        else:
            write(all_out, run)

    @pl.when((me & bit) != 0)
    def _():
        send(join(other, whole))
        write(lower_out, join(other, lower))
        write(upper_out, upper)

    @pl.when((me & bit) == 0)
    def _():
        send(join(whole, other))
        write(lower_out, lower)
        write(upper_out, join(upper, other))


def join_runs(bit, closing, whole, other, around):
    run = jax.ShapeDtypeStruct((200, 128), F32)
    half = jax.ShapeDtypeStruct((104, 128), F32)
    return pl.pallas_call(
        functools.partial(join_kernel, bit, not around, closing),
        in_specs=[vmem()] * (2 + len(around)),
        out_specs=[vmem()] * 3,
        out_shape=[half if closing else run, run, run],
        compiler_params=limit(8),
        cost_estimate=cost(20 * whole.size),
        name="join_runs",
    )(whole, other, *around)


def couple(bit, me, load, other_ref, lower_ref, upper_ref, below_ref, above_ref):
    lower, upper = read(lower_ref), read(upper_ref)
    vector, scalar = other_ref[0:96, :], other_ref[96:97, :]
    none, zero = jnp.zeros((96, 128), F32), jnp.zeros((1, 128), F32)

    def solve(lower, upper):
        _, a, _, _, _, r = lower
        b, _, q, _, _, _ = upper
        first, last, psi_f, psi_l, phi_f, phi_l = read(load)
        share = 1.0 / (1.0 - psi_f * r)
        a_next = last + psi_l * a + psi_l * r * share * (first + psi_f * a)
        r_next = phi_l + psi_l * r * share * phi_f
        above = (b + q * a_next) / (1.0 - q * r_next)
        above_ref[...] = above
        below_ref[...] = a + r * share * (first + psi_f * a + phi_f * above)

    @pl.when((me & bit) != 0)
    def _():
        solve(join((none, vector, zero, zero, zero, scalar), lower), upper)

    @pl.when((me & bit) == 0)
    def _():
        solve(lower, join(upper, (vector, none, scalar, zero, zero, zero)))


def up_kernel(block, group, token, co, adv_part, sum_part, extra_ref, rim_ref, adv_ref, sum_ref, acc_ref):
    step = pl.program_id(0)
    last = pl.num_programs(0) - 1

    @pl.when(step == 0)
    def _():
        acc_ref[...] = (GAMMA * co[FORWARD, 0]) * rim_ref[0]

    for c in range(3):
        acc = acc_ref[c]
        for k in range(block // group):
            g = step * (block // group) + k
            spread = spread_planes(extra_ref[c, g])
            for y in range(group):
                i = g * group + y
                extra = spread[32 * y : 32 * y + 32]
                adv_ref[c, k * group + y] = adv_part[c, i] + extra
                acc = acc + (GAMMA * co[FORWARD, i]) * extra
                sum_ref[c, i] = sum_part[c, i] + acc
        acc_ref[c] = acc

    @pl.when(step == 0)
    def _():
        adv_ref[:, 0] = adv_ref[:, 0] + rim_ref[0]

    @pl.when(step == last)
    def _():
        adv_ref[:, block - 1] = adv_ref[:, block - 1] + rim_ref[1]
        i = (last + 1) * block - 1
        sum_ref[:, i] = sum_ref[:, i] + (GAMMA * co[FORWARD, i]) * rim_ref[1]


def sweep_up(token, table, adv_part, sums, extra, rims, group, block):
    shape = adv_part.shape
    return pl.pallas_call(
        functools.partial(up_kernel, block, group),
        grid=(shape[1] // block,),
        in_specs=[pl.BlockSpec(memory_space=pl.ANY), smem()] + [vmem()] * 4,
        out_specs=[pl.BlockSpec((3, block, 32, 128), lambda i: (0, i, 0, 0)), vmem()],
        out_shape=[jax.ShapeDtypeStruct(shape, F32), held(shape)],
        scratch_shapes=[held((3, 32, 128))],
        compiler_params=limit(8),
        cost_estimate=cost(8 * adv_part.size, 4 * adv_part.size),
        name="sweep_up",
    )(token, table, adv_part, sums, extra, rims)


def down_kernel(bit, block, co, load, other, lower, upper, sum_ref, u_ref, below_ref, above_ref):
    step = pl.program_id(0)
    start = (pl.num_programs(0) - 1 - step) * block

    @pl.when(step == 0)
    def _():
        couple(bit, lax.axis_index("gy"), load, other, lower, upper, below_ref, above_ref)

    for c in range(3):
        lines = slice(32 * c, 32 * c + 32)
        below, value = below_ref[lines, :], above_ref[lines, :]
        for y in reversed(range(block)):
            i = start + y
            value = co[OWN, i] * (sum_ref[c, i] + below) + co[NEXT, i] * value
            u_ref[c, y] = value
        above_ref[lines, :] = value


def sweep_down(bit, table, load, other, around, sums, block):
    shape = sums.shape
    steps = shape[1] // block
    return pl.pallas_call(
        functools.partial(down_kernel, bit, block),
        grid=(steps,),
        in_specs=[smem()] + [vmem()] * 5,
        out_specs=pl.BlockSpec((3, block, 32, 128), lambda i: (0, steps - 1 - i, 0, 0)),
        out_shape=jax.ShapeDtypeStruct(shape, F32),
        scratch_shapes=[held((96, 128)), held((96, 128))],
        compiler_params=limit(8),
        cost_estimate=cost(4 * sums.size, 4 * sums.size),
        name="sweep_down",
    )(table, load, other, *around, sums)


def shards(velocity, old_advection, lower_gap, upper_gap):
    n = velocity.shape[1]
    group = max(d for d in range(1, 9) if n % (2 * d) == 0)
    block = 2 * group
    nx, ny = lax.axis_size("gx"), lax.axis_size("gy")
    ring = [(i, (i + 1) % nx) for i in range(nx)]
    line = [(i, i + 1) for i in range(ny - 1)]

    vel, left, right, bottom, top = pack(velocity, group)
    from_left = lax.ppermute(right, "gx", ring)
    from_right = lax.ppermute(left, "gx", [(j, i) for i, j in ring])
    below = lax.ppermute(top, "gy", line)
    above = lax.ppermute(bottom, "gy", [(j, i) for i, j in line])
    table, wide = coefs(lower_gap, upper_gap, group)
    adv_part, sums, b_sum = main_part(vel, old_advection, table, group, block)
    extra, rims, load = edge_part(
        from_left, from_right, left, right, sums, b_sum, wide, below, above, vel, table, group
    )
    bits = [1 << t for t in range(ny.bit_length() - 1)]
    whole, around, token = load, [], load
    for bit in bits:
        other = lax.ppermute(whole, "gy", [(i, i ^ bit) for i in range(ny)])
        if bit != bits[-1]:
            whole, *around = join_runs(bit, 2 * bit == bits[-1], whole, other, around)
            token = whole if bit == 1 else token
    adv, sums = sweep_up(token, table, adv_part, sums, extra, rims, group, block)
    return sweep_down(bits[-1], table, load, other, around, sums, block), adv


def solution(mesh):
    spec = P(None, "gy", None, "gx")
    return jax.shard_map(
        shards,
        mesh=mesh,
        in_specs=(spec, spec, P("gy"), P("gy")),
        out_specs=(spec, spec),
        check_vma=False,
    )
```

```python
import functools

import jax
import jax.numpy as jnp
import numpy as np
from jax import lax
from jax.experimental import pallas as pl
from jax.experimental.pallas import tpu as pltpu
from jax.sharding import PartitionSpec as P

STIFF = 1024
GAMMA = 5.0 / 12.0
ZETA = -17.0 / 60.0
WEIGHTS = (672.0, -168.0, 32.0, -3.0)
UNIT = 1.0 / 840.0
F32 = jnp.float32
BF16 = jnp.bfloat16
MIB = 1 << 20

INV_GAP, FORWARD, BACKWARD, PSI, PHI, OWN, NEXT = range(7)


def shift_matrix(size, periodic):
    m = np.zeros((size, size), np.float32)
    for j in range(size):
        for k, w in enumerate(WEIGHTS, 1):
            for i, s in ((j + k, w), (j - k, -w)):
                if periodic:
                    m[i % size, j] += s
                elif 0 <= i < size:
                    m[i, j] += s
    return m


def split(values):
    hi = values.astype(BF16)
    return hi, (values - hi.astype(F32)).astype(BF16)


def sublanes(shape):
    return lax.broadcasted_iota(jnp.int32, shape, len(shape) - 2)


def smem():
    return pl.BlockSpec(memory_space=pltpu.SMEM)


def vmem():
    return pl.BlockSpec(memory_space=pltpu.VMEM)


def limit(mib):
    return pltpu.CompilerParams(vmem_limit_bytes=mib * MIB)


def cost(flops, moved=0):
    return pl.CostEstimate(flops=int(flops), bytes_accessed=int(moved), transcendentals=0)


def held(shape):
    return pltpu.VMEM(shape, F32)


def pack_kernel(group, v_hbm, vel, left_ref, right_ref, bottom_ref, top_ref, sems):
    n = vel.shape[1]
    pairs = n // (2 * group)

    def copy(p):
        rows = pl.ds(p * 2 * group, 2 * group)
        return pltpu.make_async_copy(v_hbm.at[:, rows], vel.at[:, rows], sems.at[p])

    for p in range(pairs):
        copy(p).start()
    rows = group * 32
    low = sublanes((8, rows)) < 4
    r = lax.broadcasted_iota(jnp.int32, (16, 256), 0)
    lane = lax.broadcasted_iota(jnp.int32, (16, 256), 1) & 127
    inside = jnp.logical_or(r < 4, r >= 12)
    pick = jnp.where(lane == jnp.where(inside, 124, 0) + (r & 3), 1.0, 0.0).astype(BF16)
    for p in range(pairs):
        copy(p).wait()
        for c in range(3):
            picked = []
            for h in range(2):
                f = vel[c, pl.ds((2 * p + h) * group, group)].reshape(rows, 128)
                pair = jnp.concatenate(split(f), axis=1)
                picked.append(
                    lax.dot_general(pick, pair, (((1,), (1,)), ((), ())), preferred_element_type=F32)
                )
            one, two = picked
            right_ref[c, p] = jnp.where(low, one[:8], two[8:])
            left_ref[c, p] = jnp.where(low, one[8:], two[:8])
    for c in range(3):
        bottom_ref[c, 0] = vel[c, 0]
        top_ref[c, 0] = vel[c, n - 1]


def pack(velocity, group):
    n = velocity.shape[1]
    pairs = n // (2 * group)
    packed = jax.ShapeDtypeStruct((3, pairs, 8, group * 32), F32)
    row = jax.ShapeDtypeStruct((3, 1, 32, 128), F32)
    return pl.pallas_call(
        functools.partial(pack_kernel, group),
        in_specs=[pl.BlockSpec(memory_space=pltpu.HBM)],
        out_specs=[vmem()] * 5,
        out_shape=[held(velocity.shape), packed, packed, row, row],
        scratch_shapes=[pltpu.SemaphoreType.DMA((pairs,))],
        compiler_params=limit(8),
        cost_estimate=cost(velocity.size, 4 * velocity.size),
        name="pack_edges",
    )(pltpu.with_memory_space_constraint(velocity, pltpu.HBM))


def coef_kernel(n, group, lower_ref, upper_ref, out_ref, wide_ref, gap_ref):
    width = out_ref.shape[1]
    shape = (8, width)
    lane = lax.broadcasted_iota(jnp.int32, shape, 1)
    gap_ref[...] = jnp.ones_like(gap_ref)
    gap_ref[0:8, 0:n] = jnp.broadcast_to(lower_ref[...].reshape(1, n), (8, n))
    gap_ref[8:16, 0:n] = jnp.broadcast_to(upper_ref[...].reshape(1, n), (8, n))
    lower, upper = gap_ref[0:8, :], gap_ref[8:16, :]
    gap_sum = lower + upper
    kappa = gap_sum * (0.5 / STIFF)
    live = lane < n

    def at(values, place):
        return jnp.sum(jnp.where(lane == place, values, 0.0), axis=1, keepdims=True)

    def sweep(gap, start, backward):
        one, zero = jnp.ones(shape, F32), jnp.zeros(shape, F32)
        m = [jnp.where(live, v, w) for v, w in
             ((1.0 + gap * kappa, one), (gap, zero), (kappa, zero), (one, one))]
        s = 1
        while s < n:
            inside = lane < width - s if backward else lane >= s
            turn = width - s if backward else s
            a, b, c, d = (jnp.where(inside, pltpu.roll(v, turn, 1), w)
                          for v, w in zip(m, (one, zero, zero, one)))
            m = [m[0] * a + m[1] * c, m[0] * b + m[1] * d, m[2] * a + m[3] * c, m[2] * b + m[3] * d]
            s *= 2
        return m[0] * start + m[1]

    first, last = at(lower, 0), at(upper, n - 1)
    phi_next = sweep(upper, first, False)
    psi_next = sweep(lower, last, True)
    phi = jnp.where(lane == 0, first, pltpu.roll(phi_next, 1, 1))
    psi = jnp.where(lane == n - 1, last, pltpu.roll(psi_next, width - 1, 1))
    scale = 1.0 / at(phi_next, n - 1)
    forward, backward = phi * kappa, psi * kappa
    out_ref[...] = jnp.zeros_like(out_ref)
    for row, value in ((INV_GAP, 1.0 / gap_sum), (FORWARD, forward), (BACKWARD, backward),
                       (PSI, psi * scale), (PHI, phi * scale), (OWN, upper / phi_next), (NEXT, phi / phi_next)):
        out_ref[row : row + 1, :] = value[0:1]

    pairs, rows = wide_ref.shape[1], wide_ref.shape[3]
    y = lax.broadcasted_iota(jnp.int32, (pairs * 8, width), 1)
    r = lax.broadcasted_iota(jnp.int32, (pairs * 8, width), 0)
    mine = y // group == (r // 8) * 2 + (r & 7) // 4
    fold = (lax.broadcasted_iota(jnp.int32, (width, rows), 0) % group
            == lax.broadcasted_iota(jnp.int32, (width, rows), 1) // 32)
    fold = jnp.where(fold, 1.0, 0.0).astype(BF16)
    for t, value in enumerate((forward, backward)):
        value = jnp.where(live, value, 0.0)
        hi, lo = split(jnp.where(mine, jnp.broadcast_to(value[0:1], mine.shape), 0.0))
        spread = jnp.dot(hi, fold, preferred_element_type=F32) + jnp.dot(lo, fold, preferred_element_type=F32)
        wide_ref[t] = spread.reshape(pairs, 8, rows)


def coefs(lower_gap, upper_gap, group):
    n = lower_gap.shape[0]
    width = -(-n // 128) * 128
    return pl.pallas_call(
        functools.partial(coef_kernel, n, group),
        in_specs=[vmem(), vmem()],
        out_specs=[vmem(), vmem()],
        out_shape=[jax.ShapeDtypeStruct((8, width), F32), held((2, n // (2 * group), 8, group * 32))],
        scratch_shapes=[held((16, width))],
        compiler_params=limit(8),
        cost_estimate=cost(1e5),
        name="coefficients",
    )(lower_gap, upper_gap)


def main_kernel(n, block, group, co, vel_ref, old_hbm, dx_ref, dz_ref, adv_ref, sum_ref, b_ref, old_ref, a_ref, sems):
    steps = n // block
    rows = group * 32
    nothing = jnp.zeros((32, 128), F32)

    def copy(step):
        here = pl.ds(step * block, block)
        return pltpu.make_async_copy(old_hbm.at[:, here], old_ref.at[:, here], sems.at[step])

    for step in range(steps):
        copy(step).start()
    a_ref[...] = jnp.zeros_like(a_ref)
    b_ref[...] = jnp.zeros_like(b_ref)

    def part(step, _):
        copy(step).wait()
        for k in range(block // group):
            i0 = step * block + k * group
            vel = [vel_ref[c, pl.ds(i0, group)].reshape(rows, 128) for c in range(3)]
            for c in range(3):
                f = vel[c]
                pair = jnp.concatenate(split(f), axis=1)
                along_x = jnp.dot(pair, dx_ref[...], preferred_element_type=F32)
                both = jnp.dot(dz_ref[...], pair, preferred_element_type=F32)
                along_z = both[:, :128] + both[:, 128:]
                below = jnp.where(i0 == 0, nothing, vel_ref[c, jnp.maximum(i0 - 1, 0)])
                above = jnp.where(i0 == n - group, nothing, vel_ref[c, jnp.minimum(i0 + group, n - 1)])
                up, down = a_ref[c], b_ref[c]
                for y in range(group):
                    here = slice(32 * y, 32 * y + 32)
                    i = i0 + y
                    under = below if y == 0 else f[32 * y - 32 : 32 * y]
                    over = above if y == group - 1 else f[32 * y + 32 : 32 * y + 64]
                    flat = (vel[0][here] * along_x[here] + vel[2][here] * along_z[here]) * (-UNIT)
                    adv = flat - vel[1][here] * ((over - under) * co[INV_GAP, i])
                    force = f[here] + GAMMA * adv + ZETA * old_ref[c, i]
                    up = up + co[FORWARD, i] * force
                    down = down + co[BACKWARD, i] * force
                    adv_ref[c, i] = adv
                    sum_ref[c, i] = up
                a_ref[c] = up
                b_ref[c] = down
        return 0

    lax.fori_loop(0, steps, part, 0)


def main_part(vel, old, table, group, block):
    n = vel.shape[1]
    dx = shift_matrix(128, False)
    dx = jnp.asarray(np.concatenate([dx, dx]), BF16)
    dz = jnp.asarray(np.kron(np.eye(group), shift_matrix(32, True).T), BF16)
    return pl.pallas_call(
        functools.partial(main_kernel, n, block, group),
        in_specs=[smem(), vmem(), pl.BlockSpec(memory_space=pltpu.HBM), vmem(), vmem()],
        out_specs=[vmem()] * 3,
        out_shape=[held(vel.shape), held(vel.shape), held((3, 32, 128))],
        scratch_shapes=[held(vel.shape), held((3, 32, 128)), pltpu.SemaphoreType.DMA((n // block,))],
        compiler_params=limit(12),
        cost_estimate=cost(25 * old.size, 4 * old.size),
        name="inner_part",
    )(table, vel, pltpu.with_memory_space_constraint(old, pltpu.HBM), dx, dz)


def place_matrix():
    r = lax.broadcasted_iota(jnp.int32, (16, 128), 0) & 7
    lane = lax.broadcasted_iota(jnp.int32, (16, 128), 1)
    return jnp.where(lane == jnp.where(r < 4, r, r + 120), 1.0, 0.0).astype(BF16)


def spread_planes(value):
    return lax.dot_general(value, place_matrix(), (((0,), (0,)), ((), ())), preferred_element_type=F32)


def edge_kernel(pairs, group, co, from_left, from_right, left_ref, right_ref, sum_ref, b_ref, wide_ref,
                low_ref, high_ref, vel_ref, extra_ref, rim_ref, load_ref):
    n = 2 * pairs * group
    rows = group * 32
    shape = (pairs, 8, rows)
    sub = sublanes((1, 8, rows))
    low = sub[0] < 4
    quarter = sub & 3

    def swap(x):
        return pltpu.roll(x, 4, 0)

    def total(x):
        t = x[0]
        for p in range(1, pairs):
            t = t + x[p]
        t = t + swap(t)
        parts = t[:, 0:32]
        for y in range(1, group):
            parts = parts + t[:, 32 * y : 32 * y + 32]
        return parts

    for c in range(3):
        rims = (vel_ref[1, 0] * low_ref[c, 0] * co[INV_GAP, 0],
                -vel_ref[1, n - 1] * high_ref[c, 0] * co[INV_GAP, n - 1])
        rim_ref[0, c], rim_ref[1, c] = rims
        adv, totals = [], []
        for side, halo, own in ((0, from_left, left_ref), (1, from_right, right_ref)):
            h = halo[c]
            slope = jnp.zeros(shape, F32)
            for d in range(4):
                w = WEIGHTS[3 - d] * UNIT
                if side == 0:
                    weight = jnp.where(quarter + d < 4, -w, 0.0)
                    turned = pltpu.roll(h, 8 - d, 1) if d else h
                else:
                    weight = jnp.where(quarter >= d, w, 0.0)
                    turned = pltpu.roll(h, d, 1) if d else h
                slope = slope + weight * turned
            adv.append(-own[0] * slope)
            force = GAMMA * adv[side]
            totals.append([total(wide_ref[t] * force) for t in range(2)])
        for p in range(pairs):
            l, r = adv[0][p], adv[1][p]
            for h, value in ((0, jnp.where(low, l, swap(r))), (1, jnp.where(low, swap(l), r))):
                extra_ref[c, 2 * p + h] = jnp.concatenate(split(value), axis=0)
        for t, (main, weight, row, i) in enumerate(
            ((b_ref[c], BACKWARD, PHI, 0), (sum_ref[c, n - 1], FORWARD, PSI, n - 1))
        ):
            main = main + (GAMMA * co[weight, 0]) * rims[0] + (GAMMA * co[weight, n - 1]) * rims[1]
            value = jnp.where(low[:, :32], totals[0][1 - t], totals[1][1 - t])
            spread = spread_planes(jnp.concatenate(split(value), axis=0))
            load_ref[pl.ds(t * 96 + c * 32, 32), :] = (main + spread) * co[row, i]
    row = sublanes((8, 128))
    ends = jnp.where(row == 0, co[PSI, 0], co[PSI, n - 1])
    ends = jnp.where(row == 2, co[PHI, 0], ends)
    load_ref[192:200, :] = jnp.where(row == 3, co[PHI, n - 1], ends)


def edge_part(from_left, from_right, left, right, sums, b_sum, wide, low, high, vel, table, group):
    pairs = left.shape[1]
    return pl.pallas_call(
        functools.partial(edge_kernel, pairs, group),
        in_specs=[smem()] + [vmem()] * 10,
        out_specs=[vmem()] * 3,
        out_shape=[pltpu.VMEM((3, 2 * pairs, 16, group * 32), BF16), held((2, 3, 32, 128)),
                   jax.ShapeDtypeStruct((200, 128), F32)],
        compiler_params=limit(8),
        cost_estimate=cost(40 * left.size),
        name="edge_part",
    )(table, from_left, from_right, left, right, sums, b_sum, wide, low, high, vel)


def read(ref):
    return (ref[0:96, :], ref[96:192, :]) + tuple(ref[192 + t : 193 + t, :] for t in range(4))


def write(ref, run):
    ref[0:96, :] = run[0]
    ref[96:192, :] = run[1]
    for t in range(4):
        ref[192 + t : 193 + t, :] = run[2 + t]
    ref[196:200, :] = jnp.zeros((4, 128), F32)


def join(lower, upper):
    f1, l1, pf1, pl1, qf1, ql1 = lower
    f2, l2, pf2, pl2, qf2, ql2 = upper
    inverse = 1.0 / (1.0 - pf2 * ql1)
    over, under = qf1 * inverse, pl2 * inverse
    return (
        f1 + over * (f2 + pf2 * l1),
        l2 + under * (l1 + ql1 * f2),
        pf1 + over * pf2 * pl1,
        under * pl1,
        over * qf2,
        ql2 + under * ql1 * qf2,
    )


def empty():
    zero, one, none = (jnp.zeros((1, 128), F32), jnp.ones((1, 128), F32), jnp.zeros((96, 128), F32))
    return (none, none, zero, one, one, zero)


def join_kernel(bit, opening, closing, token, all_ref, other_ref, *refs):
    me = lax.axis_index("gy")
    if opening:
        lower_in = upper_in = None
        all_out, lower_out, upper_out = refs[:3]
    else:
        lower_in, upper_in, all_out, lower_out, upper_out = refs[:5]
    lower = empty() if opening else read(lower_in)
    upper = empty() if opening else read(upper_in)
    whole, other = read(all_ref), read(other_ref)

    def send(run):
        if closing:
            above_me = (me & (2 * bit)) != 0
            all_out[0:96, :] = jnp.where(above_me, run[0], run[1])
            all_out[96:104, :] = jnp.broadcast_to(jnp.where(above_me, run[2], run[5]), (8, 128))
        else:
            write(all_out, run)

    @pl.when((me & bit) != 0)
    def _():
        send(join(other, whole))
        write(lower_out, join(other, lower))
        write(upper_out, upper)

    @pl.when((me & bit) == 0)
    def _():
        send(join(whole, other))
        write(lower_out, lower)
        write(upper_out, join(upper, other))


def join_runs(bit, closing, token, whole, other, around):
    run = jax.ShapeDtypeStruct((200, 128), F32)
    half = jax.ShapeDtypeStruct((104, 128), F32)
    return pl.pallas_call(
        functools.partial(join_kernel, bit, not around, closing),
        in_specs=[pl.BlockSpec(memory_space=pl.ANY)] + [vmem()] * (2 + len(around)),
        out_specs=[vmem()] * 3,
        out_shape=[half if closing else run, run, run],
        compiler_params=limit(8),
        cost_estimate=cost(20 * whole.size),
        name="join_runs",
    )(token, whole, other, *around)


def couple(bit, me, load, other_ref, lower_ref, upper_ref, below_ref, above_ref):
    lower, upper = read(lower_ref), read(upper_ref)
    vector, scalar = other_ref[0:96, :], other_ref[96:97, :]
    none, zero = jnp.zeros((96, 128), F32), jnp.zeros((1, 128), F32)

    def solve(lower, upper):
        _, a, _, _, _, r = lower
        b, _, q, _, _, _ = upper
        first, last, psi_f, psi_l, phi_f, phi_l = read(load)
        share = 1.0 / (1.0 - psi_f * r)
        a_next = last + psi_l * a + psi_l * r * share * (first + psi_f * a)
        r_next = phi_l + psi_l * r * share * phi_f
        above = (b + q * a_next) / (1.0 - q * r_next)
        above_ref[...] = above
        below_ref[...] = a + r * share * (first + psi_f * a + phi_f * above)

    @pl.when((me & bit) != 0)
    def _():
        solve(join((none, vector, zero, zero, zero, scalar), lower), upper)

    @pl.when((me & bit) == 0)
    def _():
        solve(lower, join(upper, (vector, none, scalar, zero, zero, zero)))


def up_kernel(start, count, block, group, token, co, adv_part, sum_part, extra_ref, rim_ref, *refs):
    n = adv_part.shape[1]
    if start:
        _, before_ref, adv_hbm, sum_ref, end_ref, adv_ref, sems = refs
        end_ref[...] = before_ref[...]
    else:
        adv_hbm, sum_ref, end_ref, adv_ref, sems = refs
        end_ref[...] = (GAMMA * co[FORWARD, 0]) * rim_ref[0]
    steps = count // block

    def copy(step):
        here = pl.ds(step * block, block)
        there = pl.ds(start + step * block, block)
        return pltpu.make_async_copy(adv_ref.at[:, here], adv_hbm.at[:, there], sems.at[step])

    def part(step, _):
        for c in range(3):
            acc = end_ref[c]
            for k in range(block // group):
                here = step * block + k * group
                spread = spread_planes(extra_ref[c, start // group + step * (block // group) + k])
                for y in range(group):
                    i = here + y
                    extra = spread[32 * y : 32 * y + 32]
                    adv_ref[c, i] = adv_part[c, start + i] + extra
                    acc = acc + (GAMMA * co[FORWARD, start + i]) * extra
                    sum_ref[c, i] = sum_part[c, start + i] + acc
            end_ref[c] = acc

        if start == 0:
            @pl.when(step == 0)
            def _():
                adv_ref[:, 0] = adv_ref[:, 0] + rim_ref[0]

        if start + count == n:
            @pl.when(step == steps - 1)
            def _():
                adv_ref[:, count - 1] = adv_ref[:, count - 1] + rim_ref[1]
                sum_ref[:, count - 1] = sum_ref[:, count - 1] + (GAMMA * co[FORWARD, n - 1]) * rim_ref[1]

        copy(step).start()
        return 0

    lax.fori_loop(0, steps, part, 0)

    def finish(step, _):
        copy(step).wait()
        return 0

    lax.fori_loop(0, steps, finish, 0)


def sweep_up(start, count, token, table, adv_part, sums, extra, rims, group, before=()):
    shape = adv_part.shape
    block = max(d for d in range(group, 33, group) if count % d == 0)
    hbm = pl.BlockSpec(memory_space=pltpu.HBM)
    part = (3, count, 32, 128)
    return pl.pallas_call(
        functools.partial(up_kernel, start, count, block, group),
        in_specs=[pl.BlockSpec(memory_space=pl.ANY), smem()] + [vmem()] * 4 + ([hbm, vmem()] if before else []),
        out_specs=[hbm, vmem(), vmem()],
        out_shape=[jax.ShapeDtypeStruct(shape, F32), held(part), held((3, 32, 128))],
        scratch_shapes=[held(part), pltpu.SemaphoreType.DMA((count // block,))],
        input_output_aliases={6: 0} if before else {},
        compiler_params=limit(8),
        cost_estimate=cost(4 * adv_part.size, 2 * adv_part.size),
        name="sweep_up",
    )(token, table, adv_part, sums, extra, rims, *before)


def down_kernel(bit, n, block, co, load, other, lower, upper, low_ref, high_ref, u_hbm, u_ref, below_ref, above_ref,
                sems):
    steps = n // block
    couple(bit, lax.axis_index("gy"), load, other, lower, upper, below_ref, above_ref)
    below = below_ref[...].reshape(3, 32, 128)

    def copy(step):
        here = pl.ds(step * block, block)
        return pltpu.make_async_copy(u_ref.at[:, here], u_hbm.at[:, here], sems.at[step])

    def part(sum_ref, first):
        def run(k, value):
            step = steps // 2 - 1 - k
            for y in reversed(range(block)):
                i = step * block + y
                value = co[OWN, first + i] * (sum_ref[:, i] + below) + co[NEXT, first + i] * value
                u_ref[:, first + i] = value
            copy(first // block + step).start()
            return value

        return run

    value = above_ref[...].reshape(3, 32, 128)
    value = lax.fori_loop(0, steps // 2, part(high_ref, n // 2), value)
    lax.fori_loop(0, steps // 2, part(low_ref, 0), value)

    def finish(step, _):
        copy(step).wait()
        return 0

    lax.fori_loop(0, steps, finish, 0)


def sweep_down(bit, table, load, other, around, sums, block):
    n = 2 * sums[0].shape[1]
    shape = (3, n, 32, 128)
    return pl.pallas_call(
        functools.partial(down_kernel, bit, n, block),
        in_specs=[smem()] + [vmem()] * 6,
        out_specs=pl.BlockSpec(memory_space=pltpu.HBM),
        out_shape=jax.ShapeDtypeStruct(shape, F32),
        scratch_shapes=[held(shape), held((96, 128)), held((96, 128)), pltpu.SemaphoreType.DMA((n // block,))],
        compiler_params=limit(12),
        cost_estimate=cost(12 * sums[0].size, 8 * sums[0].size),
        name="sweep_down",
    )(table, load, other, *around, *sums)


def shards(velocity, old_advection, lower_gap, upper_gap):
    n = velocity.shape[1]
    group = max(d for d in range(1, 9) if n % (2 * d) == 0)
    block = 2 * group
    nx, ny = lax.axis_size("gx"), lax.axis_size("gy")
    ring = [(i, (i + 1) % nx) for i in range(nx)]
    line = [(i, i + 1) for i in range(ny - 1)]

    vel, left, right, bottom, top = pack(velocity, group)
    from_left = lax.ppermute(right, "gx", ring)
    from_right = lax.ppermute(left, "gx", [(j, i) for i, j in ring])
    below = lax.ppermute(top, "gy", line)
    above = lax.ppermute(bottom, "gy", [(j, i) for i, j in line])
    table, wide = coefs(lower_gap, upper_gap, group)
    adv_part, sums, b_sum = main_part(vel, old_advection, table, group, block)
    extra, rims, load = edge_part(
        from_left, from_right, left, right, sums, b_sum, wide, below, above, vel, table, group
    )
    bits = [1 << t for t in range(ny.bit_length() - 1)]
    half = n // 2
    whole, around, token = load, [], load
    for bit in bits:
        other = lax.ppermute(whole, "gy", [(i, i ^ bit) for i in range(ny)])
        if bit != bits[-1]:
            whole, *around = join_runs(bit, 2 * bit == bits[-1], token, whole, other, around)
        if bit == bits[0]:
            adv, low, end = sweep_up(0, half, whole, table, adv_part, sums, extra, rims, group)
            token = end
    adv, high, _ = sweep_up(half, half, whole, table, adv_part, sums, extra, rims, group, (adv, end))
    down_block = block if half % block == 0 else group
    return sweep_down(bits[-1], table, load, other, around, (low, high), down_block), adv


def solution(mesh):
    spec = P(None, "gy", None, "gx")
    return jax.shard_map(
        shards,
        mesh=mesh,
        in_specs=(spec, spec, P("gy"), P("gy")),
        out_specs=(spec, spec),
        check_vma=False,
    )
```

```python
import functools

import jax
import jax.numpy as jnp
import numpy as np
from jax import lax
from jax.experimental import pallas as pl
from jax.experimental.pallas import tpu as pltpu
from jax.sharding import PartitionSpec as P

STIFF = 1024
GAMMA = 5.0 / 12.0
ZETA = -17.0 / 60.0
WEIGHTS = (672.0, -168.0, 32.0, -3.0)
UNIT = 1.0 / 840.0
F32 = jnp.float32
BF16 = jnp.bfloat16
MIB = 1 << 20

INV_GAP, FORWARD, BACKWARD, PSI, PHI, OWN, NEXT = range(7)


def shift_matrix(size, periodic):
    m = np.zeros((size, size), np.float32)
    for j in range(size):
        for k, w in enumerate(WEIGHTS, 1):
            for i, s in ((j + k, w), (j - k, -w)):
                if periodic:
                    m[i % size, j] += s
                elif 0 <= i < size:
                    m[i, j] += s
    return m


def split(values):
    hi = values.astype(BF16)
    return hi, (values - hi.astype(F32)).astype(BF16)


def sublanes(shape):
    return lax.broadcasted_iota(jnp.int32, shape, len(shape) - 2)


def smem():
    return pl.BlockSpec(memory_space=pltpu.SMEM)


def vmem():
    return pl.BlockSpec(memory_space=pltpu.VMEM)


def limit(mib):
    return pltpu.CompilerParams(vmem_limit_bytes=mib * MIB)


def cost(flops, moved=0):
    return pl.CostEstimate(flops=int(flops), bytes_accessed=int(moved), transcendentals=0)


def held(shape):
    return pltpu.VMEM(shape, F32)


def coef_kernel(n, group, lower_ref, upper_ref, vel_ref, out_ref, wide_ref, near_ref, far_ref, gap_ref):
    width = out_ref.shape[1]
    shape = (8, width)
    lane = lax.broadcasted_iota(jnp.int32, shape, 1)
    gap_ref[...] = jnp.ones_like(gap_ref)
    gap_ref[0:8, 0:n] = jnp.broadcast_to(lower_ref[...].reshape(1, n), (8, n))
    gap_ref[8:16, 0:n] = jnp.broadcast_to(upper_ref[...].reshape(1, n), (8, n))
    lower, upper = gap_ref[0:8, :], gap_ref[8:16, :]
    gap_sum = lower + upper
    kappa = gap_sum * (0.5 / STIFF)
    live = lane < n

    def at(values, place):
        return jnp.sum(jnp.where(lane == place, values, 0.0), axis=1, keepdims=True)

    def sweep(gap, start, backward):
        one, zero = jnp.ones(shape, F32), jnp.zeros(shape, F32)
        m = [jnp.where(live, v, w) for v, w in
             ((1.0 + gap * kappa, one), (gap, zero), (kappa, zero), (one, one))]
        s = 1
        while s < n:
            inside = lane < width - s if backward else lane >= s
            turn = width - s if backward else s
            a, b, c, d = (jnp.where(inside, pltpu.roll(v, turn, 1), w)
                          for v, w in zip(m, (one, zero, zero, one)))
            m = [m[0] * a + m[1] * c, m[0] * b + m[1] * d, m[2] * a + m[3] * c, m[2] * b + m[3] * d]
            s *= 2
        return m[0] * start + m[1]

    first, last = at(lower, 0), at(upper, n - 1)
    phi_next = sweep(upper, first, False)
    psi_next = sweep(lower, last, True)
    phi = jnp.where(lane == 0, first, pltpu.roll(phi_next, 1, 1))
    psi = jnp.where(lane == n - 1, last, pltpu.roll(psi_next, width - 1, 1))
    scale = 1.0 / at(phi_next, n - 1)
    forward, backward = phi * kappa, psi * kappa
    out_ref[...] = jnp.zeros_like(out_ref)
    for row, value in ((INV_GAP, (1.0 / UNIT) / gap_sum), (FORWARD, forward), (BACKWARD, backward),
                       (PSI, psi * scale), (PHI, phi * scale), (OWN, upper / phi_next), (NEXT, phi / phi_next)):
        out_ref[row : row + 1, :] = value[0:1]

    pairs, rows = wide_ref.shape[1], wide_ref.shape[3]
    y = lax.broadcasted_iota(jnp.int32, (pairs * 8, width), 1)
    r = lax.broadcasted_iota(jnp.int32, (pairs * 8, width), 0)
    mine = y // group == (r // 8) * 2 + (r & 7) // 4
    fold = (lax.broadcasted_iota(jnp.int32, (width, rows), 0) % group
            == lax.broadcasted_iota(jnp.int32, (width, rows), 1) // 32)
    fold = jnp.where(fold, 1.0, 0.0).astype(BF16)
    for t, value in enumerate((forward, backward)):
        value = jnp.where(live, value, 0.0)
        hi, lo = split(jnp.where(mine, jnp.broadcast_to(value[0:1], mine.shape), 0.0))
        spread = jnp.dot(hi, fold, preferred_element_type=F32) + jnp.dot(lo, fold, preferred_element_type=F32)
        wide_ref[t] = spread.reshape(pairs, 8, rows)

    even = (lax.axis_index("gy") & 1) == 0
    for c in range(3):
        near_ref[c, 0] = jnp.where(even, vel_ref[c, n - 1], vel_ref[c, 0])
        far_ref[c, 0] = jnp.where(even, vel_ref[c, 0], vel_ref[c, n - 1])


def coefs(lower_gap, upper_gap, vel, group):
    n = lower_gap.shape[0]
    width = -(-n // 128) * 128
    row = jax.ShapeDtypeStruct((3, 1, 32, 128), F32)
    return pl.pallas_call(
        functools.partial(coef_kernel, n, group),
        in_specs=[vmem()] * 3,
        out_specs=[vmem()] * 4,
        out_shape=[jax.ShapeDtypeStruct((8, width), F32), held((2, n // (2 * group), 8, group * 32)), row, row],
        scratch_shapes=[held((16, width))],
        compiler_params=limit(4),
        cost_estimate=cost(1e5),
        name="coefficients",
    )(lower_gap, upper_gap, vel)


def pack_kernel(group, v_hbm, vel, pair_ref, left_ref, right_ref, sems):
    n = vel.shape[1]
    pairs = n // (2 * group)

    def copy(p):
        rows = pl.ds(p * 2 * group, 2 * group)
        return pltpu.make_async_copy(v_hbm.at[:, rows], vel.at[:, rows], sems.at[p])

    for p in range(pairs):
        copy(p).start()
    rows = group * 32
    low = sublanes((8, rows)) < 4
    r = lax.broadcasted_iota(jnp.int32, (16, 256), 0)
    lane = lax.broadcasted_iota(jnp.int32, (16, 256), 1) & 127
    inside = jnp.logical_or(r < 4, r >= 12)
    pick = jnp.where(lane == jnp.where(inside, 124, 0) + (r & 3), 1.0, 0.0).astype(BF16)
    for p in range(pairs):
        copy(p).wait()
        for c in range(3):
            picked = []
            for h in range(2):
                f = vel[c, pl.ds((2 * p + h) * group, group)].reshape(rows, 128)
                pair = jnp.concatenate(split(f), axis=1)
                pair_ref[c, pl.ds((2 * p + h) * rows, rows), :] = pair
                picked.append(
                    lax.dot_general(pick, pair, (((1,), (1,)), ((), ())), preferred_element_type=F32)
                )
            one, two = picked
            right_ref[c, p] = jnp.where(low, one[:8], two[8:])
            left_ref[c, p] = jnp.where(low, one[8:], two[:8])


def pack(velocity, group):
    n = velocity.shape[1]
    pairs = n // (2 * group)
    packed = jax.ShapeDtypeStruct((3, pairs, 8, group * 32), F32)
    return pl.pallas_call(
        functools.partial(pack_kernel, group),
        in_specs=[pl.BlockSpec(memory_space=pltpu.HBM)],
        out_specs=[vmem()] * 4,
        out_shape=[held(velocity.shape), pltpu.VMEM((3, n * 32, 256), BF16), packed, packed],
        scratch_shapes=[pltpu.SemaphoreType.DMA((pairs,))],
        compiler_params=limit(8),
        cost_estimate=cost(velocity.size, 4 * velocity.size),
        name="pack_edges",
    )(pltpu.with_memory_space_constraint(velocity, pltpu.HBM))


def main_plain(n, block, group, co, vel_ref, pair_ref, old_hbm, dx_ref, dz_ref, adv_ref, sum_ref, b_ref, old_ref, a_ref, w_ref, sems):
    steps = n // block
    rows = group * 32

    def copy(step):
        here = pl.ds(step * block, block)
        return pltpu.make_async_copy(old_hbm.at[:, here], old_ref.at[:, here], sems.at[step])

    for step in range(steps):
        copy(step).start()
    b_ref[...] = jnp.zeros_like(b_ref)

    def part(step, _):
        copy(step).wait()
        for k in range(block // group):
            i0 = step * block + k * group
            vel = [vel_ref[c, pl.ds(i0, group)].reshape(rows, 128) for c in range(3)]
            for c in range(3):
                f = vel[c]
                pair = pair_ref[c, pl.ds(i0 * 32, rows), :]
                along_x = jnp.dot(pair, dx_ref[...], preferred_element_type=F32)
                both = jnp.dot(dz_ref[...], pair, preferred_element_type=F32)
                along_z = both[:, :128] + both[:, 128:]
                below = jnp.where(i0 == 0, 0.0, vel_ref[c, jnp.maximum(i0 - 1, 0)])
                above = jnp.where(i0 == n - group, 0.0, vel_ref[c, jnp.minimum(i0 + group, n - 1)])
                up = jnp.where(jnp.logical_or(i0 == 0, i0 == n // 2), 0.0, a_ref[c])
                down = b_ref[c]
                for y in range(group):
                    here = slice(32 * y, 32 * y + 32)
                    i = i0 + y
                    under = below if y == 0 else f[32 * y - 32 : 32 * y]
                    over = above if y == group - 1 else f[32 * y + 32 : 32 * y + 64]
                    flat = vel[0][here] * along_x[here] + vel[2][here] * along_z[here]
                    adv = flat + vel[1][here] * ((over - under) * co[INV_GAP, i])
                    force = f[here] + (-UNIT * GAMMA) * adv + ZETA * old_ref[c, i]
                    up = up + co[FORWARD, i] * force
                    down = down + co[BACKWARD, i] * force
                    adv_ref[c, i] = adv
                    sum_ref[c, i] = up
                a_ref[c] = up
                b_ref[c] = down
        return 0

    lax.fori_loop(0, steps, part, 0)


def main_kernel(n, block, group, co, vel_ref, pair_ref, old_hbm, dx_ref, dz_ref, adv_ref, sum_ref, b_ref, old_ref,
                a_ref, w_ref, sems):
    pairs = n // (2 * group)
    half = n // 2
    rows = group * 32
    pieces = 4
    high = rows // pieces

    def copies(p):
        found = []
        for h in range(2):
            here = pl.ds(h * half + p * group, group)
            found.append(pltpu.make_async_copy(old_hbm.at[:, here], old_ref.at[:, here], sems.at[2 * p + h]))
        return found

    for p in range(pairs):
        for copy in copies(p):
            copy.start()
    a_ref[...] = jnp.zeros_like(a_ref)
    b_ref[...] = jnp.zeros_like(b_ref)

    def run(*accs):
        def issue(p, c, first=False):
            parts = [pair_ref[c, pl.ds((h * half + p * group) * 32, rows), :] for h in range(2)]
            for t in range(2):
                side = jnp.concatenate([part[:, 128 * t : 128 * t + 128] for part in parts], axis=1)
                pltpu.matmul_push_rhs(side, t, 1)
                for q in range(pieces):
                    here = slice(q * high, (q + 1) * high)
                    fresh = 0 if first and t == 0 and q == 0 else None
                    pltpu.matmul_acc_lhs(accs[c * 8 + q], side[here], load_staged_rhs=fresh)
                    pltpu.matmul_acc_lhs(accs[c * 8 + 4 + q], dz_ref[here, :], load_staged_rhs=t if q == 0 else None)

        def scale(p):
            for h in range(2):
                for y in range(group):
                    i = h * half + p * group + y
                    w_ref[h, y] = vel_ref[1, i] * co[INV_GAP, i]

        def points(p, c):
            up = [a_ref[h, c] for h in range(2)]
            down = b_ref[c]
            for q in range(pieces):
                along_x = pltpu.matmul_pop(accs[c * 8 + q])
                along_z = pltpu.matmul_pop(accs[c * 8 + 4 + q])
                for h in range(2):
                    lanes = slice(128 * h, 128 * h + 128)
                    for k in range(group // pieces):
                        y = q * (group // pieces) + k
                        i = h * half + p * group + y
                        here = slice(32 * k, 32 * k + 32)
                        under = vel_ref[c, jnp.maximum(i - 1, 0)]
                        over = vel_ref[c, jnp.minimum(i + 1, n - 1)]
                        if h == 0 and y == 0:
                            under = jnp.where(p == 0, 0.0, under)
                        if h == 1 and y == group - 1:
                            over = jnp.where(p == pairs - 1, 0.0, over)
                        adv = vel_ref[0, i] * along_x[here, lanes] + vel_ref[2, i] * along_z[here, lanes]
                        adv = adv + w_ref[h, y] * (over - under)
                        force = vel_ref[c, i] + (-UNIT * GAMMA) * adv + ZETA * old_ref[c, i]
                        up[h] = up[h] + co[FORWARD, i] * force
                        down = down + co[BACKWARD, i] * force
                        adv_ref[c, i] = adv
                        sum_ref[c, i] = up[h]
            for h in range(2):
                a_ref[h, c] = up[h]
            b_ref[c] = down

        pltpu.matmul_push_rhs(dx_ref[...], 0, 0)
        for c in range(3):
            issue(0, c, c == 0)

        def part(p, _):
            for copy in copies(p):
                copy.wait()
            scale(p)
            for c in range(3):
                points(p, c)
                issue(p + 1, c)
            return 0

        lax.fori_loop(0, pairs - 1, part, 0)
        for copy in copies(pairs - 1):
            copy.wait()
        scale(pairs - 1)
        for c in range(3):
            points(pairs - 1, c)

    pl.run_scoped(run, *(pltpu.ACC(unit)((high, 256), F32) for _ in range(3) for unit in range(2) for _ in range(pieces)))


def main_part(vel, pair, old, table, group, block):
    n = vel.shape[1]
    both_units = group == 8
    dx = shift_matrix(128, False)
    dx = np.kron(np.eye(2), dx) if both_units else np.concatenate([dx, dx])
    dz = jnp.asarray(np.kron(np.eye(group), shift_matrix(32, True).T), BF16)
    return pl.pallas_call(
        functools.partial(main_kernel if both_units else main_plain, n, block, group),
        in_specs=[smem(), vmem(), vmem(), pl.BlockSpec(memory_space=pltpu.HBM), vmem(), vmem()],
        out_specs=[vmem()] * 3,
        out_shape=[held(vel.shape), held(vel.shape), held((3, 32, 128))],
        scratch_shapes=[held(vel.shape), held((2, 3, 32, 128) if both_units else (3, 32, 128)),
                        held((2, group, 32, 128)),
                        pltpu.SemaphoreType.DMA((n // group,))],
        compiler_params=limit(15),
        cost_estimate=cost(25 * old.size, 4 * old.size),
        name="inner_part",
    )(table, vel, pair, pltpu.with_memory_space_constraint(old, pltpu.HBM), jnp.asarray(dx, BF16), dz)


def place_matrix():
    r = lax.broadcasted_iota(jnp.int32, (16, 128), 0) & 7
    lane = lax.broadcasted_iota(jnp.int32, (16, 128), 1)
    return jnp.where(lane == jnp.where(r < 4, r, r + 120), 1.0, 0.0).astype(BF16)


def spread_planes(value):
    return lax.dot_general(value, place_matrix(), (((0,), (0,)), ((), ())), preferred_element_type=F32)


def edge_kernel(pairs, group, co, from_left, from_right, left_ref, right_ref, sum_ref, b_ref, wide_ref,
                near_ref, far_ref, vel_ref, extra_ref, rim_ref, load_ref):
    even = (lax.axis_index("gy") & 1) == 0
    n = 2 * pairs * group
    rows = group * 32
    shape = (pairs, 8, rows)
    sub = sublanes((1, 8, rows))
    low = sub[0] < 4
    quarter = sub & 3

    def swap(x):
        return pltpu.roll(x, 4, 0)

    def total(x):
        t = x[0]
        for p in range(1, pairs):
            t = t + x[p]
        t = t + swap(t)
        parts = t[:, 0:32]
        for y in range(1, group):
            parts = parts + t[:, 32 * y : 32 * y + 32]
        return parts

    for c in range(3):
        below = jnp.where(even, far_ref[c, 0], near_ref[c, 0])
        above = jnp.where(even, near_ref[c, 0], far_ref[c, 0])
        rims = (vel_ref[1, 0] * below * (UNIT * co[INV_GAP, 0]),
                -vel_ref[1, n - 1] * above * (UNIT * co[INV_GAP, n - 1]))
        rim_ref[0, c], rim_ref[1, c] = rims
        adv, totals = [], []
        for side, halo, own in ((0, from_left, left_ref), (1, from_right, right_ref)):
            h = halo[c]
            slope = jnp.zeros(shape, F32)
            for d in range(4):
                w = WEIGHTS[3 - d] * UNIT
                if side == 0:
                    weight = jnp.where(quarter + d < 4, -w, 0.0)
                    turned = pltpu.roll(h, 8 - d, 1) if d else h
                else:
                    weight = jnp.where(quarter >= d, w, 0.0)
                    turned = pltpu.roll(h, d, 1) if d else h
                slope = slope + weight * turned
            adv.append(-own[0] * slope)
            force = GAMMA * adv[side]
            totals.append([total(wide_ref[t] * force) for t in range(2)])
        for p in range(pairs):
            l, r = adv[0][p], adv[1][p]
            for h, value in ((0, jnp.where(low, l, swap(r))), (1, jnp.where(low, swap(l), r))):
                extra_ref[c, 2 * p + h] = jnp.concatenate(split(value), axis=0)
        for t, (main, weight, row, i) in enumerate(
            ((b_ref[c], BACKWARD, PHI, 0), (sum_ref[c, n // 2 - 1] + sum_ref[c, n - 1], FORWARD, PSI, n - 1))
        ):
            main = main + (GAMMA * co[weight, 0]) * rims[0] + (GAMMA * co[weight, n - 1]) * rims[1]
            value = jnp.where(low[:, :32], totals[0][1 - t], totals[1][1 - t])
            spread = spread_planes(jnp.concatenate(split(value), axis=0))
            load_ref[pl.ds(t * 96 + c * 32, 32), :] = (main + spread) * co[row, i]
    row = sublanes((8, 128))
    ends = jnp.where(row == 0, co[PSI, 0], co[PSI, n - 1])
    ends = jnp.where(row == 2, co[PHI, 0], ends)
    load_ref[192:200, :] = jnp.where(row == 3, co[PHI, n - 1], ends)


def edge_part(from_left, from_right, left, right, sums, b_sum, wide, near, far, vel, table, group):
    pairs = left.shape[1]
    return pl.pallas_call(
        functools.partial(edge_kernel, pairs, group),
        in_specs=[smem()] + [vmem()] * 10,
        out_specs=[vmem()] * 3,
        out_shape=[pltpu.VMEM((3, 2 * pairs, 16, group * 32), BF16), held((2, 3, 32, 128)),
                   jax.ShapeDtypeStruct((200, 128), F32)],
        compiler_params=limit(8),
        cost_estimate=cost(40 * left.size),
        name="edge_part",
    )(table, from_left, from_right, left, right, sums, b_sum, wide, near, far, vel)


def read(ref):
    return (ref[0:96, :], ref[96:192, :]) + tuple(ref[192 + t : 193 + t, :] for t in range(4))


def write(ref, run):
    ref[0:96, :] = run[0]
    ref[96:192, :] = run[1]
    for t in range(4):
        ref[192 + t : 193 + t, :] = run[2 + t]
    ref[196:200, :] = jnp.zeros((4, 128), F32)


def join(lower, upper):
    f1, l1, pf1, pl1, qf1, ql1 = lower
    f2, l2, pf2, pl2, qf2, ql2 = upper
    inverse = 1.0 / (1.0 - pf2 * ql1)
    over, under = qf1 * inverse, pl2 * inverse
    return (
        f1 + over * (f2 + pf2 * l1),
        l2 + under * (l1 + ql1 * f2),
        pf1 + over * pf2 * pl1,
        under * pl1,
        over * qf2,
        ql2 + under * ql1 * qf2,
    )


def empty():
    zero, one, none = (jnp.zeros((1, 128), F32), jnp.ones((1, 128), F32), jnp.zeros((96, 128), F32))
    return (none, none, zero, one, one, zero)


def join_kernel(bit, opening, closing, token, all_ref, other_ref, *refs):
    me = lax.axis_index("gy")
    if opening:
        lower_in = upper_in = None
        all_out, lower_out, upper_out = refs[:3]
    else:
        lower_in, upper_in, all_out, lower_out, upper_out = refs[:5]
    lower = empty() if opening else read(lower_in)
    upper = empty() if opening else read(upper_in)
    whole, other = read(all_ref), read(other_ref)

    def send(run):
        if closing:
            above_me = (me & (2 * bit)) != 0
            all_out[0:96, :] = jnp.where(above_me, run[0], run[1])
            all_out[96:104, :] = jnp.broadcast_to(jnp.where(above_me, run[2], run[5]), (8, 128))
        else:
            write(all_out, run)

    @pl.when((me & bit) != 0)
    def _():
        send(join(other, whole))
        write(lower_out, join(other, lower))
        write(upper_out, upper)

    @pl.when((me & bit) == 0)
    def _():
        send(join(whole, other))
        write(lower_out, lower)
        write(upper_out, join(upper, other))


def join_runs(bit, closing, token, whole, other, around):
    run = jax.ShapeDtypeStruct((200, 128), F32)
    half = jax.ShapeDtypeStruct((104, 128), F32)
    return pl.pallas_call(
        functools.partial(join_kernel, bit, not around, closing),
        in_specs=[pl.BlockSpec(memory_space=pl.ANY)] + [vmem()] * (2 + len(around)),
        out_specs=[vmem()] * 3,
        out_shape=[half if closing else run, run, run],
        compiler_params=limit(8),
        cost_estimate=cost(20 * whole.size),
        name="join_runs",
    )(token, whole, other, *around)


def couple(bit, me, load, other_ref, lower_ref, upper_ref, below_ref, above_ref):
    lower, upper = read(lower_ref), read(upper_ref)
    vector, scalar = other_ref[0:96, :], other_ref[96:97, :]
    none, zero = jnp.zeros((96, 128), F32), jnp.zeros((1, 128), F32)

    def solve(lower, upper):
        _, a, _, _, _, r = lower
        b, _, q, _, _, _ = upper
        first, last, psi_f, psi_l, phi_f, phi_l = read(load)
        share = 1.0 / (1.0 - psi_f * r)
        a_next = last + psi_l * a + psi_l * r * share * (first + psi_f * a)
        r_next = phi_l + psi_l * r * share * phi_f
        above = (b + q * a_next) / (1.0 - q * r_next)
        above_ref[...] = above
        below_ref[...] = a + r * share * (first + psi_f * a + phi_f * above)

    @pl.when((me & bit) != 0)
    def _():
        solve(join((none, vector, zero, zero, zero, scalar), lower), upper)

    @pl.when((me & bit) == 0)
    def _():
        solve(lower, join(upper, (vector, none, scalar, zero, zero, zero)))


def up_kernel(start, count, block, group, token, co, adv_part, sum_part, extra_ref, rim_ref, *refs):
    n = adv_part.shape[1]
    if start:
        _, before_ref, adv_hbm, sum_ref, end_ref, adv_ref, sems = refs
        end_ref[...] = before_ref[...] + sum_part[:, start - 1]
    else:
        adv_hbm, sum_ref, end_ref, adv_ref, sems = refs
        end_ref[...] = (GAMMA * co[FORWARD, 0]) * rim_ref[0]
    steps = count // block

    def copy(step):
        here = pl.ds(step * block, block)
        there = pl.ds(start + step * block, block)
        return pltpu.make_async_copy(adv_ref.at[:, here], adv_hbm.at[:, there], sems.at[step])

    def part(step, _):
        for c in range(3):
            acc = end_ref[c]
            for k in range(block // group):
                here = step * block + k * group
                spread = spread_planes(extra_ref[c, start // group + step * (block // group) + k])
                for y in range(group):
                    i = here + y
                    extra = spread[32 * y : 32 * y + 32]
                    adv_ref[c, i] = adv_part[c, start + i] * (-UNIT) + extra
                    acc = acc + (GAMMA * co[FORWARD, start + i]) * extra
                    sum_ref[c, i] = sum_part[c, start + i] + acc
            end_ref[c] = acc

        if start == 0:
            @pl.when(step == 0)
            def _():
                adv_ref[:, 0] = adv_ref[:, 0] + rim_ref[0]

        if start + count == n:
            @pl.when(step == steps - 1)
            def _():
                adv_ref[:, count - 1] = adv_ref[:, count - 1] + rim_ref[1]
                sum_ref[:, count - 1] = sum_ref[:, count - 1] + (GAMMA * co[FORWARD, n - 1]) * rim_ref[1]

        copy(step).start()
        return 0

    lax.fori_loop(0, steps, part, 0)

    def finish(step, _):
        copy(step).wait()
        return 0

    lax.fori_loop(0, steps, finish, 0)


def sweep_up(start, count, token, table, adv_part, sums, extra, rims, group, before=()):
    shape = adv_part.shape
    block = max(d for d in range(group, 33, group) if count % d == 0)
    hbm = pl.BlockSpec(memory_space=pltpu.HBM)
    part = (3, count, 32, 128)
    return pl.pallas_call(
        functools.partial(up_kernel, start, count, block, group),
        in_specs=[pl.BlockSpec(memory_space=pl.ANY), smem()] + [vmem()] * 4 + ([hbm, vmem()] if before else []),
        out_specs=[hbm, vmem(), vmem()],
        out_shape=[jax.ShapeDtypeStruct(shape, F32), held(part), held((3, 32, 128))],
        scratch_shapes=[held(part), pltpu.SemaphoreType.DMA((count // block,))],
        input_output_aliases={6: 0} if before else {},
        compiler_params=limit(8),
        cost_estimate=cost(4 * adv_part.size, 2 * adv_part.size),
        name="sweep_up",
    )(token, table, adv_part, sums, extra, rims, *before)


def down_kernel(bit, n, block, co, load, other, lower, upper, low_ref, high_ref, u_hbm, u_ref, below_ref, above_ref,
                sems):
    steps = n // block
    couple(bit, lax.axis_index("gy"), load, other, lower, upper, below_ref, above_ref)
    below = below_ref[...].reshape(3, 32, 128)

    def copy(step):
        here = pl.ds(step * block, block)
        return pltpu.make_async_copy(u_ref.at[:, here], u_hbm.at[:, here], sems.at[step])

    def part(sum_ref, first):
        def run(k, value):
            step = steps // 2 - 1 - k
            for y in reversed(range(block)):
                i = step * block + y
                value = co[OWN, first + i] * (sum_ref[:, i] + below) + co[NEXT, first + i] * value
                u_ref[:, first + i] = value
            copy(first // block + step).start()
            return value

        return run

    value = above_ref[...].reshape(3, 32, 128)
    value = lax.fori_loop(0, steps // 2, part(high_ref, n // 2), value)
    lax.fori_loop(0, steps // 2, part(low_ref, 0), value)

    def finish(step, _):
        copy(step).wait()
        return 0

    lax.fori_loop(0, steps, finish, 0)


def sweep_down(bit, table, load, other, around, sums, block):
    n = 2 * sums[0].shape[1]
    shape = (3, n, 32, 128)
    return pl.pallas_call(
        functools.partial(down_kernel, bit, n, block),
        in_specs=[smem()] + [vmem()] * 6,
        out_specs=pl.BlockSpec(memory_space=pltpu.HBM),
        out_shape=jax.ShapeDtypeStruct(shape, F32),
        scratch_shapes=[held(shape), held((96, 128)), held((96, 128)), pltpu.SemaphoreType.DMA((n // block,))],
        compiler_params=limit(12),
        cost_estimate=cost(12 * sums[0].size, 8 * sums[0].size),
        name="sweep_down",
    )(table, load, other, *around, *sums)


def shards(velocity, old_advection, lower_gap, upper_gap):
    n = velocity.shape[1]
    group = max(d for d in range(1, 9) if n % (2 * d) == 0)
    block = 2 * group
    nx, ny = lax.axis_size("gx"), lax.axis_size("gy")
    ring = [(i, (i + 1) % nx) for i in range(nx)]
    pairs = [(i, i ^ 1) for i in range(ny)]
    others = [(i, j) for k in range(1, ny - 1, 2) for i, j in ((k, k + 1), (k + 1, k))]

    vel, pair, left, right = pack(velocity, group)
    from_left = lax.ppermute(right, "gx", ring)
    from_right = lax.ppermute(left, "gx", [(j, i) for i, j in ring])
    table, wide, near, far = coefs(lower_gap, upper_gap, vel, group)
    near = lax.ppermute(near, "gy", pairs)
    far = lax.ppermute(far, "gy", others)
    adv_part, sums, b_sum = main_part(vel, pair, old_advection, table, group, block)
    extra, rims, load = edge_part(
        from_left, from_right, left, right, sums, b_sum, wide, near, far, vel, table, group
    )
    bits = [1 << t for t in range(ny.bit_length() - 1)]
    half = n // 2
    whole, around, token = load, [], load
    for bit in bits:
        other = lax.ppermute(whole, "gy", [(i, i ^ bit) for i in range(ny)])
        if bit != bits[-1]:
            whole, *around = join_runs(bit, 2 * bit == bits[-1], token, whole, other, around)
        if bit == bits[0]:
            adv, low, end = sweep_up(0, half, whole, table, adv_part, sums, extra, rims, group)
            token = end
    adv, high, _ = sweep_up(half, half, whole, table, adv_part, sums, extra, rims, group, (adv, end))
    down_block = block if half % block == 0 else group
    return sweep_down(bits[-1], table, load, other, around, (low, high), down_block), adv


def solution(mesh):
    spec = P(None, "gy", None, "gx")
    return jax.shard_map(
        shards,
        mesh=mesh,
        in_specs=(spec, spec, P("gy"), P("gy")),
        out_specs=(spec, spec),
        check_vma=False,
    )
```

```python
import functools

import jax
import jax.numpy as jnp
import numpy as np
from jax import lax
from jax.experimental import pallas as pl
from jax.experimental.pallas import tpu as pltpu
from jax.sharding import PartitionSpec as P

STIFF = 1024
GAMMA = 5.0 / 12.0
ZETA = -17.0 / 60.0
WEIGHTS = (672.0, -168.0, 32.0, -3.0)
UNIT = 1.0 / 840.0
F32 = jnp.float32
BF16 = jnp.bfloat16
MIB = 1 << 20

INV_GAP, FORWARD, BACKWARD, PSI, PHI, OWN, NEXT = range(7)


def shift_matrix(size, periodic):
    m = np.zeros((size, size), np.float32)
    for j in range(size):
        for k, w in enumerate(WEIGHTS, 1):
            for i, s in ((j + k, w), (j - k, -w)):
                if periodic:
                    m[i % size, j] += s
                elif 0 <= i < size:
                    m[i, j] += s
    return m


def split(values):
    hi = values.astype(BF16)
    return hi, (values - hi.astype(F32)).astype(BF16)


def sublanes(shape):
    return lax.broadcasted_iota(jnp.int32, shape, len(shape) - 2)


def smem():
    return pl.BlockSpec(memory_space=pltpu.SMEM)


def vmem():
    return pl.BlockSpec(memory_space=pltpu.VMEM)


def limit(mib):
    return pltpu.CompilerParams(vmem_limit_bytes=mib * MIB)


def cost(flops, moved=0):
    return pl.CostEstimate(flops=int(flops), bytes_accessed=int(moved), transcendentals=0)


def held(shape):
    return pltpu.VMEM(shape, F32)


def coef_kernel(n, group, lower_ref, upper_ref, vel_ref, out_ref, wide_ref, near_ref, far_ref, gap_ref):
    width = out_ref.shape[1]
    shape = (8, width)
    lane = lax.broadcasted_iota(jnp.int32, shape, 1)
    gap_ref[...] = jnp.ones_like(gap_ref)
    gap_ref[0:8, 0:n] = jnp.broadcast_to(lower_ref[...].reshape(1, n), (8, n))
    gap_ref[8:16, 0:n] = jnp.broadcast_to(upper_ref[...].reshape(1, n), (8, n))
    lower, upper = gap_ref[0:8, :], gap_ref[8:16, :]
    gap_sum = lower + upper
    kappa = gap_sum * (0.5 / STIFF)
    live = lane < n

    def at(values, place):
        return jnp.sum(jnp.where(lane == place, values, 0.0), axis=1, keepdims=True)

    def sweep(gap, start, backward):
        one, zero = jnp.ones(shape, F32), jnp.zeros(shape, F32)
        m = [jnp.where(live, v, w) for v, w in
             ((1.0 + gap * kappa, one), (gap, zero), (kappa, zero), (one, one))]
        s = 1
        while s < n:
            inside = lane < width - s if backward else lane >= s
            turn = width - s if backward else s
            a, b, c, d = (jnp.where(inside, pltpu.roll(v, turn, 1), w)
                          for v, w in zip(m, (one, zero, zero, one)))
            m = [m[0] * a + m[1] * c, m[0] * b + m[1] * d, m[2] * a + m[3] * c, m[2] * b + m[3] * d]
            s *= 2
        return m[0] * start + m[1]

    first, last = at(lower, 0), at(upper, n - 1)
    phi_next = sweep(upper, first, False)
    psi_next = sweep(lower, last, True)
    phi = jnp.where(lane == 0, first, pltpu.roll(phi_next, 1, 1))
    psi = jnp.where(lane == n - 1, last, pltpu.roll(psi_next, width - 1, 1))
    scale = 1.0 / at(phi_next, n - 1)
    forward, backward = phi * kappa, psi * kappa
    out_ref[...] = jnp.zeros_like(out_ref)
    for row, value in ((INV_GAP, (1.0 / UNIT) / gap_sum), (FORWARD, forward), (BACKWARD, backward),
                       (PSI, psi * scale), (PHI, phi * scale), (OWN, upper / phi_next), (NEXT, phi / phi_next)):
        out_ref[row : row + 1, :] = value[0:1]

    pairs, rows = wide_ref.shape[1], wide_ref.shape[3]
    y = lax.broadcasted_iota(jnp.int32, (pairs * 8, width), 1)
    r = lax.broadcasted_iota(jnp.int32, (pairs * 8, width), 0)
    mine = y // group == (r // 8) * 2 + (r & 7) // 4
    fold = (lax.broadcasted_iota(jnp.int32, (width, rows), 0) % group
            == lax.broadcasted_iota(jnp.int32, (width, rows), 1) // 32)
    fold = jnp.where(fold, 1.0, 0.0).astype(BF16)
    for t, value in enumerate((forward, backward)):
        value = jnp.where(live, value, 0.0)
        hi, lo = split(jnp.where(mine, jnp.broadcast_to(value[0:1], mine.shape), 0.0))
        spread = jnp.dot(hi, fold, preferred_element_type=F32) + jnp.dot(lo, fold, preferred_element_type=F32)
        wide_ref[t] = spread.reshape(pairs, 8, rows)

    even = (lax.axis_index("gy") & 1) == 0
    for c in range(3):
        near_ref[c, 0] = jnp.where(even, vel_ref[c, n - 1], vel_ref[c, 0])
        far_ref[c, 0] = jnp.where(even, vel_ref[c, 0], vel_ref[c, n - 1])


def coefs(lower_gap, upper_gap, vel, group):
    n = lower_gap.shape[0]
    width = -(-n // 128) * 128
    row = jax.ShapeDtypeStruct((3, 1, 32, 128), F32)
    return pl.pallas_call(
        functools.partial(coef_kernel, n, group),
        in_specs=[vmem()] * 3,
        out_specs=[vmem()] * 4,
        out_shape=[jax.ShapeDtypeStruct((8, width), F32), held((2, n // (2 * group), 8, group * 32)), row, row],
        scratch_shapes=[held((16, width))],
        compiler_params=limit(4),
        cost_estimate=cost(1e5),
        name="coefficients",
    )(lower_gap, upper_gap, vel)


def pack_kernel(group, v_hbm, vel, pair_ref, left_ref, right_ref, sems):
    n = vel.shape[1]
    pairs = n // (2 * group)

    def copy(p):
        rows = pl.ds(p * 2 * group, 2 * group)
        return pltpu.make_async_copy(v_hbm.at[:, rows], vel.at[:, rows], sems.at[p])

    for p in range(pairs):
        copy(p).start()
    rows = group * 32
    low = sublanes((8, rows)) < 4
    r = lax.broadcasted_iota(jnp.int32, (16, 256), 0)
    lane = lax.broadcasted_iota(jnp.int32, (16, 256), 1) & 127
    inside = jnp.logical_or(r < 4, r >= 12)
    pick = jnp.where(lane == jnp.where(inside, 124, 0) + (r & 3), 1.0, 0.0).astype(BF16)
    for p in range(pairs):
        copy(p).wait()
        for c in range(3):
            picked = []
            for h in range(2):
                f = vel[c, pl.ds((2 * p + h) * group, group)].reshape(rows, 128)
                pair = jnp.concatenate(split(f), axis=1)
                pair_ref[c, pl.ds((2 * p + h) * rows, rows), :] = pair
                picked.append(
                    lax.dot_general(pick, pair, (((1,), (1,)), ((), ())), preferred_element_type=F32)
                )
            one, two = picked
            right_ref[c, p] = jnp.where(low, one[:8], two[8:])
            left_ref[c, p] = jnp.where(low, one[8:], two[:8])


def pack(velocity, group):
    n = velocity.shape[1]
    pairs = n // (2 * group)
    packed = jax.ShapeDtypeStruct((3, pairs, 8, group * 32), F32)
    return pl.pallas_call(
        functools.partial(pack_kernel, group),
        in_specs=[pl.BlockSpec(memory_space=pltpu.HBM)],
        out_specs=[vmem()] * 4,
        out_shape=[held(velocity.shape), pltpu.VMEM((3, n * 32, 256), BF16), packed, packed],
        scratch_shapes=[pltpu.SemaphoreType.DMA((pairs,))],
        compiler_params=limit(8),
        cost_estimate=cost(velocity.size, 4 * velocity.size),
        name="pack_edges",
    )(pltpu.with_memory_space_constraint(velocity, pltpu.HBM))


def main_plain(n, block, group, co, vel_ref, pair_ref, old_hbm, dx_ref, dz_ref, adv_ref, sum_ref, b_ref, old_ref, a_ref, w_ref, sems):
    steps = n // block
    rows = group * 32

    def copy(step):
        here = pl.ds(step * block, block)
        return pltpu.make_async_copy(old_hbm.at[:, here], old_ref.at[:, here], sems.at[step])

    for step in range(steps):
        copy(step).start()
    b_ref[...] = jnp.zeros_like(b_ref)

    def part(step, _):
        copy(step).wait()
        for k in range(block // group):
            i0 = step * block + k * group
            vel = [vel_ref[c, pl.ds(i0, group)].reshape(rows, 128) for c in range(3)]
            for c in range(3):
                f = vel[c]
                pair = pair_ref[c, pl.ds(i0 * 32, rows), :]
                along_x = jnp.dot(pair, dx_ref[...], preferred_element_type=F32)
                both = jnp.dot(dz_ref[...], pair, preferred_element_type=F32)
                along_z = both[:, :128] + both[:, 128:]
                below = jnp.where(i0 == 0, 0.0, vel_ref[c, jnp.maximum(i0 - 1, 0)])
                above = jnp.where(i0 == n - group, 0.0, vel_ref[c, jnp.minimum(i0 + group, n - 1)])
                up = jnp.where(jnp.logical_or(i0 == 0, i0 == n // 2), 0.0, a_ref[c])
                down = b_ref[c]
                for y in range(group):
                    here = slice(32 * y, 32 * y + 32)
                    i = i0 + y
                    under = below if y == 0 else f[32 * y - 32 : 32 * y]
                    over = above if y == group - 1 else f[32 * y + 32 : 32 * y + 64]
                    flat = vel[0][here] * along_x[here] + vel[2][here] * along_z[here]
                    adv = flat + vel[1][here] * ((over - under) * co[INV_GAP, i])
                    force = f[here] + (-UNIT * GAMMA) * adv + ZETA * old_ref[c, i]
                    up = up + co[FORWARD, i] * force
                    down = down + co[BACKWARD, i] * force
                    adv_ref[c, i] = adv
                    sum_ref[c, i] = up
                a_ref[c] = up
                b_ref[c] = down
        return 0

    lax.fori_loop(0, steps, part, 0)


def main_kernel(n, block, group, co, vel_ref, pair_ref, old_ref, dx_ref, dz_ref, adv_ref, sum_ref, b_ref,
                a_ref, w_ref):
    pairs = n // (2 * group)
    half = n // 2
    rows = group * 32
    pieces = 4
    high = rows // pieces

    a_ref[...] = jnp.zeros_like(a_ref)
    b_ref[...] = jnp.zeros_like(b_ref)

    def run(*accs):
        def issue(p, c, first=False):
            parts = [pair_ref[c, pl.ds((h * half + p * group) * 32, rows), :] for h in range(2)]
            sides = [jnp.concatenate([part[:, 128 * t : 128 * t + 128] for part in parts], axis=1) for t in range(2)]
            for t in range(2):
                here = slice(t * rows // 2, (t + 1) * rows // 2)
                pltpu.matmul_push_rhs(jnp.concatenate([side[here] for side in sides], axis=0), t, 1)
            for t in range(2):
                for q in range(pieces):
                    fresh = 0 if first and t == 0 and q == 0 else None
                    pltpu.matmul_acc_lhs(accs[c * 8 + q], sides[t][q * high : (q + 1) * high], load_staged_rhs=fresh)
                for q in range(2 * t, 2 * t + 2):
                    here = slice((q % 2) * high, (q % 2 + 1) * high)
                    pltpu.matmul_acc_lhs(accs[c * 8 + 4 + q], dz_ref[here, :], load_staged_rhs=t if q % 2 == 0 else None)

        def scale(p):
            for h in range(2):
                for y in range(group):
                    i = h * half + p * group + y
                    w_ref[h, y] = vel_ref[1, i] * co[INV_GAP, i]

        def points(p, c):
            up = [a_ref[h, c] for h in range(2)]
            down = b_ref[c]
            for q in range(pieces):
                along_x = pltpu.matmul_pop(accs[c * 8 + q])
                along_z = pltpu.matmul_pop(accs[c * 8 + 4 + q])
                for h in range(2):
                    lanes = slice(128 * h, 128 * h + 128)
                    for k in range(group // pieces):
                        y = q * (group // pieces) + k
                        i = h * half + p * group + y
                        here = slice(32 * k, 32 * k + 32)
                        under = vel_ref[c, jnp.maximum(i - 1, 0)]
                        over = vel_ref[c, jnp.minimum(i + 1, n - 1)]
                        if h == 0 and y == 0:
                            under = jnp.where(p == 0, 0.0, under)
                        if h == 1 and y == group - 1:
                            over = jnp.where(p == pairs - 1, 0.0, over)
                        adv = vel_ref[0, i] * along_x[here, lanes] + vel_ref[2, i] * along_z[here, lanes]
                        adv = adv + w_ref[h, y] * (over - under)
                        force = vel_ref[c, i] + (-UNIT * GAMMA) * adv + ZETA * old_ref[c, i]
                        up[h] = up[h] + co[FORWARD, i] * force
                        down = down + co[BACKWARD, i] * force
                        adv_ref[c, i] = adv
                        sum_ref[c, i] = up[h]
            for h in range(2):
                a_ref[h, c] = up[h]
            b_ref[c] = down

        pltpu.matmul_push_rhs(dx_ref[...], 0, 0)
        for c in range(3):
            issue(0, c, c == 0)

        def part(p, _):
            scale(p)
            for c in range(3):
                points(p, c)
                issue(p + 1, c)
            return 0

        lax.fori_loop(0, pairs - 1, part, 0)
        scale(pairs - 1)
        for c in range(3):
            points(pairs - 1, c)

    pl.run_scoped(run, *(pltpu.ACC(unit)((high, 256), F32) for _ in range(3) for unit in range(2) for _ in range(pieces)))


def main_part(vel, pair, old, table, group, block):
    n = vel.shape[1]
    both_units = group == 8
    dx = shift_matrix(128, False)
    dx = np.kron(np.eye(2), dx) if both_units else np.concatenate([dx, dx])
    dz = np.kron(np.eye(group // 2 if both_units else group), shift_matrix(32, True).T)
    dz = jnp.asarray(np.concatenate([dz, dz], axis=1) if both_units else dz, BF16)
    return pl.pallas_call(
        functools.partial(main_kernel if both_units else main_plain, n, block, group),
        in_specs=[smem(), vmem(), vmem(), vmem() if both_units else pl.BlockSpec(memory_space=pltpu.HBM), vmem(), vmem()],
        out_specs=[vmem()] * 3,
        out_shape=[held(vel.shape), held(vel.shape), held((3, 32, 128))],
        scratch_shapes=[held((2, 3, 32, 128)), held((2, group, 32, 128))] if both_units else [
            held(vel.shape), held((3, 32, 128)), held((2, group, 32, 128)), pltpu.SemaphoreType.DMA((n // group,))],
        compiler_params=limit(6),
        cost_estimate=cost(25 * old.size, 4 * old.size),
        name="inner_part",
    )(table, vel, pair, old if both_units else pltpu.with_memory_space_constraint(old, pltpu.HBM), jnp.asarray(dx, BF16), dz)


def place_matrix():
    r = lax.broadcasted_iota(jnp.int32, (16, 128), 0) & 7
    lane = lax.broadcasted_iota(jnp.int32, (16, 128), 1)
    return jnp.where(lane == jnp.where(r < 4, r, r + 120), 1.0, 0.0).astype(BF16)


def spread_planes(value):
    return lax.dot_general(value, place_matrix(), (((0,), (0,)), ((), ())), preferred_element_type=F32)


def edge_kernel(pairs, group, co, from_left, from_right, left_ref, right_ref, sum_ref, b_ref, wide_ref,
                near_ref, far_ref, vel_ref, extra_ref, rim_ref, load_ref):
    even = (lax.axis_index("gy") & 1) == 0
    n = 2 * pairs * group
    rows = group * 32
    shape = (pairs, 8, rows)
    sub = sublanes((1, 8, rows))
    low = sub[0] < 4
    quarter = sub & 3

    def swap(x):
        return pltpu.roll(x, 4, 0)

    def total(x):
        t = x[0]
        for p in range(1, pairs):
            t = t + x[p]
        t = t + swap(t)
        parts = t[:, 0:32]
        for y in range(1, group):
            parts = parts + t[:, 32 * y : 32 * y + 32]
        return parts

    for c in range(3):
        below = jnp.where(even, far_ref[c, 0], near_ref[c, 0])
        above = jnp.where(even, near_ref[c, 0], far_ref[c, 0])
        rims = (vel_ref[1, 0] * below * (UNIT * co[INV_GAP, 0]),
                -vel_ref[1, n - 1] * above * (UNIT * co[INV_GAP, n - 1]))
        rim_ref[0, c], rim_ref[1, c] = rims
        adv, totals = [], []
        for side, halo, own in ((0, from_left, left_ref), (1, from_right, right_ref)):
            h = halo[c]
            slope = jnp.zeros(shape, F32)
            for d in range(4):
                w = WEIGHTS[3 - d] * UNIT
                if side == 0:
                    weight = jnp.where(quarter + d < 4, -w, 0.0)
                    turned = pltpu.roll(h, 8 - d, 1) if d else h
                else:
                    weight = jnp.where(quarter >= d, w, 0.0)
                    turned = pltpu.roll(h, d, 1) if d else h
                slope = slope + weight * turned
            adv.append(-own[0] * slope)
            force = GAMMA * adv[side]
            totals.append([total(wide_ref[t] * force) for t in range(2)])
        for p in range(pairs):
            l, r = adv[0][p], adv[1][p]
            for h, value in ((0, jnp.where(low, l, swap(r))), (1, jnp.where(low, swap(l), r))):
                extra_ref[c, 2 * p + h] = jnp.concatenate(split(value), axis=0)
        for t, (main, weight, row, i) in enumerate(
            ((b_ref[c], BACKWARD, PHI, 0), (sum_ref[c, n // 2 - 1] + sum_ref[c, n - 1], FORWARD, PSI, n - 1))
        ):
            main = main + (GAMMA * co[weight, 0]) * rims[0] + (GAMMA * co[weight, n - 1]) * rims[1]
            value = jnp.where(low[:, :32], totals[0][1 - t], totals[1][1 - t])
            spread = spread_planes(jnp.concatenate(split(value), axis=0))
            load_ref[pl.ds(t * 96 + c * 32, 32), :] = (main + spread) * co[row, i]
    row = sublanes((8, 128))
    ends = jnp.where(row == 0, co[PSI, 0], co[PSI, n - 1])
    ends = jnp.where(row == 2, co[PHI, 0], ends)
    load_ref[192:200, :] = jnp.where(row == 3, co[PHI, n - 1], ends)


def edge_part(from_left, from_right, left, right, sums, b_sum, wide, near, far, vel, table, group):
    pairs = left.shape[1]
    return pl.pallas_call(
        functools.partial(edge_kernel, pairs, group),
        in_specs=[smem()] + [vmem()] * 10,
        out_specs=[vmem()] * 3,
        out_shape=[pltpu.VMEM((3, 2 * pairs, 16, group * 32), BF16), held((2, 3, 32, 128)),
                   jax.ShapeDtypeStruct((200, 128), F32)],
        compiler_params=limit(8),
        cost_estimate=cost(40 * left.size),
        name="edge_part",
    )(table, from_left, from_right, left, right, sums, b_sum, wide, near, far, vel)


def read(ref):
    return (ref[0:96, :], ref[96:192, :]) + tuple(ref[192 + t : 193 + t, :] for t in range(4))


def write(ref, run):
    ref[0:96, :] = run[0]
    ref[96:192, :] = run[1]
    for t in range(4):
        ref[192 + t : 193 + t, :] = run[2 + t]
    ref[196:200, :] = jnp.zeros((4, 128), F32)


def join(lower, upper):
    f1, l1, pf1, pl1, qf1, ql1 = lower
    f2, l2, pf2, pl2, qf2, ql2 = upper
    inverse = 1.0 / (1.0 - pf2 * ql1)
    over, under = qf1 * inverse, pl2 * inverse
    return (
        f1 + over * (f2 + pf2 * l1),
        l2 + under * (l1 + ql1 * f2),
        pf1 + over * pf2 * pl1,
        under * pl1,
        over * qf2,
        ql2 + under * ql1 * qf2,
    )


def empty():
    zero, one, none = (jnp.zeros((1, 128), F32), jnp.ones((1, 128), F32), jnp.zeros((96, 128), F32))
    return (none, none, zero, one, one, zero)


def join_kernel(bit, opening, closing, token, all_ref, other_ref, *refs):
    me = lax.axis_index("gy")
    if opening:
        lower_in = upper_in = None
        all_out, lower_out, upper_out = refs[:3]
    else:
        lower_in, upper_in, all_out, lower_out, upper_out = refs[:5]
    lower = empty() if opening else read(lower_in)
    upper = empty() if opening else read(upper_in)
    whole, other = read(all_ref), read(other_ref)

    def send(run):
        if closing:
            above_me = (me & (2 * bit)) != 0
            all_out[0:96, :] = jnp.where(above_me, run[0], run[1])
            all_out[96:104, :] = jnp.broadcast_to(jnp.where(above_me, run[2], run[5]), (8, 128))
        else:
            write(all_out, run)

    @pl.when((me & bit) != 0)
    def _():
        send(join(other, whole))
        write(lower_out, join(other, lower))
        write(upper_out, upper)

    @pl.when((me & bit) == 0)
    def _():
        send(join(whole, other))
        write(lower_out, lower)
        write(upper_out, join(upper, other))


def join_runs(bit, closing, token, whole, other, around):
    run = jax.ShapeDtypeStruct((200, 128), F32)
    half = jax.ShapeDtypeStruct((104, 128), F32)
    return pl.pallas_call(
        functools.partial(join_kernel, bit, not around, closing),
        in_specs=[pl.BlockSpec(memory_space=pl.ANY)] + [vmem()] * (2 + len(around)),
        out_specs=[vmem()] * 3,
        out_shape=[half if closing else run, run, run],
        compiler_params=limit(8),
        cost_estimate=cost(20 * whole.size),
        name="join_runs",
    )(token, whole, other, *around)


def couple(bit, me, load, other_ref, lower_ref, upper_ref, below_ref, above_ref):
    lower, upper = read(lower_ref), read(upper_ref)
    vector, scalar = other_ref[0:96, :], other_ref[96:97, :]
    none, zero = jnp.zeros((96, 128), F32), jnp.zeros((1, 128), F32)

    def solve(lower, upper):
        _, a, _, _, _, r = lower
        b, _, q, _, _, _ = upper
        first, last, psi_f, psi_l, phi_f, phi_l = read(load)
        share = 1.0 / (1.0 - psi_f * r)
        a_next = last + psi_l * a + psi_l * r * share * (first + psi_f * a)
        r_next = phi_l + psi_l * r * share * phi_f
        above = (b + q * a_next) / (1.0 - q * r_next)
        above_ref[...] = above
        below_ref[...] = a + r * share * (first + psi_f * a + phi_f * above)

    @pl.when((me & bit) != 0)
    def _():
        solve(join((none, vector, zero, zero, zero, scalar), lower), upper)

    @pl.when((me & bit) == 0)
    def _():
        solve(lower, join(upper, (vector, none, scalar, zero, zero, zero)))


def up_kernel(start, count, block, group, token, co, adv_part, sum_part, extra_ref, rim_ref, *refs):
    n = adv_part.shape[1]
    if start:
        _, before_ref, adv_hbm, sum_ref, end_ref, adv_ref, sems = refs
        end_ref[...] = before_ref[...] + sum_part[:, start - 1]
    else:
        adv_hbm, sum_ref, end_ref, adv_ref, sems = refs
        end_ref[...] = (GAMMA * co[FORWARD, 0]) * rim_ref[0]
    steps = count // block

    def copy(step):
        here = pl.ds(step * block, block)
        there = pl.ds(start + step * block, block)
        return pltpu.make_async_copy(adv_ref.at[:, here], adv_hbm.at[:, there], sems.at[step])

    def part(step, _):
        for c in range(3):
            acc = end_ref[c]
            for k in range(block // group):
                here = step * block + k * group
                spread = spread_planes(extra_ref[c, start // group + step * (block // group) + k])
                for y in range(group):
                    i = here + y
                    extra = spread[32 * y : 32 * y + 32]
                    adv_ref[c, i] = adv_part[c, start + i] * (-UNIT) + extra
                    acc = acc + (GAMMA * co[FORWARD, start + i]) * extra
                    sum_ref[c, i] = sum_part[c, start + i] + acc
            end_ref[c] = acc

        if start == 0:
            @pl.when(step == 0)
            def _():
                adv_ref[:, 0] = adv_ref[:, 0] + rim_ref[0]

        if start + count == n:
            @pl.when(step == steps - 1)
            def _():
                adv_ref[:, count - 1] = adv_ref[:, count - 1] + rim_ref[1]
                sum_ref[:, count - 1] = sum_ref[:, count - 1] + (GAMMA * co[FORWARD, n - 1]) * rim_ref[1]

        copy(step).start()
        return 0

    lax.fori_loop(0, steps, part, 0)

    def finish(step, _):
        copy(step).wait()
        return 0

    lax.fori_loop(0, steps, finish, 0)


def sweep_up(start, count, token, table, adv_part, sums, extra, rims, group, before=()):
    shape = adv_part.shape
    block = max(d for d in range(group, 33, group) if count % d == 0)
    hbm = pl.BlockSpec(memory_space=pltpu.HBM)
    part = (3, count, 32, 128)
    return pl.pallas_call(
        functools.partial(up_kernel, start, count, block, group),
        in_specs=[pl.BlockSpec(memory_space=pl.ANY), smem()] + [vmem()] * 4 + ([hbm, vmem()] if before else []),
        out_specs=[hbm, vmem(), vmem()],
        out_shape=[jax.ShapeDtypeStruct(shape, F32), held(part), held((3, 32, 128))],
        scratch_shapes=[held(part), pltpu.SemaphoreType.DMA((count // block,))],
        input_output_aliases={6: 0} if before else {},
        compiler_params=limit(8),
        cost_estimate=cost(4 * adv_part.size, 2 * adv_part.size),
        name="sweep_up",
    )(token, table, adv_part, sums, extra, rims, *before)


def down_kernel(bit, n, block, co, load, other, lower, upper, low_ref, high_ref, u_hbm, u_ref, below_ref, above_ref,
                sems):
    steps = n // block
    couple(bit, lax.axis_index("gy"), load, other, lower, upper, below_ref, above_ref)
    below = below_ref[...].reshape(3, 32, 128)

    def copy(step):
        here = pl.ds(step * block, block)
        return pltpu.make_async_copy(u_ref.at[:, here], u_hbm.at[:, here], sems.at[step])

    def part(sum_ref, first):
        def run(k, value):
            step = steps // 2 - 1 - k
            for y in reversed(range(block)):
                i = step * block + y
                value = co[OWN, first + i] * (sum_ref[:, i] + below) + co[NEXT, first + i] * value
                u_ref[:, first + i] = value
            copy(first // block + step).start()
            return value

        return run

    value = above_ref[...].reshape(3, 32, 128)
    value = lax.fori_loop(0, steps // 2, part(high_ref, n // 2), value)
    lax.fori_loop(0, steps // 2, part(low_ref, 0), value)

    def finish(step, _):
        copy(step).wait()
        return 0

    lax.fori_loop(0, steps, finish, 0)


def sweep_down(bit, table, load, other, around, sums, block):
    n = 2 * sums[0].shape[1]
    shape = (3, n, 32, 128)
    return pl.pallas_call(
        functools.partial(down_kernel, bit, n, block),
        in_specs=[smem()] + [vmem()] * 6,
        out_specs=pl.BlockSpec(memory_space=pltpu.HBM),
        out_shape=jax.ShapeDtypeStruct(shape, F32),
        scratch_shapes=[held(shape), held((96, 128)), held((96, 128)), pltpu.SemaphoreType.DMA((n // block,))],
        compiler_params=limit(12),
        cost_estimate=cost(12 * sums[0].size, 8 * sums[0].size),
        name="sweep_down",
    )(table, load, other, *around, *sums)


def shards(velocity, old_advection, lower_gap, upper_gap):
    n = velocity.shape[1]
    group = max(d for d in range(1, 9) if n % (2 * d) == 0)
    block = 2 * group
    nx, ny = lax.axis_size("gx"), lax.axis_size("gy")
    ring = [(i, (i + 1) % nx) for i in range(nx)]
    pairs = [(i, i ^ 1) for i in range(ny)]
    others = [(i, j) for k in range(1, ny - 1, 2) for i, j in ((k, k + 1), (k + 1, k))]

    vel, pair, left, right = pack(velocity, group)
    from_left = lax.ppermute(right, "gx", ring)
    from_right = lax.ppermute(left, "gx", [(j, i) for i, j in ring])
    table, wide, near, far = coefs(lower_gap, upper_gap, vel, group)
    near = lax.ppermute(near, "gy", pairs)
    far = lax.ppermute(far, "gy", others)
    adv_part, sums, b_sum = main_part(vel, pair, old_advection, table, group, block)
    extra, rims, load = edge_part(
        from_left, from_right, left, right, sums, b_sum, wide, near, far, vel, table, group
    )
    bits = [1 << t for t in range(ny.bit_length() - 1)]
    half = n // 2
    whole, around, token = load, [], load
    for bit in bits:
        other = lax.ppermute(whole, "gy", [(i, i ^ bit) for i in range(ny)])
        if bit != bits[-1]:
            whole, *around = join_runs(bit, 2 * bit == bits[-1], token, whole, other, around)
        if bit == bits[0]:
            adv, low, end = sweep_up(0, half, whole, table, adv_part, sums, extra, rims, group)
            token = end
    adv, high, _ = sweep_up(half, half, whole, table, adv_part, sums, extra, rims, group, (adv, end))
    down_block = block if half % block == 0 else group
    return sweep_down(bits[-1], table, load, other, around, (low, high), down_block), adv


def solution(mesh):
    spec = P(None, "gy", None, "gx")
    return jax.shard_map(
        shards,
        mesh=mesh,
        in_specs=(spec, spec, P("gy"), P("gy")),
        out_specs=(spec, spec),
        check_vma=False,
    )
```

```python
import functools

import jax
import jax.numpy as jnp
import numpy as np
from jax import lax
from jax.experimental import pallas as pl
from jax.experimental.pallas import tpu as pltpu
from jax.sharding import PartitionSpec as P

STIFF = 1024
GAMMA = 5.0 / 12.0
ZETA = -17.0 / 60.0
WEIGHTS = (672.0, -168.0, 32.0, -3.0)
UNIT = 1.0 / 840.0
F32 = jnp.float32
BF16 = jnp.bfloat16
MIB = 1 << 20

INV_GAP, FORWARD, BACKWARD, PSI, PHI, OWN, NEXT = range(7)


def shift_matrix(size, periodic):
    m = np.zeros((size, size), np.float32)
    for j in range(size):
        for k, w in enumerate(WEIGHTS, 1):
            for i, s in ((j + k, w), (j - k, -w)):
                if periodic:
                    m[i % size, j] += s
                elif 0 <= i < size:
                    m[i, j] += s
    return m


def split(values):
    hi = values.astype(BF16)
    return hi, (values - hi.astype(F32)).astype(BF16)


def sublanes(shape):
    return lax.broadcasted_iota(jnp.int32, shape, len(shape) - 2)


def vmem():
    return pl.BlockSpec(memory_space=pltpu.VMEM)


def limit(mib):
    return pltpu.CompilerParams(vmem_limit_bytes=mib * MIB)


def cost(flops, moved=0):
    return pl.CostEstimate(flops=int(flops), bytes_accessed=int(moved), transcendentals=0)


def held(shape):
    return pltpu.VMEM(shape, F32)


def coef_kernel(n, group, lower_ref, upper_ref, vel_ref, out_ref, wide_ref, near_ref, far_ref, gap_ref):
    width = gap_ref.shape[1]
    shape = (8, width)
    lane = lax.broadcasted_iota(jnp.int32, shape, 1)
    gap_ref[...] = jnp.ones_like(gap_ref)
    gap_ref[0:8, 0:n] = jnp.broadcast_to(lower_ref[...].reshape(1, n), (8, n))
    gap_ref[8:16, 0:n] = jnp.broadcast_to(upper_ref[...].reshape(1, n), (8, n))
    lower, upper = gap_ref[0:8, :], gap_ref[8:16, :]
    gap_sum = lower + upper
    kappa = gap_sum * (0.5 / STIFF)
    live = lane < n

    def at(values, place):
        return jnp.sum(jnp.where(lane == place, values, 0.0), axis=1, keepdims=True)

    def sweep(gap, start, backward):
        one, zero = jnp.ones(shape, F32), jnp.zeros(shape, F32)
        m = [jnp.where(live, v, w) for v, w in
             ((1.0 + gap * kappa, one), (gap, zero), (kappa, zero), (one, one))]
        s = 1
        while s < n:
            inside = lane < width - s if backward else lane >= s
            turn = width - s if backward else s
            a, b, c, d = (jnp.where(inside, pltpu.roll(v, turn, 1), w)
                          for v, w in zip(m, (one, zero, zero, one)))
            m = [m[0] * a + m[1] * c, m[0] * b + m[1] * d, m[2] * a + m[3] * c, m[2] * b + m[3] * d]
            s *= 2
        return m[0] * start + m[1]

    first, last = at(lower, 0), at(upper, n - 1)
    phi_next = sweep(upper, first, False)
    psi_next = sweep(lower, last, True)
    phi = jnp.where(lane == 0, first, pltpu.roll(phi_next, 1, 1))
    psi = jnp.where(lane == n - 1, last, pltpu.roll(psi_next, width - 1, 1))
    scale = 1.0 / at(phi_next, n - 1)
    forward, backward = phi * kappa, psi * kappa
    sub = sublanes(shape)
    table = jnp.zeros(shape, F32)
    for row, value in ((INV_GAP, (1.0 / UNIT) / gap_sum), (FORWARD, forward), (BACKWARD, backward),
                       (PSI, psi * scale), (PHI, phi * scale), (OWN, upper / phi_next), (NEXT, phi / phi_next)):
        table = jnp.where(jnp.logical_and(sub == row, live), value, table)
    high = split(table)[0]
    middle, low = split(table - high.astype(F32))
    parts = jnp.concatenate([high, middle, low, jnp.zeros_like(low)], axis=0)
    count = out_ref.shape[0]
    k = lax.broadcasted_iota(jnp.int32, (32, count * 128), 0)
    t = lax.broadcasted_iota(jnp.int32, (32, count * 128), 1) // 128
    pick = jnp.where(jnp.logical_and((k & 7) == t, k < 24), 1.0, 0.0).astype(BF16)
    rows = lax.dot_general(parts, pick, (((0,), (0,)), ((), ())), preferred_element_type=F32)
    for row in range(count):
        out_ref[row] = rows[:n, 128 * row : 128 * row + 128]

    pairs, rows = wide_ref.shape[1], wide_ref.shape[3]
    y = lax.broadcasted_iota(jnp.int32, (pairs * 8, width), 1)
    r = lax.broadcasted_iota(jnp.int32, (pairs * 8, width), 0)
    mine = y // group == (r // 8) * 2 + (r & 7) // 4
    fold = (lax.broadcasted_iota(jnp.int32, (width, rows), 0) % group
            == lax.broadcasted_iota(jnp.int32, (width, rows), 1) // 32)
    fold = jnp.where(fold, 1.0, 0.0).astype(BF16)
    for t, value in enumerate((forward, backward)):
        value = jnp.where(live, value, 0.0)
        hi, lo = split(jnp.where(mine, jnp.broadcast_to(value[0:1], mine.shape), 0.0))
        spread = jnp.dot(hi, fold, preferred_element_type=F32) + jnp.dot(lo, fold, preferred_element_type=F32)
        wide_ref[t] = spread.reshape(pairs, 8, rows)

    even = (lax.axis_index("gy") & 1) == 0
    for c in range(3):
        near_ref[c, 0] = jnp.where(even, vel_ref[c, n - 1], vel_ref[c, 0])
        far_ref[c, 0] = jnp.where(even, vel_ref[c, 0], vel_ref[c, n - 1])


def coefs(lower_gap, upper_gap, vel, group):
    n = lower_gap.shape[0]
    width = -(-n // 128) * 128
    row = jax.ShapeDtypeStruct((3, 1, 32, 128), F32)
    return pl.pallas_call(
        functools.partial(coef_kernel, n, group),
        in_specs=[vmem()] * 3,
        out_specs=[vmem()] * 4,
        out_shape=[held((NEXT + 1, n, 128)), held((2, n // (2 * group), 8, group * 32)), row, row],
        scratch_shapes=[held((16, width))],
        compiler_params=limit(4),
        cost_estimate=cost(1e5),
        name="coefficients",
    )(lower_gap, upper_gap, vel)


def pack_kernel(group, v_hbm, vel, pair_ref, left_ref, right_ref, sems):
    n = vel.shape[1]
    pairs = n // (2 * group)

    cuts = [2, 2, 2, 2, 2, 2] if pairs == 12 else [1] * pairs
    starts = [sum(cuts[:k]) for k in range(len(cuts))]

    def copy(k):
        rows = pl.ds(starts[k] * 2 * group, cuts[k] * 2 * group)
        return pltpu.make_async_copy(v_hbm.at[:, rows], vel.at[:, rows], sems.at[k])

    for k in range(len(cuts)):
        copy(k).start()
    rows = group * 32
    low = sublanes((8, rows)) < 4
    r = lax.broadcasted_iota(jnp.int32, (16, 256), 0)
    lane = lax.broadcasted_iota(jnp.int32, (16, 256), 1) & 127
    inside = jnp.logical_or(r < 4, r >= 12)
    pick = jnp.where(lane == jnp.where(inside, 124, 0) + (r & 3), 1.0, 0.0).astype(BF16)
    for p in range(pairs):
        if p in starts:
            copy(starts.index(p)).wait()
        for c in range(3):
            picked = []
            for h in range(2):
                f = vel[c, pl.ds((2 * p + h) * group, group)].reshape(rows, 128)
                pair = jnp.concatenate(split(f), axis=1)
                pair_ref[c, pl.ds((2 * p + h) * rows, rows), :] = pair
                picked.append(
                    lax.dot_general(pick, pair, (((1,), (1,)), ((), ())), preferred_element_type=F32)
                )
            one, two = picked
            right_ref[c, p] = jnp.where(low, one[:8], two[8:])
            left_ref[c, p] = jnp.where(low, one[8:], two[:8])


def pack(velocity, group):
    n = velocity.shape[1]
    pairs = n // (2 * group)
    packed = jax.ShapeDtypeStruct((3, pairs, 8, group * 32), F32)
    return pl.pallas_call(
        functools.partial(pack_kernel, group),
        in_specs=[pl.BlockSpec(memory_space=pltpu.HBM)],
        out_specs=[vmem()] * 4,
        out_shape=[held(velocity.shape), pltpu.VMEM((3, n * 32, 256), BF16), packed, packed],
        scratch_shapes=[pltpu.SemaphoreType.DMA((pairs,))],
        compiler_params=limit(8),
        cost_estimate=cost(velocity.size, 4 * velocity.size),
        name="pack_edges",
    )(pltpu.with_memory_space_constraint(velocity, pltpu.HBM))


def main_plain(n, block, group, co, vel_ref, pair_ref, old_hbm, dx_ref, dz_ref, adv_ref, sum_ref, b_ref, old_ref, a_ref, w_ref, sems):
    steps = n // block
    rows = group * 32

    def copy(step):
        here = pl.ds(step * block, block)
        return pltpu.make_async_copy(old_hbm.at[:, here], old_ref.at[:, here], sems.at[step])

    for step in range(steps):
        copy(step).start()
    b_ref[...] = jnp.zeros_like(b_ref)

    def part(step, _):
        copy(step).wait()
        for k in range(block // group):
            i0 = step * block + k * group
            vel = [vel_ref[c, pl.ds(i0, group)].reshape(rows, 128) for c in range(3)]
            for c in range(3):
                f = vel[c]
                pair = pair_ref[c, pl.ds(i0 * 32, rows), :]
                along_x = jnp.dot(pair, dx_ref[...], preferred_element_type=F32)
                both = jnp.dot(dz_ref[...], pair, preferred_element_type=F32)
                along_z = both[:, :128] + both[:, 128:]
                below = jnp.where(i0 == 0, 0.0, vel_ref[c, jnp.maximum(i0 - 1, 0)])
                above = jnp.where(i0 == n - group, 0.0, vel_ref[c, jnp.minimum(i0 + group, n - 1)])
                up = jnp.where(jnp.logical_or(i0 == 0, i0 == n // 2), 0.0, a_ref[c])
                down = b_ref[c]
                for y in range(group):
                    here = slice(32 * y, 32 * y + 32)
                    i = i0 + y
                    under = below if y == 0 else f[32 * y - 32 : 32 * y]
                    over = above if y == group - 1 else f[32 * y + 32 : 32 * y + 64]
                    flat = vel[0][here] * along_x[here] + vel[2][here] * along_z[here]
                    adv = flat + vel[1][here] * ((over - under) * co[INV_GAP, pl.ds(i, 1), :])
                    force = f[here] + (-UNIT * GAMMA) * adv + ZETA * old_ref[c, i]
                    up = up + co[FORWARD, pl.ds(i, 1), :] * force
                    down = down + co[BACKWARD, pl.ds(i, 1), :] * force
                    adv_ref[c, i] = adv
                    sum_ref[c, i] = up
                a_ref[c] = up
                b_ref[c] = down
        return 0

    lax.fori_loop(0, steps, part, 0)


def main_kernel(n, block, group, co, vel_ref, pair_ref, old_ref, dx_ref, dz_ref, adv_ref, sum_ref, b_ref,
                a_ref, w_ref):
    pairs = n // (2 * group)
    half = n // 2
    rows = group * 32
    pieces = 4
    high = rows // pieces

    a_ref[...] = jnp.zeros_like(a_ref)
    b_ref[...] = jnp.zeros_like(b_ref)

    def run(*accs):
        def issue(p, c, first=False):
            parts = [pair_ref[c, pl.ds((h * half + p * group) * 32, rows), :] for h in range(2)]
            sides = [jnp.concatenate([part[:, 128 * t : 128 * t + 128] for part in parts], axis=1) for t in range(2)]
            for t in range(2):
                here = slice(t * rows // 2, (t + 1) * rows // 2)
                pltpu.matmul_push_rhs(jnp.concatenate([side[here] for side in sides], axis=0), t, 1)
            for t in range(2):
                for q in range(pieces):
                    fresh = 0 if first and t == 0 and q == 0 else None
                    pltpu.matmul_acc_lhs(accs[c * 8 + q], sides[t][q * high : (q + 1) * high], load_staged_rhs=fresh)
                for q in range(2 * t, 2 * t + 2):
                    here = slice((q % 2) * high, (q % 2 + 1) * high)
                    pltpu.matmul_acc_lhs(accs[c * 8 + 4 + q], dz_ref[here, :], load_staged_rhs=t if q % 2 == 0 else None)

        def scale(p):
            for h in range(2):
                for y in range(group):
                    i = h * half + p * group + y
                    w_ref[h, y] = vel_ref[1, i] * co[INV_GAP, pl.ds(i, 1), :]

        def points(p, c):
            up = [a_ref[h, c] for h in range(2)]
            down = b_ref[c]
            for q in range(pieces):
                along_x = pltpu.matmul_pop(accs[c * 8 + q])
                along_z = pltpu.matmul_pop(accs[c * 8 + 4 + q])
                for h in range(2):
                    lanes = slice(128 * h, 128 * h + 128)
                    for k in range(group // pieces):
                        y = q * (group // pieces) + k
                        i = h * half + p * group + y
                        here = slice(32 * k, 32 * k + 32)
                        under = vel_ref[c, jnp.maximum(i - 1, 0)]
                        over = vel_ref[c, jnp.minimum(i + 1, n - 1)]
                        if h == 0 and y == 0:
                            under = jnp.where(p == 0, 0.0, under)
                        if h == 1 and y == group - 1:
                            over = jnp.where(p == pairs - 1, 0.0, over)
                        adv = vel_ref[0, i] * along_x[here, lanes] + vel_ref[2, i] * along_z[here, lanes]
                        adv = adv + w_ref[h, y] * (over - under)
                        force = vel_ref[c, i] + (-UNIT * GAMMA) * adv + ZETA * old_ref[c, i]
                        up[h] = up[h] + co[FORWARD, pl.ds(i, 1), :] * force
                        down = down + co[BACKWARD, pl.ds(i, 1), :] * force
                        adv_ref[c, i] = adv
                        sum_ref[c, i] = up[h]
            for h in range(2):
                a_ref[h, c] = up[h]
            b_ref[c] = down

        pltpu.matmul_push_rhs(dx_ref[...], 0, 0)
        for c in range(3):
            issue(0, c, c == 0)

        def part(p, _):
            scale(p)
            for c in range(3):
                points(p, c)
                issue(p + 1, c)
            return 0

        lax.fori_loop(0, pairs - 1, part, 0)
        scale(pairs - 1)
        for c in range(3):
            points(pairs - 1, c)

    pl.run_scoped(run, *(pltpu.ACC(unit)((high, 256), F32) for _ in range(3) for unit in range(2) for _ in range(pieces)))


def main_part(vel, pair, old, table, group, block):
    n = vel.shape[1]
    both_units = group == 8
    dx = shift_matrix(128, False)
    dx = np.kron(np.eye(2), dx) if both_units else np.concatenate([dx, dx])
    dz = np.kron(np.eye(group // 2 if both_units else group), shift_matrix(32, True).T)
    dz = jnp.asarray(np.concatenate([dz, dz], axis=1) if both_units else dz, BF16)
    return pl.pallas_call(
        functools.partial(main_kernel if both_units else main_plain, n, block, group),
        in_specs=[vmem(), vmem(), vmem(), vmem() if both_units else pl.BlockSpec(memory_space=pltpu.HBM), vmem(), vmem()],
        out_specs=[vmem()] * 3,
        out_shape=[held(vel.shape), held(vel.shape), held((3, 32, 128))],
        scratch_shapes=[held((2, 3, 32, 128)), held((2, group, 32, 128))] if both_units else [
            held(vel.shape), held((3, 32, 128)), held((2, group, 32, 128)), pltpu.SemaphoreType.DMA((n // group,))],
        compiler_params=limit(6),
        cost_estimate=cost(25 * old.size, 4 * old.size),
        name="inner_part",
    )(table, vel, pair, old if both_units else pltpu.with_memory_space_constraint(old, pltpu.HBM), jnp.asarray(dx, BF16), dz)


def place_matrix():
    r = lax.broadcasted_iota(jnp.int32, (16, 128), 0) & 7
    lane = lax.broadcasted_iota(jnp.int32, (16, 128), 1)
    return jnp.where(lane == jnp.where(r < 4, r, r + 120), 1.0, 0.0).astype(BF16)


def spread_planes(value):
    return lax.dot_general(value, place_matrix(), (((0,), (0,)), ((), ())), preferred_element_type=F32)


def edge_kernel(pairs, group, co, from_left, from_right, left_ref, right_ref, sum_ref, b_ref, wide_ref,
                near_ref, far_ref, vel_ref, extra_ref, rim_ref, load_ref):
    even = (lax.axis_index("gy") & 1) == 0
    n = 2 * pairs * group
    rows = group * 32
    shape = (pairs, 8, rows)
    sub = sublanes((1, 8, rows))
    low = sub[0] < 4
    quarter = sub & 3

    def swap(x):
        return pltpu.roll(x, 4, 0)

    def total(x):
        t = x[0]
        for p in range(1, pairs):
            t = t + x[p]
        t = t + swap(t)
        parts = t[:, 0:32]
        for y in range(1, group):
            parts = parts + t[:, 32 * y : 32 * y + 32]
        return parts

    for c in range(3):
        below = jnp.where(even, far_ref[c, 0], near_ref[c, 0])
        above = jnp.where(even, near_ref[c, 0], far_ref[c, 0])
        rims = (vel_ref[1, 0] * below * (UNIT * co[INV_GAP, pl.ds(0, 1), :]),
                -vel_ref[1, n - 1] * above * (UNIT * co[INV_GAP, pl.ds(n - 1, 1), :]))
        rim_ref[0, c], rim_ref[1, c] = rims
        adv, totals = [], []
        for side, halo, own in ((0, from_left, left_ref), (1, from_right, right_ref)):
            h = halo[c]
            slope = jnp.zeros(shape, F32)
            for d in range(4):
                w = WEIGHTS[3 - d] * UNIT
                if side == 0:
                    weight = jnp.where(quarter + d < 4, -w, 0.0)
                    turned = pltpu.roll(h, 8 - d, 1) if d else h
                else:
                    weight = jnp.where(quarter >= d, w, 0.0)
                    turned = pltpu.roll(h, d, 1) if d else h
                slope = slope + weight * turned
            adv.append(-own[0] * slope)
            force = GAMMA * adv[side]
            totals.append([total(wide_ref[t] * force) for t in range(2)])
        for p in range(pairs):
            l, r = adv[0][p], adv[1][p]
            for h, value in ((0, jnp.where(low, l, swap(r))), (1, jnp.where(low, swap(l), r))):
                extra_ref[c, 2 * p + h] = jnp.concatenate(split(value), axis=0)
        for t, (main, weight, row, i) in enumerate(
            ((b_ref[c], BACKWARD, PHI, 0), (sum_ref[c, n // 2 - 1] + sum_ref[c, n - 1], FORWARD, PSI, n - 1))
        ):
            main = main + (GAMMA * co[weight, pl.ds(0, 1), :]) * rims[0] + (GAMMA * co[weight, pl.ds(n - 1, 1), :]) * rims[1]
            value = jnp.where(low[:, :32], totals[0][1 - t], totals[1][1 - t])
            spread = spread_planes(jnp.concatenate(split(value), axis=0))
            load_ref[pl.ds(t * 96 + c * 32, 32), :] = (main + spread) * co[row, pl.ds(i, 1), :]
    row = sublanes((8, 128))
    ends = jnp.where(row == 0, co[PSI, pl.ds(0, 1), :], co[PSI, pl.ds(n - 1, 1), :])
    ends = jnp.where(row == 2, co[PHI, pl.ds(0, 1), :], ends)
    load_ref[192:200, :] = jnp.where(row == 3, co[PHI, pl.ds(n - 1, 1), :], ends)


def edge_part(from_left, from_right, left, right, sums, b_sum, wide, near, far, vel, table, group):
    pairs = left.shape[1]
    return pl.pallas_call(
        functools.partial(edge_kernel, pairs, group),
        in_specs=[vmem()] + [vmem()] * 10,
        out_specs=[vmem()] * 3,
        out_shape=[pltpu.VMEM((3, 2 * pairs, 16, group * 32), BF16), held((2, 3, 32, 128)),
                   jax.ShapeDtypeStruct((200, 128), F32)],
        compiler_params=limit(8),
        cost_estimate=cost(40 * left.size),
        name="edge_part",
    )(table, from_left, from_right, left, right, sums, b_sum, wide, near, far, vel)


def read(ref):
    return (ref[0:96, :], ref[96:192, :]) + tuple(ref[192 + t : 193 + t, :] for t in range(4))


def write(ref, run):
    ref[0:96, :] = run[0]
    ref[96:192, :] = run[1]
    for t in range(4):
        ref[192 + t : 193 + t, :] = run[2 + t]
    ref[196:200, :] = jnp.zeros((4, 128), F32)


def join(lower, upper):
    f1, l1, pf1, pl1, qf1, ql1 = lower
    f2, l2, pf2, pl2, qf2, ql2 = upper
    inverse = 1.0 / (1.0 - pf2 * ql1)
    over, under = qf1 * inverse, pl2 * inverse
    return (
        f1 + over * (f2 + pf2 * l1),
        l2 + under * (l1 + ql1 * f2),
        pf1 + over * pf2 * pl1,
        under * pl1,
        over * qf2,
        ql2 + under * ql1 * qf2,
    )


def empty():
    zero, one, none = (jnp.zeros((1, 128), F32), jnp.ones((1, 128), F32), jnp.zeros((96, 128), F32))
    return (none, none, zero, one, one, zero)


def join_kernel(bit, opening, closing, token, all_ref, other_ref, *refs):
    me = lax.axis_index("gy")
    if opening:
        lower_in = upper_in = None
        all_out, lower_out, upper_out = refs[:3]
    else:
        lower_in, upper_in, all_out, lower_out, upper_out = refs[:5]
    lower = empty() if opening else read(lower_in)
    upper = empty() if opening else read(upper_in)
    whole, other = read(all_ref), read(other_ref)

    def send(run):
        if closing:
            above_me = (me & (2 * bit)) != 0
            all_out[0:96, :] = jnp.where(above_me, run[0], run[1])
            all_out[96:104, :] = jnp.broadcast_to(jnp.where(above_me, run[2], run[5]), (8, 128))
        else:
            write(all_out, run)

    @pl.when((me & bit) != 0)
    def _():
        send(join(other, whole))
        write(lower_out, join(other, lower))
        write(upper_out, upper)

    @pl.when((me & bit) == 0)
    def _():
        send(join(whole, other))
        write(lower_out, lower)
        write(upper_out, join(upper, other))


def join_runs(bit, closing, token, whole, other, around):
    run = jax.ShapeDtypeStruct((200, 128), F32)
    half = jax.ShapeDtypeStruct((104, 128), F32)
    return pl.pallas_call(
        functools.partial(join_kernel, bit, not around, closing),
        in_specs=[pl.BlockSpec(memory_space=pl.ANY)] + [vmem()] * (2 + len(around)),
        out_specs=[vmem()] * 3,
        out_shape=[half if closing else run, run, run],
        compiler_params=limit(8),
        cost_estimate=cost(20 * whole.size),
        name="join_runs",
    )(token, whole, other, *around)


def couple(bit, me, load, other_ref, lower_ref, upper_ref, below_ref, above_ref):
    lower, upper = read(lower_ref), read(upper_ref)
    vector, scalar = other_ref[0:96, :], other_ref[96:97, :]
    none, zero = jnp.zeros((96, 128), F32), jnp.zeros((1, 128), F32)

    def solve(lower, upper):
        _, a, _, _, _, r = lower
        b, _, q, _, _, _ = upper
        first, last, psi_f, psi_l, phi_f, phi_l = read(load)
        share = 1.0 / (1.0 - psi_f * r)
        a_next = last + psi_l * a + psi_l * r * share * (first + psi_f * a)
        r_next = phi_l + psi_l * r * share * phi_f
        above = (b + q * a_next) / (1.0 - q * r_next)
        above_ref[...] = above
        below_ref[...] = a + r * share * (first + psi_f * a + phi_f * above)

    @pl.when((me & bit) != 0)
    def _():
        solve(join((none, vector, zero, zero, zero, scalar), lower), upper)

    @pl.when((me & bit) == 0)
    def _():
        solve(lower, join(upper, (vector, none, scalar, zero, zero, zero)))


def up_kernel(start, count, block, group, token, co, adv_part, sum_part, extra_ref, rim_ref, *refs):
    n = adv_part.shape[1]
    if start:
        _, before_ref, adv_hbm, sum_ref, end_ref, adv_ref, sems = refs
        end_ref[...] = before_ref[...] + sum_part[:, start - 1]
    else:
        adv_hbm, sum_ref, end_ref, adv_ref, sems = refs
        end_ref[...] = (GAMMA * co[FORWARD, pl.ds(0, 1), :]) * rim_ref[0]
    steps = count // block

    def copy(step):
        here = pl.ds(step * block, block)
        there = pl.ds(start + step * block, block)
        return pltpu.make_async_copy(adv_ref.at[:, here], adv_hbm.at[:, there], sems.at[step])

    def part(step, _):
        for c in range(3):
            acc = end_ref[c]
            for k in range(block // group):
                here = step * block + k * group
                spread = spread_planes(extra_ref[c, start // group + step * (block // group) + k])
                for y in range(group):
                    i = here + y
                    extra = spread[32 * y : 32 * y + 32]
                    adv_ref[c, i] = adv_part[c, start + i] * (-UNIT) + extra
                    acc = acc + (GAMMA * co[FORWARD, pl.ds(start + i, 1), :]) * extra
                    sum_ref[c, i] = sum_part[c, start + i] + acc
            end_ref[c] = acc

        if start == 0:
            @pl.when(step == 0)
            def _():
                adv_ref[:, 0] = adv_ref[:, 0] + rim_ref[0]

        if start + count == n:
            @pl.when(step == steps - 1)
            def _():
                adv_ref[:, count - 1] = adv_ref[:, count - 1] + rim_ref[1]
                sum_ref[:, count - 1] = sum_ref[:, count - 1] + (GAMMA * co[FORWARD, pl.ds(n - 1, 1), :]) * rim_ref[1]

        copy(step).start()
        return 0

    lax.fori_loop(0, steps, part, 0)

    def finish(step, _):
        copy(step).wait()
        return 0

    lax.fori_loop(0, steps, finish, 0)


def sweep_up(start, count, token, table, adv_part, sums, extra, rims, group, before=()):
    shape = adv_part.shape
    block = max(d for d in range(group, 33, group) if count % d == 0)
    hbm = pl.BlockSpec(memory_space=pltpu.HBM)
    part = (3, count, 32, 128)
    return pl.pallas_call(
        functools.partial(up_kernel, start, count, block, group),
        in_specs=[pl.BlockSpec(memory_space=pl.ANY), vmem()] + [vmem()] * 4 + ([hbm, vmem()] if before else []),
        out_specs=[hbm, vmem(), vmem()],
        out_shape=[jax.ShapeDtypeStruct(shape, F32), held(part), held((3, 32, 128))],
        scratch_shapes=[held(part), pltpu.SemaphoreType.DMA((count // block,))],
        input_output_aliases={6: 0} if before else {},
        compiler_params=limit(8),
        cost_estimate=cost(4 * adv_part.size, 2 * adv_part.size),
        name="sweep_up",
    )(token, table, adv_part, sums, extra, rims, *before)


def down_kernel(bit, n, block, co, load, other, lower, upper, low_ref, high_ref, u_hbm, u_ref, below_ref, above_ref,
                sems):
    steps = n // block
    couple(bit, lax.axis_index("gy"), load, other, lower, upper, below_ref, above_ref)
    below = below_ref[...].reshape(3, 32, 128)

    def copy(step):
        here = pl.ds(step * block, block)
        return pltpu.make_async_copy(u_ref.at[:, here], u_hbm.at[:, here], sems.at[step])

    def part(sum_ref, first):
        def run(k, value):
            step = steps // 2 - 1 - k
            for y in reversed(range(block)):
                i = step * block + y
                value = co[OWN, pl.ds(first + i, 1), :] * (sum_ref[:, i] + below) + co[NEXT, pl.ds(first + i, 1), :] * value
                u_ref[:, first + i] = value
            copy(first // block + step).start()
            return value

        return run

    value = above_ref[...].reshape(3, 32, 128)
    value = lax.fori_loop(0, steps // 2, part(high_ref, n // 2), value)
    lax.fori_loop(0, steps // 2, part(low_ref, 0), value)

    def finish(step, _):
        copy(step).wait()
        return 0

    lax.fori_loop(0, steps, finish, 0)


def sweep_down(bit, table, load, other, around, sums, block):
    n = 2 * sums[0].shape[1]
    shape = (3, n, 32, 128)
    return pl.pallas_call(
        functools.partial(down_kernel, bit, n, block),
        in_specs=[vmem()] + [vmem()] * 6,
        out_specs=pl.BlockSpec(memory_space=pltpu.HBM),
        out_shape=jax.ShapeDtypeStruct(shape, F32),
        scratch_shapes=[held(shape), held((96, 128)), held((96, 128)), pltpu.SemaphoreType.DMA((n // block,))],
        compiler_params=limit(12),
        cost_estimate=cost(12 * sums[0].size, 8 * sums[0].size),
        name="sweep_down",
    )(table, load, other, *around, *sums)


def shards(velocity, old_advection, lower_gap, upper_gap):
    n = velocity.shape[1]
    group = max(d for d in range(1, 9) if n % (2 * d) == 0)
    block = 2 * group
    nx, ny = lax.axis_size("gx"), lax.axis_size("gy")
    ring = [(i, (i + 1) % nx) for i in range(nx)]
    pairs = [(i, i ^ 1) for i in range(ny)]
    others = [(i, j) for k in range(1, ny - 1, 2) for i, j in ((k, k + 1), (k + 1, k))]

    vel, pair, left, right = pack(velocity, group)
    from_left = lax.ppermute(right, "gx", ring)
    from_right = lax.ppermute(left, "gx", [(j, i) for i, j in ring])
    table, wide, near, far = coefs(lower_gap, upper_gap, vel, group)
    near = lax.ppermute(near, "gy", pairs)
    far = lax.ppermute(far, "gy", others)
    adv_part, sums, b_sum = main_part(vel, pair, old_advection, table, group, block)
    extra, rims, load = edge_part(
        from_left, from_right, left, right, sums, b_sum, wide, near, far, vel, table, group
    )
    bits = [1 << t for t in range(ny.bit_length() - 1)]
    half = n // 2
    whole, around, token = load, [], load
    for bit in bits:
        other = lax.ppermute(whole, "gy", [(i, i ^ bit) for i in range(ny)])
        if bit != bits[-1]:
            whole, *around = join_runs(bit, 2 * bit == bits[-1], token, whole, other, around)
        if bit == bits[0]:
            adv, low, end = sweep_up(0, half, whole, table, adv_part, sums, extra, rims, group)
            token = end
    adv, high, _ = sweep_up(half, half, whole, table, adv_part, sums, extra, rims, group, (adv, end))
    down_block = block if half % block == 0 else group
    return sweep_down(bits[-1], table, load, other, around, (low, high), down_block), adv


def solution(mesh):
    spec = P(None, "gy", None, "gx")
    return jax.shard_map(
        shards,
        mesh=mesh,
        in_specs=(spec, spec, P("gy"), P("gy")),
        out_specs=(spec, spec),
        check_vma=False,
    )
```

```python
import functools

import jax
import jax.numpy as jnp
import numpy as np
from jax import lax
from jax.experimental import pallas as pl
from jax.experimental.pallas import tpu as pltpu
from jax.sharding import PartitionSpec as P

STIFF = 1024
GAMMA = 5.0 / 12.0
ZETA = -17.0 / 60.0
WEIGHTS = (672.0, -168.0, 32.0, -3.0)
UNIT = 1.0 / 840.0
F32 = jnp.float32
BF16 = jnp.bfloat16
MIB = 1 << 20
CUT = 16

INV_GAP, FORWARD, BACKWARD, PSI, PHI, OWN, NEXT = range(7)


def shift_matrix(size, periodic):
    m = np.zeros((size, size), np.float32)
    for j in range(size):
        for k, w in enumerate(WEIGHTS, 1):
            for i, s in ((j + k, w), (j - k, -w)):
                if periodic:
                    m[i % size, j] += s
                elif 0 <= i < size:
                    m[i, j] += s
    return m


def split(values):
    hi = values.astype(BF16)
    return hi, (values - hi.astype(F32)).astype(BF16)


def sublanes(shape):
    return lax.broadcasted_iota(jnp.int32, shape, len(shape) - 2)


def vmem():
    return pl.BlockSpec(memory_space=pltpu.VMEM)


def limit(mib):
    return pltpu.CompilerParams(vmem_limit_bytes=mib * MIB)


def cost(flops, moved=0):
    return pl.CostEstimate(flops=int(flops), bytes_accessed=int(moved), transcendentals=0)


def held(shape):
    return pltpu.VMEM(shape, F32)


def coef_kernel(n, group, lower_ref, upper_ref, vel_ref, out_ref, wide_ref, near_ref, far_ref, gap_ref):
    width = gap_ref.shape[1]
    shape = (8, width)
    lane = lax.broadcasted_iota(jnp.int32, shape, 1)
    gap_ref[...] = jnp.ones_like(gap_ref)
    gap_ref[0:8, 0:n] = jnp.broadcast_to(lower_ref[...].reshape(1, n), (8, n))
    gap_ref[8:16, 0:n] = jnp.broadcast_to(upper_ref[...].reshape(1, n), (8, n))
    lower, upper = gap_ref[0:8, :], gap_ref[8:16, :]
    gap_sum = lower + upper
    kappa = gap_sum * (0.5 / STIFF)
    live = lane < n

    def at(values, place):
        return jnp.sum(jnp.where(lane == place, values, 0.0), axis=1, keepdims=True)

    def sweep(gap, start, backward):
        one, zero = jnp.ones(shape, F32), jnp.zeros(shape, F32)
        m = [jnp.where(live, v, w) for v, w in
             ((1.0 + gap * kappa, one), (gap, zero), (kappa, zero), (one, one))]
        s = 1
        while s < n:
            inside = lane < width - s if backward else lane >= s
            turn = width - s if backward else s
            a, b, c, d = (jnp.where(inside, pltpu.roll(v, turn, 1), w)
                          for v, w in zip(m, (one, zero, zero, one)))
            m = [m[0] * a + m[1] * c, m[0] * b + m[1] * d, m[2] * a + m[3] * c, m[2] * b + m[3] * d]
            s *= 2
        return m[0] * start + m[1]

    first, last = at(lower, 0), at(upper, n - 1)
    phi_next = sweep(upper, first, False)
    psi_next = sweep(lower, last, True)
    phi = jnp.where(lane == 0, first, pltpu.roll(phi_next, 1, 1))
    psi = jnp.where(lane == n - 1, last, pltpu.roll(psi_next, width - 1, 1))
    scale = 1.0 / at(phi_next, n - 1)
    forward, backward = phi * kappa, psi * kappa
    sub = sublanes(shape)
    table = jnp.zeros(shape, F32)
    for row, value in ((INV_GAP, (1.0 / UNIT) / gap_sum), (FORWARD, forward), (BACKWARD, backward),
                       (PSI, psi * scale), (PHI, phi * scale), (OWN, upper / phi_next), (NEXT, phi / phi_next)):
        table = jnp.where(jnp.logical_and(sub == row, live), value, table)
    high = split(table)[0]
    middle, low = split(table - high.astype(F32))
    parts = jnp.concatenate([high, middle, low, jnp.zeros_like(low)], axis=0)
    count = out_ref.shape[0]
    k = lax.broadcasted_iota(jnp.int32, (32, count * 128), 0)
    t = lax.broadcasted_iota(jnp.int32, (32, count * 128), 1) // 128
    pick = jnp.where(jnp.logical_and((k & 7) == t, k < 24), 1.0, 0.0).astype(BF16)
    rows = lax.dot_general(parts, pick, (((0,), (0,)), ((), ())), preferred_element_type=F32)
    for row in range(count):
        out_ref[row] = rows[:n, 128 * row : 128 * row + 128]

    pairs, rows = wide_ref.shape[1], wide_ref.shape[3]
    y = lax.broadcasted_iota(jnp.int32, (pairs * 8, width), 1)
    r = lax.broadcasted_iota(jnp.int32, (pairs * 8, width), 0)
    mine = y // group == (r // 8) * 2 + (r & 7) // 4
    fold = (lax.broadcasted_iota(jnp.int32, (width, rows), 0) % group
            == lax.broadcasted_iota(jnp.int32, (width, rows), 1) // 32)
    fold = jnp.where(fold, 1.0, 0.0).astype(BF16)
    for t, value in enumerate((forward, backward)):
        value = jnp.where(live, value, 0.0)
        hi, lo = split(jnp.where(mine, jnp.broadcast_to(value[0:1], mine.shape), 0.0))
        spread = jnp.dot(hi, fold, preferred_element_type=F32) + jnp.dot(lo, fold, preferred_element_type=F32)
        wide_ref[t] = spread.reshape(pairs, 8, rows)

    even = (lax.axis_index("gy") & 1) == 0
    for c in range(3):
        near_ref[c, 0] = jnp.where(even, vel_ref[c, n - 1], vel_ref[c, 0])
        far_ref[c, 0] = jnp.where(even, vel_ref[c, 0], vel_ref[c, n - 1])


def coefs(lower_gap, upper_gap, vel, group):
    n = lower_gap.shape[0]
    width = -(-n // 128) * 128
    row = jax.ShapeDtypeStruct((3, 1, 32, 128), F32)
    return pl.pallas_call(
        functools.partial(coef_kernel, n, group),
        in_specs=[vmem()] * 3,
        out_specs=[vmem()] * 4,
        out_shape=[held((NEXT + 1, n, 128)), held((2, n // (2 * group), 8, group * 32)), row, row],
        scratch_shapes=[held((16, width))],
        compiler_params=limit(4),
        cost_estimate=cost(1e5),
        name="coefficients",
    )(lower_gap, upper_gap, vel)


def pack_kernel(group, v_hbm, vel, pair_ref, left_ref, right_ref, sems):
    n = vel.shape[1]
    pairs = n // (2 * group)

    cuts = [2, 2, 2, 2, 2, 2] if pairs == 12 else [1] * pairs
    starts = [sum(cuts[:k]) for k in range(len(cuts))]

    def copy(k):
        rows = pl.ds(starts[k] * 2 * group, cuts[k] * 2 * group)
        return pltpu.make_async_copy(v_hbm.at[:, rows], vel.at[:, rows], sems.at[k])

    for k in range(len(cuts)):
        copy(k).start()
    rows = group * 32
    low = sublanes((8, rows)) < 4
    r = lax.broadcasted_iota(jnp.int32, (16, 256), 0)
    lane = lax.broadcasted_iota(jnp.int32, (16, 256), 1) & 127
    inside = jnp.logical_or(r < 4, r >= 12)
    pick = jnp.where(lane == jnp.where(inside, 124, 0) + (r & 3), 1.0, 0.0).astype(BF16)
    for p in range(pairs):
        if p in starts:
            copy(starts.index(p)).wait()
        for c in range(3):
            picked = []
            for h in range(2):
                f = vel[c, pl.ds((2 * p + h) * group, group)].reshape(rows, 128)
                pair = jnp.concatenate(split(f), axis=1)
                pair_ref[c, pl.ds((2 * p + h) * rows, rows), :] = pair
                picked.append(
                    lax.dot_general(pick, pair, (((1,), (1,)), ((), ())), preferred_element_type=F32)
                )
            one, two = picked
            right_ref[c, p] = jnp.where(low, one[:8], two[8:])
            left_ref[c, p] = jnp.where(low, one[8:], two[:8])


def pack(velocity, group):
    n = velocity.shape[1]
    pairs = n // (2 * group)
    packed = jax.ShapeDtypeStruct((3, pairs, 8, group * 32), F32)
    return pl.pallas_call(
        functools.partial(pack_kernel, group),
        in_specs=[pl.BlockSpec(memory_space=pltpu.HBM)],
        out_specs=[vmem()] * 4,
        out_shape=[held(velocity.shape), pltpu.VMEM((3, n * 32, 256), BF16), packed, packed],
        scratch_shapes=[pltpu.SemaphoreType.DMA((pairs,))],
        compiler_params=limit(8),
        cost_estimate=cost(velocity.size, 4 * velocity.size),
        name="pack_edges",
    )(pltpu.with_memory_space_constraint(velocity, pltpu.HBM))


def main_plain(n, block, group, co, vel_ref, pair_ref, old_hbm, dx_ref, dz_ref, adv_ref, sum_ref, b_ref, old_ref, a_ref, w_ref, sems):
    steps = n // block
    rows = group * 32

    def copy(step):
        here = pl.ds(step * block, block)
        return pltpu.make_async_copy(old_hbm.at[:, here], old_ref.at[:, here], sems.at[step])

    for step in range(steps):
        copy(step).start()
    b_ref[...] = jnp.zeros_like(b_ref)

    def part(step, _):
        copy(step).wait()
        for k in range(block // group):
            i0 = step * block + k * group
            vel = [vel_ref[c, pl.ds(i0, group)].reshape(rows, 128) for c in range(3)]
            for c in range(3):
                f = vel[c]
                pair = pair_ref[c, pl.ds(i0 * 32, rows), :]
                along_x = jnp.dot(pair, dx_ref[...], preferred_element_type=F32)
                both = jnp.dot(dz_ref[...], pair, preferred_element_type=F32)
                along_z = both[:, :128] + both[:, 128:]
                below = jnp.where(i0 == 0, 0.0, vel_ref[c, jnp.maximum(i0 - 1, 0)])
                above = jnp.where(i0 == n - group, 0.0, vel_ref[c, jnp.minimum(i0 + group, n - 1)])
                up = jnp.where(jnp.logical_or(i0 == 0, i0 == n // 2), 0.0, a_ref[c])
                down = b_ref[c]
                for y in range(group):
                    here = slice(32 * y, 32 * y + 32)
                    i = i0 + y
                    under = below if y == 0 else f[32 * y - 32 : 32 * y]
                    over = above if y == group - 1 else f[32 * y + 32 : 32 * y + 64]
                    flat = vel[0][here] * along_x[here] + vel[2][here] * along_z[here]
                    adv = flat + vel[1][here] * ((over - under) * co[INV_GAP, pl.ds(i, 1), :])
                    force = f[here] + (-UNIT * GAMMA) * adv + ZETA * old_ref[c, i]
                    up = up + co[FORWARD, pl.ds(i, 1), :] * force
                    down = down + co[BACKWARD, pl.ds(i, 1), :] * force
                    adv_ref[c, i] = adv
                    sum_ref[c, i] = up
                a_ref[c] = up
                b_ref[c] = down
        return 0

    lax.fori_loop(0, steps, part, 0)


def main_kernel(n, block, group, co, vel_ref, pair_ref, old_ref, dx_ref, dz_ref, adv_ref, sum_ref, b_ref,
                a_ref, w_ref):
    pairs = n // (2 * group)
    half = n // 2
    rows = group * 32
    pieces = 4
    high = rows // pieces

    a_ref[...] = jnp.zeros_like(a_ref)
    b_ref[...] = jnp.zeros_like(b_ref)

    def run(*accs):
        def issue(p, c, first=False):
            parts = [pair_ref[c, pl.ds((h * half + p * group) * 32, rows), :] for h in range(2)]
            sides = [jnp.concatenate([part[:, 128 * t : 128 * t + 128] for part in parts], axis=1) for t in range(2)]
            for t in range(2):
                here = slice(t * rows // 2, (t + 1) * rows // 2)
                pltpu.matmul_push_rhs(jnp.concatenate([side[here] for side in sides], axis=0), t, 1)
            for t in range(2):
                for q in range(pieces):
                    fresh = 0 if first and t == 0 and q == 0 else None
                    pltpu.matmul_acc_lhs(accs[c * 8 + q], sides[t][q * high : (q + 1) * high], load_staged_rhs=fresh)
                for q in range(2 * t, 2 * t + 2):
                    here = slice((q % 2) * high, (q % 2 + 1) * high)
                    pltpu.matmul_acc_lhs(accs[c * 8 + 4 + q], dz_ref[here, :], load_staged_rhs=t if q % 2 == 0 else None)

        def scale(p):
            for h in range(2):
                for y in range(group):
                    i = h * half + p * group + y
                    w_ref[h, y] = vel_ref[1, i] * co[INV_GAP, pl.ds(i, 1), :]

        def points(p, c):
            up = [a_ref[h, c] for h in range(2)]
            down = b_ref[c]
            for q in range(pieces):
                along_x = pltpu.matmul_pop(accs[c * 8 + q])
                along_z = pltpu.matmul_pop(accs[c * 8 + 4 + q])
                for h in range(2):
                    lanes = slice(128 * h, 128 * h + 128)
                    for k in range(group // pieces):
                        y = q * (group // pieces) + k
                        i = h * half + p * group + y
                        here = slice(32 * k, 32 * k + 32)
                        under = vel_ref[c, jnp.maximum(i - 1, 0)]
                        over = vel_ref[c, jnp.minimum(i + 1, n - 1)]
                        if h == 0 and y == 0:
                            under = jnp.where(p == 0, 0.0, under)
                        if h == 1 and y == group - 1:
                            over = jnp.where(p == pairs - 1, 0.0, over)
                        adv = vel_ref[0, i] * along_x[here, lanes] + vel_ref[2, i] * along_z[here, lanes]
                        adv = adv + w_ref[h, y] * (over - under)
                        force = vel_ref[c, i] + (-UNIT * GAMMA) * adv + ZETA * old_ref[c, i]
                        up[h] = up[h] + co[FORWARD, pl.ds(i, 1), :] * force
                        down = down + co[BACKWARD, pl.ds(i, 1), :] * force
                        adv_ref[c, i] = adv
                        sum_ref[c, i] = up[h]
            for h in range(2):
                a_ref[h, c] = up[h]
            b_ref[c] = down

        pltpu.matmul_push_rhs(dx_ref[...], 0, 0)
        for c in range(3):
            issue(0, c, c == 0)

        def part(p, _):
            scale(p)
            for c in range(3):
                points(p, c)
                issue(p + 1, c)
            return 0

        lax.fori_loop(0, pairs - 1, part, 0)
        scale(pairs - 1)
        for c in range(3):
            points(pairs - 1, c)

    pl.run_scoped(run, *(pltpu.ACC(unit)((high, 256), F32) for _ in range(3) for unit in range(2) for _ in range(pieces)))


def main_part(vel, pair, old, table, group, block):
    n = vel.shape[1]
    both_units = group == 8
    dx = shift_matrix(128, False)
    dx = np.kron(np.eye(2), dx) if both_units else np.concatenate([dx, dx])
    dz = np.kron(np.eye(group // 2 if both_units else group), shift_matrix(32, True).T)
    dz = jnp.asarray(np.concatenate([dz, dz], axis=1) if both_units else dz, BF16)
    return pl.pallas_call(
        functools.partial(main_kernel if both_units else main_plain, n, block, group),
        in_specs=[vmem(), vmem(), vmem(), vmem() if both_units else pl.BlockSpec(memory_space=pltpu.HBM), vmem(), vmem()],
        out_specs=[vmem()] * 3,
        out_shape=[held(vel.shape), held(vel.shape), held((3, 32, 128))],
        scratch_shapes=[held((2, 3, 32, 128)), held((2, group, 32, 128))] if both_units else [
            held(vel.shape), held((3, 32, 128)), held((2, group, 32, 128)), pltpu.SemaphoreType.DMA((n // group,))],
        compiler_params=limit(6),
        cost_estimate=cost(25 * old.size, 4 * old.size),
        name="inner_part",
    )(table, vel, pair, old if both_units else pltpu.with_memory_space_constraint(old, pltpu.HBM), jnp.asarray(dx, BF16), dz)


def place_matrix():
    r = lax.broadcasted_iota(jnp.int32, (16, 128), 0) & 7
    lane = lax.broadcasted_iota(jnp.int32, (16, 128), 1)
    return jnp.where(lane == jnp.where(r < 4, r, r + 120), 1.0, 0.0).astype(BF16)


def spread_planes(value):
    return lax.dot_general(value, place_matrix(), (((0,), (0,)), ((), ())), preferred_element_type=F32)


def edge_kernel(pairs, group, co, from_left, from_right, left_ref, right_ref, sum_ref, b_ref, wide_ref,
                near_ref, far_ref, vel_ref, extra_ref, rim_ref, load_ref):
    even = (lax.axis_index("gy") & 1) == 0
    n = 2 * pairs * group
    rows = group * 32
    shape = (pairs, 8, rows)
    sub = sublanes((1, 8, rows))
    low = sub[0] < 4
    quarter = sub & 3

    def swap(x):
        return pltpu.roll(x, 4, 0)

    def total(x):
        t = x[0]
        for p in range(1, pairs):
            t = t + x[p]
        t = t + swap(t)
        parts = t[:, 0:32]
        for y in range(1, group):
            parts = parts + t[:, 32 * y : 32 * y + 32]
        return parts

    for c in range(3):
        below = jnp.where(even, far_ref[c, 0], near_ref[c, 0])
        above = jnp.where(even, near_ref[c, 0], far_ref[c, 0])
        rims = (vel_ref[1, 0] * below * (UNIT * co[INV_GAP, pl.ds(0, 1), :]),
                -vel_ref[1, n - 1] * above * (UNIT * co[INV_GAP, pl.ds(n - 1, 1), :]))
        rim_ref[0, c], rim_ref[1, c] = rims
        adv, totals = [], []
        for side, halo, own in ((0, from_left, left_ref), (1, from_right, right_ref)):
            h = halo[c]
            slope = jnp.zeros(shape, F32)
            for d in range(4):
                w = WEIGHTS[3 - d] * UNIT
                if side == 0:
                    weight = jnp.where(quarter + d < 4, -w, 0.0)
                    turned = pltpu.roll(h, 8 - d, 1) if d else h
                else:
                    weight = jnp.where(quarter >= d, w, 0.0)
                    turned = pltpu.roll(h, d, 1) if d else h
                slope = slope + weight * turned
            adv.append(-own[0] * slope)
            force = GAMMA * adv[side]
            totals.append([total(wide_ref[t] * force) for t in range(2)])
        for p in range(pairs):
            l, r = adv[0][p], adv[1][p]
            for h, value in ((0, jnp.where(low, l, swap(r))), (1, jnp.where(low, swap(l), r))):
                extra_ref[c, 2 * p + h] = jnp.concatenate(split(value), axis=0)
        for t, (main, weight, row, i) in enumerate(
            ((b_ref[c], BACKWARD, PHI, 0), (sum_ref[c, n // 2 - 1] + sum_ref[c, n - 1], FORWARD, PSI, n - 1))
        ):
            main = main + (GAMMA * co[weight, pl.ds(0, 1), :]) * rims[0] + (GAMMA * co[weight, pl.ds(n - 1, 1), :]) * rims[1]
            value = jnp.where(low[:, :32], totals[0][1 - t], totals[1][1 - t])
            spread = spread_planes(jnp.concatenate(split(value), axis=0))
            load_ref[pl.ds(t * 96 + c * 32, 32), :] = (main + spread) * co[row, pl.ds(i, 1), :]
    row = sublanes((8, 128))
    ends = jnp.where(row == 0, co[PSI, pl.ds(0, 1), :], co[PSI, pl.ds(n - 1, 1), :])
    ends = jnp.where(row == 2, co[PHI, pl.ds(0, 1), :], ends)
    load_ref[192:200, :] = jnp.where(row == 3, co[PHI, pl.ds(n - 1, 1), :], ends)


def edge_part(from_left, from_right, left, right, sums, b_sum, wide, near, far, vel, table, group):
    pairs = left.shape[1]
    return pl.pallas_call(
        functools.partial(edge_kernel, pairs, group),
        in_specs=[vmem()] + [vmem()] * 10,
        out_specs=[vmem()] * 3,
        out_shape=[pltpu.VMEM((3, 2 * pairs, 16, group * 32), BF16), held((2, 3, 32, 128)),
                   jax.ShapeDtypeStruct((200, 128), F32)],
        compiler_params=limit(8),
        cost_estimate=cost(40 * left.size),
        name="edge_part",
    )(table, from_left, from_right, left, right, sums, b_sum, wide, near, far, vel)


def read(ref):
    return (ref[0:96, :], ref[96:192, :]) + tuple(ref[192 + t : 193 + t, :] for t in range(4))


def write(ref, run):
    ref[0:96, :] = run[0]
    ref[96:192, :] = run[1]
    for t in range(4):
        ref[192 + t : 193 + t, :] = run[2 + t]
    ref[196:200, :] = jnp.zeros((4, 128), F32)


def join(lower, upper):
    f1, l1, pf1, pl1, qf1, ql1 = lower
    f2, l2, pf2, pl2, qf2, ql2 = upper
    inverse = 1.0 / (1.0 - pf2 * ql1)
    over, under = qf1 * inverse, pl2 * inverse
    return (
        f1 + over * (f2 + pf2 * l1),
        l2 + under * (l1 + ql1 * f2),
        pf1 + over * pf2 * pl1,
        under * pl1,
        over * qf2,
        ql2 + under * ql1 * qf2,
    )


def empty():
    zero, one, none = (jnp.zeros((1, 128), F32), jnp.ones((1, 128), F32), jnp.zeros((96, 128), F32))
    return (none, none, zero, one, one, zero)


def join_kernel(bit, opening, closing, token, all_ref, other_ref, *refs):
    me = lax.axis_index("gy")
    if opening:
        lower_in = upper_in = None
        all_out, lower_out, upper_out = refs[:3]
    else:
        lower_in, upper_in, all_out, lower_out, upper_out = refs[:5]
    lower = empty() if opening else read(lower_in)
    upper = empty() if opening else read(upper_in)
    whole, other = read(all_ref), read(other_ref)

    def send(run):
        if closing:
            above_me = (me & (2 * bit)) != 0
            all_out[0:96, :] = jnp.where(above_me, run[0], run[1])
            all_out[96:104, :] = jnp.broadcast_to(jnp.where(above_me, run[2], run[5]), (8, 128))
        else:
            write(all_out, run)

    @pl.when((me & bit) != 0)
    def _():
        send(join(other, whole))
        write(lower_out, join(other, lower))
        write(upper_out, upper)

    @pl.when((me & bit) == 0)
    def _():
        send(join(whole, other))
        write(lower_out, lower)
        write(upper_out, join(upper, other))


def join_runs(bit, closing, token, whole, other, around):
    run = jax.ShapeDtypeStruct((200, 128), F32)
    half = jax.ShapeDtypeStruct((104, 128), F32)
    return pl.pallas_call(
        functools.partial(join_kernel, bit, not around, closing),
        in_specs=[pl.BlockSpec(memory_space=pl.ANY)] + [vmem()] * (2 + len(around)),
        out_specs=[vmem()] * 3,
        out_shape=[half if closing else run, run, run],
        compiler_params=limit(8),
        cost_estimate=cost(20 * whole.size),
        name="join_runs",
    )(token, whole, other, *around)


def couple(bit, me, load, other_ref, lower_ref, upper_ref, below_ref, above_ref):
    lower, upper = read(lower_ref), read(upper_ref)
    vector, scalar = other_ref[0:96, :], other_ref[96:97, :]
    none, zero = jnp.zeros((96, 128), F32), jnp.zeros((1, 128), F32)

    def solve(lower, upper):
        _, a, _, _, _, r = lower
        b, _, q, _, _, _ = upper
        first, last, psi_f, psi_l, phi_f, phi_l = read(load)
        share = 1.0 / (1.0 - psi_f * r)
        a_next = last + psi_l * a + psi_l * r * share * (first + psi_f * a)
        r_next = phi_l + psi_l * r * share * phi_f
        above = (b + q * a_next) / (1.0 - q * r_next)
        above_ref[...] = above
        below_ref[...] = a + r * share * (first + psi_f * a + phi_f * above)

    @pl.when((me & bit) != 0)
    def _():
        solve(join((none, vector, zero, zero, zero, scalar), lower), upper)

    @pl.when((me & bit) == 0)
    def _():
        solve(lower, join(upper, (vector, none, scalar, zero, zero, zero)))


def up_kernel(start, count, block, group, token, co, adv_part, sum_part, extra_ref, rim_ref, *refs):
    n = adv_part.shape[1]
    if start:
        _, before_ref, adv_hbm, sum_ref, end_ref, adv_ref, sems = refs
        end_ref[...] = before_ref[...]
    else:
        adv_hbm, sum_ref, end_ref, adv_ref, sems = refs
        end_ref[...] = (GAMMA * co[FORWARD, pl.ds(0, 1), :]) * rim_ref[0]
    steps = count // block

    def copy(step):
        here = pl.ds(step * block, block)
        there = pl.ds(start + step * block, block)
        return pltpu.make_async_copy(adv_ref.at[:, here], adv_hbm.at[:, there], sems.at[step])

    def part(step, _):
        for c in range(3):
            acc = end_ref[c]
            for k in range(block // group):
                here = step * block + k * group
                chunk = start // group + step * (block // group) + k
                acc = jnp.where(chunk == n // (2 * group), acc + sum_part[c, n // 2 - 1], acc)
                spread = spread_planes(extra_ref[c, chunk])
                for y in range(group):
                    i = here + y
                    extra = spread[32 * y : 32 * y + 32]
                    adv_ref[c, i] = adv_part[c, start + i] * (-UNIT) + extra
                    acc = acc + (GAMMA * co[FORWARD, pl.ds(start + i, 1), :]) * extra
                    sum_ref[c, i] = sum_part[c, start + i] + acc
            end_ref[c] = acc

        if start == 0:
            @pl.when(step == 0)
            def _():
                adv_ref[:, 0] = adv_ref[:, 0] + rim_ref[0]

        if start + count == n:
            @pl.when(step == steps - 1)
            def _():
                adv_ref[:, count - 1] = adv_ref[:, count - 1] + rim_ref[1]
                sum_ref[:, count - 1] = sum_ref[:, count - 1] + (GAMMA * co[FORWARD, pl.ds(n - 1, 1), :]) * rim_ref[1]

        copy(step).start()
        return 0

    lax.fori_loop(0, steps, part, 0, unroll=True)

    def finish(step, _):
        copy(step).wait()
        return 0

    lax.fori_loop(0, steps, finish, 0, unroll=True)


def sweep_up(start, count, token, table, adv_part, sums, extra, rims, group, before=()):
    shape = adv_part.shape
    block = max(d for d in range(group, 17, group) if count % d == 0)
    hbm = pl.BlockSpec(memory_space=pltpu.HBM)
    part = (3, count, 32, 128)
    return pl.pallas_call(
        functools.partial(up_kernel, start, count, block, group),
        in_specs=[pl.BlockSpec(memory_space=pl.ANY), vmem()] + [vmem()] * 4 + ([hbm, vmem()] if before else []),
        out_specs=[hbm, vmem(), vmem()],
        out_shape=[jax.ShapeDtypeStruct(shape, F32), held(part), held((3, 32, 128))],
        scratch_shapes=[held(part), pltpu.SemaphoreType.DMA((count // block,))],
        input_output_aliases={6: 0} if before else {},
        compiler_params=limit(8),
        cost_estimate=cost(4 * adv_part.size, 2 * adv_part.size),
        name="sweep_up",
    )(token, table, adv_part, sums, extra, rims, *before)


def down_kernel(bit, n, block, co, load, other, lower, upper, low_ref, high_ref, u_hbm, u_ref, below_ref, above_ref,
                sems):
    steps = n // block
    couple(bit, lax.axis_index("gy"), load, other, lower, upper, below_ref, above_ref)
    below = below_ref[...].reshape(3, 32, 128)

    def copy(step):
        here = pl.ds(step * block, block)
        return pltpu.make_async_copy(u_ref.at[:, here], u_hbm.at[:, here], sems.at[step])

    def part(sum_ref, first):
        count = sum_ref.shape[1] // block

        def run(k, value):
            step = count - 1 - k
            for y in reversed(range(block)):
                i = step * block + y
                value = co[OWN, pl.ds(first + i, 1), :] * (sum_ref[:, i] + below) + co[NEXT, pl.ds(first + i, 1), :] * value
                u_ref[:, first + i] = value
            copy(first // block + step).start()
            return value

        return run

    value = above_ref[...].reshape(3, 32, 128)
    cut = low_ref.shape[1]
    value = lax.fori_loop(0, (n - cut) // block, part(high_ref, cut), value)
    lax.fori_loop(0, cut // block, part(low_ref, 0), value)

    def finish(step, _):
        copy(step).wait()
        return 0

    lax.fori_loop(0, steps, finish, 0)


def sweep_down(bit, table, load, other, around, sums, block):
    n = sums[0].shape[1] + sums[1].shape[1]
    shape = (3, n, 32, 128)
    return pl.pallas_call(
        functools.partial(down_kernel, bit, n, block),
        in_specs=[vmem()] + [vmem()] * 6,
        out_specs=pl.BlockSpec(memory_space=pltpu.HBM),
        out_shape=jax.ShapeDtypeStruct(shape, F32),
        scratch_shapes=[held(shape), held((96, 128)), held((96, 128)), pltpu.SemaphoreType.DMA((n // block,))],
        compiler_params=limit(12),
        cost_estimate=cost(12 * sums[0].size, 8 * sums[0].size),
        name="sweep_down",
    )(table, load, other, *around, *sums)


def shards(velocity, old_advection, lower_gap, upper_gap):
    n = velocity.shape[1]
    group = max(d for d in range(1, 9) if n % (2 * d) == 0)
    block = 2 * group
    nx, ny = lax.axis_size("gx"), lax.axis_size("gy")
    ring = [(i, (i + 1) % nx) for i in range(nx)]
    pairs = [(i, i ^ 1) for i in range(ny)]
    others = [(i, j) for k in range(1, ny - 1, 2) for i, j in ((k, k + 1), (k + 1, k))]

    vel, pair, left, right = pack(velocity, group)
    from_left = lax.ppermute(right, "gx", ring)
    from_right = lax.ppermute(left, "gx", [(j, i) for i, j in ring])
    table, wide, near, far = coefs(lower_gap, upper_gap, vel, group)
    near = lax.ppermute(near, "gy", pairs)
    far = lax.ppermute(far, "gy", others)
    adv_part, sums, b_sum = main_part(vel, pair, old_advection, table, group, block)
    extra, rims, load = edge_part(
        from_left, from_right, left, right, sums, b_sum, wide, near, far, vel, table, group
    )
    bits = [1 << t for t in range(ny.bit_length() - 1)]
    cut = group * (CUT * (n // group) // 24)
    whole, around, token = load, [], load
    for bit in bits:
        other = lax.ppermute(whole, "gy", [(i, i ^ bit) for i in range(ny)])
        if bit != bits[-1]:
            whole, *around = join_runs(bit, 2 * bit == bits[-1], token, whole, other, around)
        if bit == bits[0]:
            adv, low, end = sweep_up(0, cut, whole, table, adv_part, sums, extra, rims, group)
            token = end
    adv, high, _ = sweep_up(cut, n - cut, whole, table, adv_part, sums, extra, rims, group, (adv, end))
    down_block = max(d for d in range(group, 17, group) if cut % d == 0 and n % d == 0)
    return sweep_down(bits[-1], table, load, other, around, (low, high), down_block), adv


def solution(mesh):
    spec = P(None, "gy", None, "gx")
    return jax.shard_map(
        shards,
        mesh=mesh,
        in_specs=(spec, spec, P("gy"), P("gy")),
        out_specs=(spec, spec),
        check_vma=False,
    )
```

```python
import functools

import jax
import jax.numpy as jnp
import numpy as np
from jax import lax
from jax.experimental import pallas as pl
from jax.experimental.pallas import tpu as pltpu
from jax.sharding import PartitionSpec as P

STIFF = 1024
GAMMA = 5.0 / 12.0
ZETA = -17.0 / 60.0
WEIGHTS = (672.0, -168.0, 32.0, -3.0)
UNIT = 1.0 / 840.0
F32 = jnp.float32
BF16 = jnp.bfloat16
MIB = 1 << 20
CUT = 16

INV_GAP, FORWARD, BACKWARD, PSI, PHI, OWN, NEXT = range(7)


def shift_matrix(size, periodic):
    m = np.zeros((size, size), np.float32)
    for j in range(size):
        for k, w in enumerate(WEIGHTS, 1):
            for i, s in ((j + k, w), (j - k, -w)):
                if periodic:
                    m[i % size, j] += s
                elif 0 <= i < size:
                    m[i, j] += s
    return m


def split(values):
    hi = values.astype(BF16)
    return hi, (values - hi.astype(F32)).astype(BF16)


def sublanes(shape):
    return lax.broadcasted_iota(jnp.int32, shape, len(shape) - 2)


def vmem():
    return pl.BlockSpec(memory_space=pltpu.VMEM)


def limit(mib):
    return pltpu.CompilerParams(vmem_limit_bytes=mib * MIB)


def cost(flops, moved=0):
    return pl.CostEstimate(flops=int(flops), bytes_accessed=int(moved), transcendentals=0)


def held(shape):
    return pltpu.VMEM(shape, F32)


def coef_kernel(n, group, lower_ref, upper_ref, vel_ref, out_ref, wide_ref, near_ref, far_ref, gap_ref):
    width = gap_ref.shape[1]
    shape = (8, width)
    lane = lax.broadcasted_iota(jnp.int32, shape, 1)
    gap_ref[...] = jnp.ones_like(gap_ref)
    gap_ref[0:8, 0:n] = jnp.broadcast_to(lower_ref[...].reshape(1, n), (8, n))
    gap_ref[8:16, 0:n] = jnp.broadcast_to(upper_ref[...].reshape(1, n), (8, n))
    lower, upper = gap_ref[0:8, :], gap_ref[8:16, :]
    gap_sum = lower + upper
    kappa = gap_sum * (0.5 / STIFF)
    live = lane < n

    def at(values, place):
        return jnp.sum(jnp.where(lane == place, values, 0.0), axis=1, keepdims=True)

    def sweep(gap, start, backward):
        one, zero = jnp.ones(shape, F32), jnp.zeros(shape, F32)
        m = [jnp.where(live, v, w) for v, w in
             ((1.0 + gap * kappa, one), (gap, zero), (kappa, zero), (one, one))]
        s = 1
        while s < n:
            inside = lane < width - s if backward else lane >= s
            turn = width - s if backward else s
            a, b, c, d = (jnp.where(inside, pltpu.roll(v, turn, 1), w)
                          for v, w in zip(m, (one, zero, zero, one)))
            m = [m[0] * a + m[1] * c, m[0] * b + m[1] * d, m[2] * a + m[3] * c, m[2] * b + m[3] * d]
            s *= 2
        return m[0] * start + m[1]

    first, last = at(lower, 0), at(upper, n - 1)
    phi_next = sweep(upper, first, False)
    psi_next = sweep(lower, last, True)
    phi = jnp.where(lane == 0, first, pltpu.roll(phi_next, 1, 1))
    psi = jnp.where(lane == n - 1, last, pltpu.roll(psi_next, width - 1, 1))
    scale = 1.0 / at(phi_next, n - 1)
    forward, backward = phi * kappa, psi * kappa
    sub = sublanes(shape)
    table = jnp.zeros(shape, F32)
    for row, value in ((INV_GAP, (1.0 / UNIT) / gap_sum), (FORWARD, forward), (BACKWARD, backward),
                       (PSI, psi * scale), (PHI, phi * scale), (OWN, upper / phi_next), (NEXT, phi / phi_next)):
        table = jnp.where(jnp.logical_and(sub == row, live), value, table)
    high = split(table)[0]
    middle, low = split(table - high.astype(F32))
    parts = jnp.concatenate([high, middle, low, jnp.zeros_like(low)], axis=0)
    count = out_ref.shape[0]
    k = lax.broadcasted_iota(jnp.int32, (32, count * 128), 0)
    t = lax.broadcasted_iota(jnp.int32, (32, count * 128), 1) // 128
    pick = jnp.where(jnp.logical_and((k & 7) == t, k < 24), 1.0, 0.0).astype(BF16)
    rows = lax.dot_general(parts, pick, (((0,), (0,)), ((), ())), preferred_element_type=F32)
    for row in range(count):
        out_ref[row] = rows[:n, 128 * row : 128 * row + 128]

    pairs, rows = wide_ref.shape[1], wide_ref.shape[3]
    y = lax.broadcasted_iota(jnp.int32, (pairs * 8, width), 1)
    r = lax.broadcasted_iota(jnp.int32, (pairs * 8, width), 0)
    mine = y // group == (r // 8) * 2 + (r & 7) // 4
    fold = (lax.broadcasted_iota(jnp.int32, (width, rows), 0) % group
            == lax.broadcasted_iota(jnp.int32, (width, rows), 1) // 32)
    fold = jnp.where(fold, 1.0, 0.0).astype(BF16)
    for t, value in enumerate((forward, backward)):
        value = jnp.where(live, value, 0.0)
        hi, lo = split(jnp.where(mine, jnp.broadcast_to(value[0:1], mine.shape), 0.0))
        spread = jnp.dot(hi, fold, preferred_element_type=F32) + jnp.dot(lo, fold, preferred_element_type=F32)
        wide_ref[t] = spread.reshape(pairs, 8, rows)

    even = (lax.axis_index("gy") & 1) == 0
    for c in range(3):
        near_ref[c, 0] = jnp.where(even, vel_ref[c, n - 1], vel_ref[c, 0])
        far_ref[c, 0] = jnp.where(even, vel_ref[c, 0], vel_ref[c, n - 1])


def coefs(lower_gap, upper_gap, vel, group):
    n = lower_gap.shape[0]
    width = -(-n // 128) * 128
    row = jax.ShapeDtypeStruct((3, 1, 32, 128), F32)
    return pl.pallas_call(
        functools.partial(coef_kernel, n, group),
        in_specs=[vmem()] * 3,
        out_specs=[vmem()] * 4,
        out_shape=[held((NEXT + 1, n, 128)), held((2, n // (2 * group), 8, group * 32)), row, row],
        scratch_shapes=[held((16, width))],
        compiler_params=limit(4),
        cost_estimate=cost(1e5),
        name="coefficients",
    )(lower_gap, upper_gap, vel)


def pack_kernel(group, v_hbm, vel, pair_ref, left_ref, right_ref, sems):
    n = vel.shape[1]
    pairs = n // (2 * group)

    cuts = [2, 2, 2, 2, 2, 2] if pairs == 12 else [1] * pairs
    starts = [sum(cuts[:k]) for k in range(len(cuts))]

    def copy(k):
        rows = pl.ds(starts[k] * 2 * group, cuts[k] * 2 * group)
        return pltpu.make_async_copy(v_hbm.at[:, rows], vel.at[:, rows], sems.at[k])

    for k in range(len(cuts)):
        copy(k).start()
    rows = group * 32
    low = sublanes((8, rows)) < 4
    r = lax.broadcasted_iota(jnp.int32, (16, 256), 0)
    lane = lax.broadcasted_iota(jnp.int32, (16, 256), 1) & 127
    inside = jnp.logical_or(r < 4, r >= 12)
    pick = jnp.where(lane == jnp.where(inside, 124, 0) + (r & 3), 1.0, 0.0).astype(BF16)
    for p in range(pairs):
        if p in starts:
            copy(starts.index(p)).wait()
        for c in range(3):
            picked = []
            for h in range(2):
                f = vel[c, pl.ds((2 * p + h) * group, group)].reshape(rows, 128)
                pair = jnp.concatenate(split(f), axis=1)
                pair_ref[c, pl.ds((2 * p + h) * rows, rows), :] = pair
                picked.append(
                    lax.dot_general(pick, pair, (((1,), (1,)), ((), ())), preferred_element_type=F32)
                )
            one, two = picked
            right_ref[c, p] = jnp.where(low, one[:8], two[8:])
            left_ref[c, p] = jnp.where(low, one[8:], two[:8])


def pack(velocity, group):
    n = velocity.shape[1]
    pairs = n // (2 * group)
    packed = jax.ShapeDtypeStruct((3, pairs, 8, group * 32), F32)
    return pl.pallas_call(
        functools.partial(pack_kernel, group),
        in_specs=[pl.BlockSpec(memory_space=pltpu.HBM)],
        out_specs=[vmem()] * 4,
        out_shape=[held(velocity.shape), pltpu.VMEM((3, n * 32, 256), BF16), packed, packed],
        scratch_shapes=[pltpu.SemaphoreType.DMA((pairs,))],
        compiler_params=limit(8),
        cost_estimate=cost(velocity.size, 4 * velocity.size),
        name="pack_edges",
    )(pltpu.with_memory_space_constraint(velocity, pltpu.HBM))


def main_plain(n, block, group, co, vel_ref, pair_ref, old_hbm, dx_ref, dz_ref, adv_ref, sum_ref, b_ref, old_ref, a_ref, w_ref, sems):
    steps = n // block
    rows = group * 32

    def copy(step):
        here = pl.ds(step * block, block)
        return pltpu.make_async_copy(old_hbm.at[:, here], old_ref.at[:, here], sems.at[step])

    for step in range(steps):
        copy(step).start()
    b_ref[...] = jnp.zeros_like(b_ref)

    def part(step, _):
        copy(step).wait()
        for k in range(block // group):
            i0 = step * block + k * group
            vel = [vel_ref[c, pl.ds(i0, group)].reshape(rows, 128) for c in range(3)]
            for c in range(3):
                f = vel[c]
                pair = pair_ref[c, pl.ds(i0 * 32, rows), :]
                along_x = jnp.dot(pair, dx_ref[...], preferred_element_type=F32)
                both = jnp.dot(dz_ref[...], pair, preferred_element_type=F32)
                along_z = both[:, :128] + both[:, 128:]
                below = jnp.where(i0 == 0, 0.0, vel_ref[c, jnp.maximum(i0 - 1, 0)])
                above = jnp.where(i0 == n - group, 0.0, vel_ref[c, jnp.minimum(i0 + group, n - 1)])
                up = jnp.where(jnp.logical_or(i0 == 0, i0 == n // 2), 0.0, a_ref[c])
                down = b_ref[c]
                for y in range(group):
                    here = slice(32 * y, 32 * y + 32)
                    i = i0 + y
                    under = below if y == 0 else f[32 * y - 32 : 32 * y]
                    over = above if y == group - 1 else f[32 * y + 32 : 32 * y + 64]
                    flat = vel[0][here] * along_x[here] + vel[2][here] * along_z[here]
                    adv = flat + vel[1][here] * ((over - under) * co[INV_GAP, pl.ds(i, 1), :])
                    force = f[here] + (-UNIT * GAMMA) * adv + ZETA * old_ref[c, i]
                    up = up + co[FORWARD, pl.ds(i, 1), :] * force
                    down = down + co[BACKWARD, pl.ds(i, 1), :] * force
                    adv_ref[c, i] = adv
                    sum_ref[c, i] = up
                a_ref[c] = up
                b_ref[c] = down
        return 0

    lax.fori_loop(0, steps, part, 0)


def main_kernel(n, block, group, co, vel_ref, pair_ref, old_ref, dx_ref, dz_ref, adv_ref, sum_ref, b_ref,
                a_ref, w_ref):
    pairs = n // (2 * group)
    half = n // 2
    rows = group * 32
    pieces = 4
    high = rows // pieces

    a_ref[...] = jnp.zeros_like(a_ref)
    b_ref[...] = jnp.zeros_like(b_ref)

    def run(*accs):
        def issue(p, c, first=False):
            parts = [pair_ref[c, pl.ds((h * half + p * group) * 32, rows), :] for h in range(2)]
            sides = [jnp.concatenate([part[:, 128 * t : 128 * t + 128] for part in parts], axis=1) for t in range(2)]
            for t in range(2):
                here = slice(t * rows // 2, (t + 1) * rows // 2)
                pltpu.matmul_push_rhs(jnp.concatenate([side[here] for side in sides], axis=0), t, 1)
            for t in range(2):
                for q in range(pieces):
                    fresh = 0 if first and t == 0 and q == 0 else None
                    pltpu.matmul_acc_lhs(accs[c * 8 + q], sides[t][q * high : (q + 1) * high], load_staged_rhs=fresh)
                for q in range(2 * t, 2 * t + 2):
                    here = slice((q % 2) * high, (q % 2 + 1) * high)
                    pltpu.matmul_acc_lhs(accs[c * 8 + 4 + q], dz_ref[here, :], load_staged_rhs=t if q % 2 == 0 else None)

        def scale(p):
            for h in range(2):
                for y in range(group):
                    i = h * half + p * group + y
                    w_ref[h, y] = vel_ref[1, i] * co[INV_GAP, pl.ds(i, 1), :]

        def points(p, c):
            up = [a_ref[h, c] for h in range(2)]
            down = b_ref[c]
            for q in range(pieces):
                along_x = pltpu.matmul_pop(accs[c * 8 + q])
                along_z = pltpu.matmul_pop(accs[c * 8 + 4 + q])
                for h in range(2):
                    lanes = slice(128 * h, 128 * h + 128)
                    for k in range(group // pieces):
                        y = q * (group // pieces) + k
                        i = h * half + p * group + y
                        here = slice(32 * k, 32 * k + 32)
                        under = vel_ref[c, jnp.maximum(i - 1, 0)]
                        over = vel_ref[c, jnp.minimum(i + 1, n - 1)]
                        if h == 0 and y == 0:
                            under = jnp.where(p == 0, 0.0, under)
                        if h == 1 and y == group - 1:
                            over = jnp.where(p == pairs - 1, 0.0, over)
                        adv = vel_ref[0, i] * along_x[here, lanes] + vel_ref[2, i] * along_z[here, lanes]
                        adv = adv + w_ref[h, y] * (over - under)
                        force = vel_ref[c, i] + (-UNIT * GAMMA) * adv + ZETA * old_ref[c, i]
                        up[h] = up[h] + co[FORWARD, pl.ds(i, 1), :] * force
                        down = down + co[BACKWARD, pl.ds(i, 1), :] * force
                        adv_ref[c, i] = adv
                        sum_ref[c, i] = up[h]
            for h in range(2):
                a_ref[h, c] = up[h]
            b_ref[c] = down

        pltpu.matmul_push_rhs(dx_ref[...], 0, 0)
        for c in range(3):
            issue(0, c, c == 0)

        def part(p, _):
            scale(p)
            for c in range(3):
                points(p, c)
                issue(p + 1, c)
            return 0

        lax.fori_loop(0, pairs - 1, part, 0)
        scale(pairs - 1)
        for c in range(3):
            points(pairs - 1, c)

    pl.run_scoped(run, *(pltpu.ACC(unit)((high, 256), F32) for _ in range(3) for unit in range(2) for _ in range(pieces)))


def main_part(vel, pair, old, table, group, block):
    n = vel.shape[1]
    both_units = group == 8
    dx = shift_matrix(128, False)
    dx = np.kron(np.eye(2), dx) if both_units else np.concatenate([dx, dx])
    dz = np.kron(np.eye(group // 2 if both_units else group), shift_matrix(32, True).T)
    dz = jnp.asarray(np.concatenate([dz, dz], axis=1) if both_units else dz, BF16)
    return pl.pallas_call(
        functools.partial(main_kernel if both_units else main_plain, n, block, group),
        in_specs=[vmem(), vmem(), vmem(), vmem() if both_units else pl.BlockSpec(memory_space=pltpu.HBM), vmem(), vmem()],
        out_specs=[vmem()] * 3,
        out_shape=[held(vel.shape), held(vel.shape), held((3, 32, 128))],
        scratch_shapes=[held((2, 3, 32, 128)), held((2, group, 32, 128))] if both_units else [
            held(vel.shape), held((3, 32, 128)), held((2, group, 32, 128)), pltpu.SemaphoreType.DMA((n // group,))],
        compiler_params=limit(6),
        cost_estimate=cost(25 * old.size, 4 * old.size),
        name="inner_part",
    )(table, vel, pair, old if both_units else pltpu.with_memory_space_constraint(old, pltpu.HBM), jnp.asarray(dx, BF16), dz)


def place_matrix():
    r = lax.broadcasted_iota(jnp.int32, (16, 128), 0) & 7
    lane = lax.broadcasted_iota(jnp.int32, (16, 128), 1)
    return jnp.where(lane == jnp.where(r < 4, r, r + 120), 1.0, 0.0).astype(BF16)


def spread_planes(value):
    return lax.dot_general(value, place_matrix(), (((0,), (0,)), ((), ())), preferred_element_type=F32)


def edge_kernel(pairs, group, co, from_left, from_right, left_ref, right_ref, sum_ref, b_ref, wide_ref,
                near_ref, far_ref, vel_ref, adv_l, adv_r, rim_ref, load_ref):
    even = (lax.axis_index("gy") & 1) == 0
    n = 2 * pairs * group
    rows = group * 32
    shape = (pairs, 8, rows)
    sub = sublanes((1, 8, rows))
    low = sub[0] < 4
    quarter = sub & 3

    def swap(x):
        return pltpu.roll(x, 4, 0)

    def total(x):
        t = x[0]
        for p in range(1, pairs):
            t = t + x[p]
        t = t + swap(t)
        parts = t[:, 0:32]
        for y in range(1, group):
            parts = parts + t[:, 32 * y : 32 * y + 32]
        return parts

    for c in range(3):
        below = jnp.where(even, far_ref[c, 0], near_ref[c, 0])
        above = jnp.where(even, near_ref[c, 0], far_ref[c, 0])
        rims = (vel_ref[1, 0] * below * (UNIT * co[INV_GAP, pl.ds(0, 1), :]),
                -vel_ref[1, n - 1] * above * (UNIT * co[INV_GAP, pl.ds(n - 1, 1), :]))
        rim_ref[0, c], rim_ref[1, c] = rims
        adv, totals = [], []
        for side, halo, own in ((0, from_left, left_ref), (1, from_right, right_ref)):
            h = halo[c]
            slope = jnp.zeros(shape, F32)
            for d in range(4):
                w = WEIGHTS[3 - d] * UNIT
                if side == 0:
                    weight = jnp.where(quarter + d < 4, -w, 0.0)
                    turned = pltpu.roll(h, 8 - d, 1) if d else h
                else:
                    weight = jnp.where(quarter >= d, w, 0.0)
                    turned = pltpu.roll(h, d, 1) if d else h
                slope = slope + weight * turned
            adv.append(-own[0] * slope)
            force = GAMMA * adv[side]
            totals.append([total(wide_ref[t] * force) for t in range(2)])
        adv_l[c], adv_r[c] = adv
        for t, (main, weight, row, i) in enumerate(
            ((b_ref[c], BACKWARD, PHI, 0), (sum_ref[c, n // 2 - 1] + sum_ref[c, n - 1], FORWARD, PSI, n - 1))
        ):
            main = main + (GAMMA * co[weight, pl.ds(0, 1), :]) * rims[0] + (GAMMA * co[weight, pl.ds(n - 1, 1), :]) * rims[1]
            value = jnp.where(low[:, :32], totals[0][1 - t], totals[1][1 - t])
            spread = spread_planes(jnp.concatenate(split(value), axis=0))
            load_ref[pl.ds(t * 96 + c * 32, 32), :] = (main + spread) * co[row, pl.ds(i, 1), :]
    row = sublanes((8, 128))
    ends = jnp.where(row == 0, co[PSI, pl.ds(0, 1), :], co[PSI, pl.ds(n - 1, 1), :])
    ends = jnp.where(row == 2, co[PHI, pl.ds(0, 1), :], ends)
    load_ref[192:200, :] = jnp.where(row == 3, co[PHI, pl.ds(n - 1, 1), :], ends)


def edge_part(from_left, from_right, left, right, sums, b_sum, wide, near, far, vel, table, group):
    pairs = left.shape[1]
    return pl.pallas_call(
        functools.partial(edge_kernel, pairs, group),
        in_specs=[vmem()] + [vmem()] * 10,
        out_specs=[vmem()] * 4,
        out_shape=[held(left.shape), held(left.shape), held((2, 3, 32, 128)),
                   jax.ShapeDtypeStruct((200, 128), F32)],
        compiler_params=limit(8),
        cost_estimate=cost(40 * left.size),
        name="edge_part",
    )(table, from_left, from_right, left, right, sums, b_sum, wide, near, far, vel)


def extra_kernel(pairs, adv_l, adv_r, extra_ref):
    low = sublanes(adv_l.shape[2:]) < 4
    for c in range(3):
        for p in range(pairs):
            l, r = adv_l[c, p], adv_r[c, p]
            first = jnp.where(low, l, pltpu.roll(r, 4, 0))
            second = jnp.where(low, pltpu.roll(l, 4, 0), r)
            for h, value in ((0, first), (1, second)):
                extra_ref[c, 2 * p + h] = jnp.concatenate(split(value), axis=0)


def extra_part(adv_l, adv_r):
    _, pairs, _, rows = adv_l.shape
    return pl.pallas_call(
        functools.partial(extra_kernel, pairs),
        in_specs=[vmem()] * 2,
        out_specs=vmem(),
        out_shape=pltpu.VMEM((3, 2 * pairs, 16, rows), BF16),
        compiler_params=limit(4),
        cost_estimate=cost(10 * adv_l.size),
        name="extra_part",
    )(adv_l, adv_r)


def read(ref):
    return (ref[0:96, :], ref[96:192, :]) + tuple(ref[192 + t : 193 + t, :] for t in range(4))


def write(ref, run):
    ref[0:96, :] = run[0]
    ref[96:192, :] = run[1]
    for t in range(4):
        ref[192 + t : 193 + t, :] = run[2 + t]
    ref[196:200, :] = jnp.zeros((4, 128), F32)


def join(lower, upper):
    f1, l1, pf1, pl1, qf1, ql1 = lower
    f2, l2, pf2, pl2, qf2, ql2 = upper
    inverse = 1.0 / (1.0 - pf2 * ql1)
    over, under = qf1 * inverse, pl2 * inverse
    return (
        f1 + over * (f2 + pf2 * l1),
        l2 + under * (l1 + ql1 * f2),
        pf1 + over * pf2 * pl1,
        under * pl1,
        over * qf2,
        ql2 + under * ql1 * qf2,
    )


def empty():
    zero, one, none = (jnp.zeros((1, 128), F32), jnp.ones((1, 128), F32), jnp.zeros((96, 128), F32))
    return (none, none, zero, one, one, zero)


def join_kernel(bit, opening, closing, token, all_ref, other_ref, *refs):
    me = lax.axis_index("gy")
    if opening:
        lower_in = upper_in = None
        all_out, lower_out, upper_out = refs[:3]
    else:
        lower_in, upper_in, all_out, lower_out, upper_out = refs[:5]
    lower = empty() if opening else read(lower_in)
    upper = empty() if opening else read(upper_in)
    whole, other = read(all_ref), read(other_ref)

    def send(run):
        if closing:
            above_me = (me & (2 * bit)) != 0
            all_out[0:96, :] = jnp.where(above_me, run[0], run[1])
            all_out[96:104, :] = jnp.broadcast_to(jnp.where(above_me, run[2], run[5]), (8, 128))
        else:
            write(all_out, run)

    @pl.when((me & bit) != 0)
    def _():
        send(join(other, whole))
        write(lower_out, join(other, lower))
        write(upper_out, upper)

    @pl.when((me & bit) == 0)
    def _():
        send(join(whole, other))
        write(lower_out, lower)
        write(upper_out, join(upper, other))


def join_runs(bit, closing, token, whole, other, around):
    run = jax.ShapeDtypeStruct((200, 128), F32)
    half = jax.ShapeDtypeStruct((104, 128), F32)
    return pl.pallas_call(
        functools.partial(join_kernel, bit, not around, closing),
        in_specs=[pl.BlockSpec(memory_space=pl.ANY)] + [vmem()] * (2 + len(around)),
        out_specs=[vmem()] * 3,
        out_shape=[half if closing else run, run, run],
        compiler_params=limit(8),
        cost_estimate=cost(20 * whole.size),
        name="join_runs",
    )(token, whole, other, *around)


def couple(bit, me, load, other_ref, lower_ref, upper_ref, below_ref, above_ref):
    lower, upper = read(lower_ref), read(upper_ref)
    vector, scalar = other_ref[0:96, :], other_ref[96:97, :]
    none, zero = jnp.zeros((96, 128), F32), jnp.zeros((1, 128), F32)

    def solve(lower, upper):
        _, a, _, _, _, r = lower
        b, _, q, _, _, _ = upper
        first, last, psi_f, psi_l, phi_f, phi_l = read(load)
        share = 1.0 / (1.0 - psi_f * r)
        a_next = last + psi_l * a + psi_l * r * share * (first + psi_f * a)
        r_next = phi_l + psi_l * r * share * phi_f
        above = (b + q * a_next) / (1.0 - q * r_next)
        above_ref[...] = above
        below_ref[...] = a + r * share * (first + psi_f * a + phi_f * above)

    @pl.when((me & bit) != 0)
    def _():
        solve(join((none, vector, zero, zero, zero, scalar), lower), upper)

    @pl.when((me & bit) == 0)
    def _():
        solve(lower, join(upper, (vector, none, scalar, zero, zero, zero)))


def up_kernel(start, count, block, group, token, co, adv_part, sum_part, extra_ref, rim_ref, *refs):
    n = adv_part.shape[1]
    if start:
        _, before_ref, adv_hbm, sum_ref, end_ref, adv_ref, sems = refs
        end_ref[...] = before_ref[...]
    else:
        adv_hbm, sum_ref, end_ref, adv_ref, sems = refs
        end_ref[...] = (GAMMA * co[FORWARD, pl.ds(0, 1), :]) * rim_ref[0]
    steps = count // block

    def copy(step):
        here = pl.ds(step * block, block)
        there = pl.ds(start + step * block, block)
        return pltpu.make_async_copy(adv_ref.at[:, here], adv_hbm.at[:, there], sems.at[step])

    def part(step, _):
        for c in range(3):
            acc = end_ref[c]
            for k in range(block // group):
                here = step * block + k * group
                chunk = start // group + step * (block // group) + k
                acc = jnp.where(chunk == n // (2 * group), acc + sum_part[c, n // 2 - 1], acc)
                spread = spread_planes(extra_ref[c, chunk])
                for y in range(group):
                    i = here + y
                    extra = spread[32 * y : 32 * y + 32]
                    adv_ref[c, i] = adv_part[c, start + i] * (-UNIT) + extra
                    acc = acc + (GAMMA * co[FORWARD, pl.ds(start + i, 1), :]) * extra
                    sum_ref[c, i] = sum_part[c, start + i] + acc
            end_ref[c] = acc

        if start == 0:
            @pl.when(step == 0)
            def _():
                adv_ref[:, 0] = adv_ref[:, 0] + rim_ref[0]

        if start + count == n:
            @pl.when(step == steps - 1)
            def _():
                adv_ref[:, count - 1] = adv_ref[:, count - 1] + rim_ref[1]
                sum_ref[:, count - 1] = sum_ref[:, count - 1] + (GAMMA * co[FORWARD, pl.ds(n - 1, 1), :]) * rim_ref[1]

        copy(step).start()
        return 0

    lax.fori_loop(0, steps, part, 0, unroll=True)

    def finish(step, _):
        copy(step).wait()
        return 0

    lax.fori_loop(0, steps, finish, 0, unroll=True)


def sweep_up(start, count, token, table, adv_part, sums, extra, rims, group, before=()):
    shape = adv_part.shape
    block = max(d for d in range(group, 17, group) if count % d == 0)
    hbm = pl.BlockSpec(memory_space=pltpu.HBM)
    part = (3, count, 32, 128)
    return pl.pallas_call(
        functools.partial(up_kernel, start, count, block, group),
        in_specs=[pl.BlockSpec(memory_space=pl.ANY), vmem()] + [vmem()] * 4 + ([hbm, vmem()] if before else []),
        out_specs=[hbm, vmem(), vmem()],
        out_shape=[jax.ShapeDtypeStruct(shape, F32), held(part), held((3, 32, 128))],
        scratch_shapes=[held(part), pltpu.SemaphoreType.DMA((count // block,))],
        input_output_aliases={6: 0} if before else {},
        compiler_params=limit(8),
        cost_estimate=cost(4 * adv_part.size, 2 * adv_part.size),
        name="sweep_up",
    )(token, table, adv_part, sums, extra, rims, *before)


def down_kernel(bit, n, block, co, load, other, lower, upper, low_ref, high_ref, u_hbm, u_ref, below_ref, above_ref,
                sems):
    steps = n // block
    couple(bit, lax.axis_index("gy"), load, other, lower, upper, below_ref, above_ref)
    below = below_ref[...].reshape(3, 32, 128)

    def copy(step):
        here = pl.ds(step * block, block)
        return pltpu.make_async_copy(u_ref.at[:, here], u_hbm.at[:, here], sems.at[step])

    def part(sum_ref, first):
        count = sum_ref.shape[1] // block

        def run(k, value):
            step = count - 1 - k
            for y in reversed(range(block)):
                i = step * block + y
                value = co[OWN, pl.ds(first + i, 1), :] * (sum_ref[:, i] + below) + co[NEXT, pl.ds(first + i, 1), :] * value
                u_ref[:, first + i] = value
            copy(first // block + step).start()
            return value

        return run

    value = above_ref[...].reshape(3, 32, 128)
    cut = low_ref.shape[1]
    value = lax.fori_loop(0, (n - cut) // block, part(high_ref, cut), value)
    lax.fori_loop(0, cut // block, part(low_ref, 0), value)

    def finish(step, _):
        copy(step).wait()
        return 0

    lax.fori_loop(0, steps, finish, 0)


def sweep_down(bit, table, load, other, around, sums, block):
    n = sums[0].shape[1] + sums[1].shape[1]
    shape = (3, n, 32, 128)
    return pl.pallas_call(
        functools.partial(down_kernel, bit, n, block),
        in_specs=[vmem()] + [vmem()] * 6,
        out_specs=pl.BlockSpec(memory_space=pltpu.HBM),
        out_shape=jax.ShapeDtypeStruct(shape, F32),
        scratch_shapes=[held(shape), held((96, 128)), held((96, 128)), pltpu.SemaphoreType.DMA((n // block,))],
        compiler_params=limit(12),
        cost_estimate=cost(12 * sums[0].size, 8 * sums[0].size),
        name="sweep_down",
    )(table, load, other, *around, *sums)


def shards(velocity, old_advection, lower_gap, upper_gap):
    n = velocity.shape[1]
    group = max(d for d in range(1, 9) if n % (2 * d) == 0)
    block = 2 * group
    nx, ny = lax.axis_size("gx"), lax.axis_size("gy")
    ring = [(i, (i + 1) % nx) for i in range(nx)]
    pairs = [(i, i ^ 1) for i in range(ny)]
    others = [(i, j) for k in range(1, ny - 1, 2) for i, j in ((k, k + 1), (k + 1, k))]

    vel, pair, left, right = pack(velocity, group)
    from_left = lax.ppermute(right, "gx", ring)
    from_right = lax.ppermute(left, "gx", [(j, i) for i, j in ring])
    table, wide, near, far = coefs(lower_gap, upper_gap, vel, group)
    near = lax.ppermute(near, "gy", pairs)
    far = lax.ppermute(far, "gy", others)
    adv_part, sums, b_sum = main_part(vel, pair, old_advection, table, group, block)
    *adv_edges, rims, load = edge_part(
        from_left, from_right, left, right, sums, b_sum, wide, near, far, vel, table, group
    )
    bits = [1 << t for t in range(ny.bit_length() - 1)]
    cut = group * (CUT * (n // group) // 24)
    extra = extra_part(*adv_edges)
    whole, around, token = load, [], extra
    for bit in bits:
        other = lax.ppermute(whole, "gy", [(i, i ^ bit) for i in range(ny)])
        if bit != bits[-1]:
            whole, *around = join_runs(bit, 2 * bit == bits[-1], token, whole, other, around)
        if bit == bits[0]:
            adv, low, end = sweep_up(0, cut, whole, table, adv_part, sums, extra, rims, group)
            token = end
    adv, high, _ = sweep_up(cut, n - cut, whole, table, adv_part, sums, extra, rims, group, (adv, end))
    down_block = max(d for d in range(group, 17, group) if cut % d == 0 and n % d == 0)
    return sweep_down(bits[-1], table, load, other, around, (low, high), down_block), adv


def solution(mesh):
    spec = P(None, "gy", None, "gx")
    return jax.shard_map(
        shards,
        mesh=mesh,
        in_specs=(spec, spec, P("gy"), P("gy")),
        out_specs=(spec, spec),
        check_vma=False,
    )
```

```python
import functools

import jax
import jax.numpy as jnp
import numpy as np
from jax import lax
from jax.experimental import pallas as pl
from jax.experimental.pallas import tpu as pltpu
from jax.sharding import PartitionSpec as P

STIFF = 1024
GAMMA = 5.0 / 12.0
ZETA = -17.0 / 60.0
WEIGHTS = (672.0, -168.0, 32.0, -3.0)
UNIT = 1.0 / 840.0
F32 = jnp.float32
BF16 = jnp.bfloat16
MIB = 1 << 20
CUT = 16

INV_GAP, FORWARD, BACKWARD, PSI, PHI, OWN, NEXT = range(7)


def shift_matrix(size, periodic):
    m = np.zeros((size, size), np.float32)
    for j in range(size):
        for k, w in enumerate(WEIGHTS, 1):
            for i, s in ((j + k, w), (j - k, -w)):
                if periodic:
                    m[i % size, j] += s
                elif 0 <= i < size:
                    m[i, j] += s
    return m


def split(values):
    hi = values.astype(BF16)
    return hi, (values - hi.astype(F32)).astype(BF16)


def sublanes(shape):
    return lax.broadcasted_iota(jnp.int32, shape, len(shape) - 2)


def vmem():
    return pl.BlockSpec(memory_space=pltpu.VMEM)


def limit(mib):
    return pltpu.CompilerParams(vmem_limit_bytes=mib * MIB)


def cost(flops, moved=0):
    return pl.CostEstimate(flops=int(flops), bytes_accessed=int(moved), transcendentals=0)


def held(shape):
    return pltpu.VMEM(shape, F32)


def coef_kernel(n, group, lower_ref, upper_ref, vel_ref, out_ref, wide_ref, near_ref, far_ref, gap_ref):
    width = gap_ref.shape[1]
    shape = (8, width)
    lane = lax.broadcasted_iota(jnp.int32, shape, 1)
    gap_ref[...] = jnp.ones_like(gap_ref)
    gap_ref[0:8, 0:n] = jnp.broadcast_to(lower_ref[...].reshape(1, n), (8, n))
    gap_ref[8:16, 0:n] = jnp.broadcast_to(upper_ref[...].reshape(1, n), (8, n))
    lower, upper = gap_ref[0:8, :], gap_ref[8:16, :]
    gap_sum = lower + upper
    kappa = gap_sum * (0.5 / STIFF)
    live = lane < n

    def at(values, place):
        return jnp.sum(jnp.where(lane == place, values, 0.0), axis=1, keepdims=True)

    def sweep(gap, start, backward):
        one, zero = jnp.ones(shape, F32), jnp.zeros(shape, F32)
        m = [jnp.where(live, v, w) for v, w in
             ((1.0 + gap * kappa, one), (gap, zero), (kappa, zero), (one, one))]
        s = 1
        while s < n:
            inside = lane < width - s if backward else lane >= s
            turn = width - s if backward else s
            a, b, c, d = (jnp.where(inside, pltpu.roll(v, turn, 1), w)
                          for v, w in zip(m, (one, zero, zero, one)))
            m = [m[0] * a + m[1] * c, m[0] * b + m[1] * d, m[2] * a + m[3] * c, m[2] * b + m[3] * d]
            s *= 2
        return m[0] * start + m[1]

    first, last = at(lower, 0), at(upper, n - 1)
    phi_next = sweep(upper, first, False)
    psi_next = sweep(lower, last, True)
    phi = jnp.where(lane == 0, first, pltpu.roll(phi_next, 1, 1))
    psi = jnp.where(lane == n - 1, last, pltpu.roll(psi_next, width - 1, 1))
    scale = 1.0 / at(phi_next, n - 1)
    forward, backward = phi * kappa, psi * kappa
    sub = sublanes(shape)
    table = jnp.zeros(shape, F32)
    for row, value in ((INV_GAP, (1.0 / UNIT) / gap_sum), (FORWARD, forward), (BACKWARD, backward),
                       (PSI, psi * scale), (PHI, phi * scale), (OWN, upper / phi_next), (NEXT, phi / phi_next)):
        table = jnp.where(jnp.logical_and(sub == row, live), value, table)
    high = split(table)[0]
    middle, low = split(table - high.astype(F32))
    parts = jnp.concatenate([high, middle, low, jnp.zeros_like(low)], axis=0)
    count = out_ref.shape[0]
    k = lax.broadcasted_iota(jnp.int32, (32, count * 128), 0)
    t = lax.broadcasted_iota(jnp.int32, (32, count * 128), 1) // 128
    pick = jnp.where(jnp.logical_and((k & 7) == t, k < 24), 1.0, 0.0).astype(BF16)
    rows = lax.dot_general(parts, pick, (((0,), (0,)), ((), ())), preferred_element_type=F32)
    for row in range(count):
        out_ref[row] = rows[:n, 128 * row : 128 * row + 128]

    pairs, rows = wide_ref.shape[1], wide_ref.shape[3]
    y = lax.broadcasted_iota(jnp.int32, (pairs * 8, width), 1)
    r = lax.broadcasted_iota(jnp.int32, (pairs * 8, width), 0)
    mine = y // group == (r // 8) * 2 + (r & 7) // 4
    fold = (lax.broadcasted_iota(jnp.int32, (width, rows), 0) % group
            == lax.broadcasted_iota(jnp.int32, (width, rows), 1) // 32)
    fold = jnp.where(fold, 1.0, 0.0).astype(BF16)
    for t, value in enumerate((forward, backward)):
        value = jnp.where(live, value * -GAMMA, 0.0)
        hi, lo = split(jnp.where(mine, jnp.broadcast_to(value[0:1], mine.shape), 0.0))
        spread = jnp.dot(hi, fold, preferred_element_type=F32) + jnp.dot(lo, fold, preferred_element_type=F32)
        wide_ref[t] = spread.reshape(pairs, 8, rows)

    even = (lax.axis_index("gy") & 1) == 0
    for c in range(3):
        near_ref[c, 0] = jnp.where(even, vel_ref[c, n - 1], vel_ref[c, 0])
        far_ref[c, 0] = jnp.where(even, vel_ref[c, 0], vel_ref[c, n - 1])


def coefs(lower_gap, upper_gap, vel, group):
    n = lower_gap.shape[0]
    width = -(-n // 128) * 128
    row = jax.ShapeDtypeStruct((3, 1, 32, 128), F32)
    return pl.pallas_call(
        functools.partial(coef_kernel, n, group),
        in_specs=[vmem()] * 3,
        out_specs=[vmem()] * 4,
        out_shape=[held((NEXT + 1, n, 128)), held((2, n // (2 * group), 8, group * 32)), row, row],
        scratch_shapes=[held((16, width))],
        compiler_params=limit(4),
        cost_estimate=cost(1e5),
        name="coefficients",
    )(lower_gap, upper_gap, vel)


def pack_kernel(group, v_hbm, vel, pair_ref, left_ref, right_ref, sems):
    n = vel.shape[1]
    pairs = n // (2 * group)

    cuts = [2, 2, 2, 2, 2, 2] if pairs == 12 else [1] * pairs
    starts = [sum(cuts[:k]) for k in range(len(cuts))]

    def copy(k):
        rows = pl.ds(starts[k] * 2 * group, cuts[k] * 2 * group)
        return pltpu.make_async_copy(v_hbm.at[:, rows], vel.at[:, rows], sems.at[k])

    for k in range(len(cuts)):
        copy(k).start()
    rows = group * 32
    low = sublanes((8, rows)) < 4
    r = lax.broadcasted_iota(jnp.int32, (16, 256), 0)
    lane = lax.broadcasted_iota(jnp.int32, (16, 256), 1) & 127
    inside = jnp.logical_or(r < 4, r >= 12)
    pick = jnp.where(lane == jnp.where(inside, 124, 0) + (r & 3), 1.0, 0.0).astype(BF16)
    for p in range(pairs):
        if p in starts:
            copy(starts.index(p)).wait()
        for c in range(3):
            picked = []
            for h in range(2):
                f = vel[c, pl.ds((2 * p + h) * group, group)].reshape(rows, 128)
                pair = jnp.concatenate(split(f), axis=1)
                pair_ref[c, pl.ds((2 * p + h) * rows, rows), :] = pair
                picked.append(
                    lax.dot_general(pick, pair, (((1,), (1,)), ((), ())), preferred_element_type=F32)
                )
            one, two = picked
            right_ref[c, p] = jnp.where(low, one[:8], two[8:])
            left_ref[c, p] = jnp.where(low, one[8:], two[:8])


def pack(velocity, group):
    n = velocity.shape[1]
    pairs = n // (2 * group)
    packed = jax.ShapeDtypeStruct((3, pairs, 8, group * 32), F32)
    return pl.pallas_call(
        functools.partial(pack_kernel, group),
        in_specs=[pl.BlockSpec(memory_space=pltpu.HBM)],
        out_specs=[vmem()] * 4,
        out_shape=[held(velocity.shape), pltpu.VMEM((3, n * 32, 256), BF16), packed, packed],
        scratch_shapes=[pltpu.SemaphoreType.DMA((pairs,))],
        compiler_params=limit(8),
        cost_estimate=cost(velocity.size, 4 * velocity.size),
        name="pack_edges",
    )(pltpu.with_memory_space_constraint(velocity, pltpu.HBM))


def main_plain(n, block, group, co, vel_ref, pair_ref, old_hbm, dx_ref, dz_ref, adv_ref, sum_ref, b_ref, old_ref, a_ref, w_ref, sems):
    steps = n // block
    rows = group * 32

    def copy(step):
        here = pl.ds(step * block, block)
        return pltpu.make_async_copy(old_hbm.at[:, here], old_ref.at[:, here], sems.at[step])

    for step in range(steps):
        copy(step).start()
    b_ref[...] = jnp.zeros_like(b_ref)

    def part(step, _):
        copy(step).wait()
        for k in range(block // group):
            i0 = step * block + k * group
            vel = [vel_ref[c, pl.ds(i0, group)].reshape(rows, 128) for c in range(3)]
            for c in range(3):
                f = vel[c]
                pair = pair_ref[c, pl.ds(i0 * 32, rows), :]
                along_x = jnp.dot(pair, dx_ref[...], preferred_element_type=F32)
                both = jnp.dot(dz_ref[...], pair, preferred_element_type=F32)
                along_z = both[:, :128] + both[:, 128:]
                below = jnp.where(i0 == 0, 0.0, vel_ref[c, jnp.maximum(i0 - 1, 0)])
                above = jnp.where(i0 == n - group, 0.0, vel_ref[c, jnp.minimum(i0 + group, n - 1)])
                up = jnp.where(jnp.logical_or(i0 == 0, i0 == n // 2), 0.0, a_ref[c])
                down = b_ref[c]
                for y in range(group):
                    here = slice(32 * y, 32 * y + 32)
                    i = i0 + y
                    under = below if y == 0 else f[32 * y - 32 : 32 * y]
                    over = above if y == group - 1 else f[32 * y + 32 : 32 * y + 64]
                    flat = vel[0][here] * along_x[here] + vel[2][here] * along_z[here]
                    adv = flat + vel[1][here] * ((over - under) * co[INV_GAP, pl.ds(i, 1), :])
                    force = f[here] + (-UNIT * GAMMA) * adv + ZETA * old_ref[c, i]
                    up = up + co[FORWARD, pl.ds(i, 1), :] * force
                    down = down + co[BACKWARD, pl.ds(i, 1), :] * force
                    adv_ref[c, i] = adv
                    sum_ref[c, i] = up
                a_ref[c] = up
                b_ref[c] = down
        return 0

    lax.fori_loop(0, steps, part, 0)


def main_kernel(n, block, group, co, vel_ref, pair_ref, old_ref, dx_ref, dz_ref, adv_ref, sum_ref, b_ref,
                a_ref, w_ref):
    pairs = n // (2 * group)
    half = n // 2
    rows = group * 32
    pieces = 4
    high = rows // pieces

    a_ref[...] = jnp.zeros_like(a_ref)
    b_ref[...] = jnp.zeros_like(b_ref)

    def run(*accs):
        def issue(p, c, first=False):
            parts = [pair_ref[c, pl.ds((h * half + p * group) * 32, rows), :] for h in range(2)]
            sides = [jnp.concatenate([part[:, 128 * t : 128 * t + 128] for part in parts], axis=1) for t in range(2)]
            for t in range(2):
                here = slice(t * rows // 2, (t + 1) * rows // 2)
                pltpu.matmul_push_rhs(jnp.concatenate([side[here] for side in sides], axis=0), t, 1)
            for t in range(2):
                for q in range(pieces):
                    fresh = 0 if first and t == 0 and q == 0 else None
                    pltpu.matmul_acc_lhs(accs[c * 8 + q], sides[t][q * high : (q + 1) * high], load_staged_rhs=fresh)
                for q in range(2 * t, 2 * t + 2):
                    here = slice((q % 2) * high, (q % 2 + 1) * high)
                    pltpu.matmul_acc_lhs(accs[c * 8 + 4 + q], dz_ref[here, :], load_staged_rhs=t if q % 2 == 0 else None)

        def scale(p):
            for h in range(2):
                for y in range(group):
                    i = h * half + p * group + y
                    w_ref[h, y] = vel_ref[1, i] * co[INV_GAP, pl.ds(i, 1), :]

        def points(p, c):
            up = [a_ref[h, c] for h in range(2)]
            down = b_ref[c]
            for q in range(pieces):
                along_x = pltpu.matmul_pop(accs[c * 8 + q])
                along_z = pltpu.matmul_pop(accs[c * 8 + 4 + q])
                for h in range(2):
                    lanes = slice(128 * h, 128 * h + 128)
                    for k in range(group // pieces):
                        y = q * (group // pieces) + k
                        i = h * half + p * group + y
                        here = slice(32 * k, 32 * k + 32)
                        under = vel_ref[c, jnp.maximum(i - 1, 0)]
                        over = vel_ref[c, jnp.minimum(i + 1, n - 1)]
                        if h == 0 and y == 0:
                            under = jnp.where(p == 0, 0.0, under)
                        if h == 1 and y == group - 1:
                            over = jnp.where(p == pairs - 1, 0.0, over)
                        adv = vel_ref[0, i] * along_x[here, lanes] + vel_ref[2, i] * along_z[here, lanes]
                        adv = adv + w_ref[h, y] * (over - under)
                        force = vel_ref[c, i] + (-UNIT * GAMMA) * adv + ZETA * old_ref[c, i]
                        up[h] = up[h] + co[FORWARD, pl.ds(i, 1), :] * force
                        down = down + co[BACKWARD, pl.ds(i, 1), :] * force
                        adv_ref[c, i] = adv
                        sum_ref[c, i] = up[h]
            for h in range(2):
                a_ref[h, c] = up[h]
            b_ref[c] = down

        pltpu.matmul_push_rhs(dx_ref[...], 0, 0)
        for c in range(3):
            issue(0, c, c == 0)

        def part(p, _):
            scale(p)
            for c in range(3):
                points(p, c)
                issue(p + 1, c)
            return 0

        lax.fori_loop(0, pairs - 2, part, 0, unroll=2)
        part(pairs - 2, 0)
        scale(pairs - 1)
        for c in range(3):
            points(pairs - 1, c)

    pl.run_scoped(run, *(pltpu.ACC(unit)((high, 256), F32) for _ in range(3) for unit in range(2) for _ in range(pieces)))


def main_part(vel, pair, old, table, group, block):
    n = vel.shape[1]
    both_units = group == 8
    dx = shift_matrix(128, False)
    dx = np.kron(np.eye(2), dx) if both_units else np.concatenate([dx, dx])
    dz = np.kron(np.eye(group // 2 if both_units else group), shift_matrix(32, True).T)
    dz = jnp.asarray(np.concatenate([dz, dz], axis=1) if both_units else dz, BF16)
    return pl.pallas_call(
        functools.partial(main_kernel if both_units else main_plain, n, block, group),
        in_specs=[vmem(), vmem(), vmem(), vmem() if both_units else pl.BlockSpec(memory_space=pltpu.HBM), vmem(), vmem()],
        out_specs=[vmem()] * 3,
        out_shape=[held(vel.shape), held(vel.shape), held((3, 32, 128))],
        scratch_shapes=[held((2, 3, 32, 128)), held((2, group, 32, 128))] if both_units else [
            held(vel.shape), held((3, 32, 128)), held((2, group, 32, 128)), pltpu.SemaphoreType.DMA((n // group,))],
        compiler_params=limit(6),
        cost_estimate=cost(25 * old.size, 4 * old.size),
        name="inner_part",
    )(table, vel, pair, old if both_units else pltpu.with_memory_space_constraint(old, pltpu.HBM), jnp.asarray(dx, BF16), dz)


def place_matrix():
    r = lax.broadcasted_iota(jnp.int32, (16, 128), 0) & 7
    lane = lax.broadcasted_iota(jnp.int32, (16, 128), 1)
    return jnp.where(lane == jnp.where(r < 4, r, r + 120), 1.0, 0.0).astype(BF16)


def spread_planes(value):
    return lax.dot_general(value, place_matrix(), (((0,), (0,)), ((), ())), preferred_element_type=F32)


def edge_kernel(pairs, group, co, from_left, from_right, left_ref, right_ref, sum_ref, b_ref, wide_ref,
                near_ref, far_ref, vel_ref, adv_l, adv_r, rim_ref, load_ref):
    even = (lax.axis_index("gy") & 1) == 0
    n = 2 * pairs * group
    rows = group * 32
    shape = (pairs, 8, rows)
    sub = sublanes((1, 8, rows))
    low = sub[0] < 4
    quarter = sub & 3

    def swap(x):
        return pltpu.roll(x, 4, 0)

    def total(x):
        t = x[0]
        for p in range(1, pairs):
            t = t + x[p]
        t = t + swap(t)
        parts = t[:, 0:32]
        for y in range(1, group):
            parts = parts + t[:, 32 * y : 32 * y + 32]
        return parts

    for c in range(3):
        below = jnp.where(even, far_ref[c, 0], near_ref[c, 0])
        above = jnp.where(even, near_ref[c, 0], far_ref[c, 0])
        rims = (vel_ref[1, 0] * below * (UNIT * co[INV_GAP, pl.ds(0, 1), :]),
                -vel_ref[1, n - 1] * above * (UNIT * co[INV_GAP, pl.ds(n - 1, 1), :]))
        rim_ref[0, c], rim_ref[1, c] = rims
        adv, totals = [], []
        for side, halo, own in ((0, from_left, left_ref), (1, from_right, right_ref)):
            h = halo[c]
            slope = None
            for d in range(4):
                w = WEIGHTS[3 - d] * UNIT
                if side == 0:
                    weight = jnp.where(quarter + d < 4, -w, 0.0)
                    turned = pltpu.roll(h, 8 - d, 1) if d else h
                else:
                    weight = jnp.where(quarter >= d, w, 0.0)
                    turned = pltpu.roll(h, d, 1) if d else h
                slope = weight * turned if slope is None else slope + weight * turned
            adv.append(own[0] * slope)
            totals.append([total(wide_ref[t] * adv[side]) for t in range(2)])
        adv_l[c], adv_r[c] = adv
        for t, (main, weight, row, i) in enumerate(
            ((b_ref[c], BACKWARD, PHI, 0), (sum_ref[c, n // 2 - 1] + sum_ref[c, n - 1], FORWARD, PSI, n - 1))
        ):
            main = main + (GAMMA * co[weight, pl.ds(0, 1), :]) * rims[0] + (GAMMA * co[weight, pl.ds(n - 1, 1), :]) * rims[1]
            value = jnp.where(low[:, :32], totals[0][1 - t], totals[1][1 - t])
            spread = spread_planes(jnp.concatenate(split(value), axis=0))
            load_ref[pl.ds(t * 96 + c * 32, 32), :] = (main + spread) * co[row, pl.ds(i, 1), :]
    row = sublanes((8, 128))
    ends = jnp.where(row == 0, co[PSI, pl.ds(0, 1), :], co[PSI, pl.ds(n - 1, 1), :])
    ends = jnp.where(row == 2, co[PHI, pl.ds(0, 1), :], ends)
    load_ref[192:200, :] = jnp.where(row == 3, co[PHI, pl.ds(n - 1, 1), :], ends)


def edge_part(from_left, from_right, left, right, sums, b_sum, wide, near, far, vel, table, group):
    pairs = left.shape[1]
    return pl.pallas_call(
        functools.partial(edge_kernel, pairs, group),
        in_specs=[vmem()] + [vmem()] * 10,
        out_specs=[vmem()] * 4,
        out_shape=[held(left.shape), held(left.shape), held((2, 3, 32, 128)),
                   jax.ShapeDtypeStruct((200, 128), F32)],
        compiler_params=limit(8),
        cost_estimate=cost(40 * left.size),
        name="edge_part",
    )(table, from_left, from_right, left, right, sums, b_sum, wide, near, far, vel)


def extra_kernel(pairs, adv_l, adv_r, extra_ref):
    low = sublanes(adv_l.shape[2:]) < 4
    for c in range(3):
        for p in range(pairs):
            l, r = -adv_l[c, p], -adv_r[c, p]
            first = jnp.where(low, l, pltpu.roll(r, 4, 0))
            second = jnp.where(low, pltpu.roll(l, 4, 0), r)
            for h, value in ((0, first), (1, second)):
                extra_ref[c, 2 * p + h] = jnp.concatenate(split(value), axis=0)


def extra_part(adv_l, adv_r):
    _, pairs, _, rows = adv_l.shape
    return pl.pallas_call(
        functools.partial(extra_kernel, pairs),
        in_specs=[vmem()] * 2,
        out_specs=vmem(),
        out_shape=pltpu.VMEM((3, 2 * pairs, 16, rows), BF16),
        compiler_params=limit(4),
        cost_estimate=cost(10 * adv_l.size),
        name="extra_part",
    )(adv_l, adv_r)


def read(ref):
    return (ref[0:96, :], ref[96:192, :]) + tuple(ref[192 + t : 193 + t, :] for t in range(4))


def write(ref, run):
    ref[0:96, :] = run[0]
    ref[96:192, :] = run[1]
    for t in range(4):
        ref[192 + t : 193 + t, :] = run[2 + t]
    ref[196:200, :] = jnp.zeros((4, 128), F32)


def join(lower, upper):
    f1, l1, pf1, pl1, qf1, ql1 = lower
    f2, l2, pf2, pl2, qf2, ql2 = upper
    inverse = 1.0 / (1.0 - pf2 * ql1)
    over, under = qf1 * inverse, pl2 * inverse
    return (
        f1 + over * (f2 + pf2 * l1),
        l2 + under * (l1 + ql1 * f2),
        pf1 + over * pf2 * pl1,
        under * pl1,
        over * qf2,
        ql2 + under * ql1 * qf2,
    )


def empty():
    zero, one, none = (jnp.zeros((1, 128), F32), jnp.ones((1, 128), F32), jnp.zeros((96, 128), F32))
    return (none, none, zero, one, one, zero)


def join_kernel(bit, opening, closing, token, all_ref, other_ref, *refs):
    me = lax.axis_index("gy")
    if opening:
        lower_in = upper_in = None
        all_out, lower_out, upper_out = refs[:3]
    else:
        lower_in, upper_in, all_out, lower_out, upper_out = refs[:5]
    lower = empty() if opening else read(lower_in)
    upper = empty() if opening else read(upper_in)
    whole, other = read(all_ref), read(other_ref)

    def send(run):
        if closing:
            above_me = (me & (2 * bit)) != 0
            all_out[0:96, :] = jnp.where(above_me, run[0], run[1])
            all_out[96:104, :] = jnp.broadcast_to(jnp.where(above_me, run[2], run[5]), (8, 128))
        else:
            write(all_out, run)

    @pl.when((me & bit) != 0)
    def _():
        send(join(other, whole))
        write(lower_out, join(other, lower))
        write(upper_out, upper)

    @pl.when((me & bit) == 0)
    def _():
        send(join(whole, other))
        write(lower_out, lower)
        write(upper_out, join(upper, other))


def join_runs(bit, closing, token, whole, other, around):
    run = jax.ShapeDtypeStruct((200, 128), F32)
    half = jax.ShapeDtypeStruct((104, 128), F32)
    return pl.pallas_call(
        functools.partial(join_kernel, bit, not around, closing),
        in_specs=[pl.BlockSpec(memory_space=pl.ANY)] + [vmem()] * (2 + len(around)),
        out_specs=[vmem()] * 3,
        out_shape=[half if closing else run, run, run],
        compiler_params=limit(8),
        cost_estimate=cost(20 * whole.size),
        name="join_runs",
    )(token, whole, other, *around)


def couple(bit, me, load, other_ref, lower_ref, upper_ref, below_ref, above_ref):
    lower, upper = read(lower_ref), read(upper_ref)
    vector, scalar = other_ref[0:96, :], other_ref[96:97, :]
    none, zero = jnp.zeros((96, 128), F32), jnp.zeros((1, 128), F32)

    def solve(lower, upper):
        _, a, _, _, _, r = lower
        b, _, q, _, _, _ = upper
        first, last, psi_f, psi_l, phi_f, phi_l = read(load)
        share = 1.0 / (1.0 - psi_f * r)
        a_next = last + psi_l * a + psi_l * r * share * (first + psi_f * a)
        r_next = phi_l + psi_l * r * share * phi_f
        above = (b + q * a_next) / (1.0 - q * r_next)
        above_ref[...] = above
        below_ref[...] = a + r * share * (first + psi_f * a + phi_f * above)

    @pl.when((me & bit) != 0)
    def _():
        solve(join((none, vector, zero, zero, zero, scalar), lower), upper)

    @pl.when((me & bit) == 0)
    def _():
        solve(lower, join(upper, (vector, none, scalar, zero, zero, zero)))


def up_kernel(start, count, block, group, token, co, adv_part, sum_part, extra_ref, rim_ref, *refs):
    n = adv_part.shape[1]
    if start:
        _, before_ref, adv_hbm, sum_ref, end_ref, adv_ref, sems = refs
        end_ref[...] = before_ref[...]
    else:
        adv_hbm, sum_ref, end_ref, adv_ref, sems = refs
        end_ref[...] = (GAMMA * co[FORWARD, pl.ds(0, 1), :]) * rim_ref[0]
    steps = count // block

    def copy(step):
        here = pl.ds(step * block, block)
        there = pl.ds(start + step * block, block)
        return pltpu.make_async_copy(adv_ref.at[:, here], adv_hbm.at[:, there], sems.at[step])

    def part(step, _):
        for c in range(3):
            acc = end_ref[c]
            for k in range(block // group):
                here = step * block + k * group
                chunk = start // group + step * (block // group) + k
                acc = jnp.where(chunk == n // (2 * group), acc + sum_part[c, n // 2 - 1], acc)
                spread = spread_planes(extra_ref[c, chunk])
                for y in range(group):
                    i = here + y
                    extra = spread[32 * y : 32 * y + 32]
                    adv_ref[c, i] = adv_part[c, start + i] * (-UNIT) + extra
                    acc = acc + (GAMMA * co[FORWARD, pl.ds(start + i, 1), :]) * extra
                    sum_ref[c, i] = sum_part[c, start + i] + acc
            end_ref[c] = acc

        if start == 0:
            @pl.when(step == 0)
            def _():
                adv_ref[:, 0] = adv_ref[:, 0] + rim_ref[0]

        if start + count == n:
            @pl.when(step == steps - 1)
            def _():
                adv_ref[:, count - 1] = adv_ref[:, count - 1] + rim_ref[1]
                sum_ref[:, count - 1] = sum_ref[:, count - 1] + (GAMMA * co[FORWARD, pl.ds(n - 1, 1), :]) * rim_ref[1]

        copy(step).start()
        return 0

    lax.fori_loop(0, steps, part, 0, unroll=True)

    def finish(step, _):
        copy(step).wait()
        return 0

    lax.fori_loop(0, steps, finish, 0, unroll=True)


def sweep_up(start, count, token, table, adv_part, sums, extra, rims, group, before=()):
    shape = adv_part.shape
    block = max(d for d in range(group, 17, group) if count % d == 0)
    hbm = pl.BlockSpec(memory_space=pltpu.HBM)
    part = (3, count, 32, 128)
    return pl.pallas_call(
        functools.partial(up_kernel, start, count, block, group),
        in_specs=[pl.BlockSpec(memory_space=pl.ANY), vmem()] + [vmem()] * 4 + ([hbm, vmem()] if before else []),
        out_specs=[hbm, vmem(), vmem()],
        out_shape=[jax.ShapeDtypeStruct(shape, F32), held(part), held((3, 32, 128))],
        scratch_shapes=[held(part), pltpu.SemaphoreType.DMA((count // block,))],
        input_output_aliases={6: 0} if before else {},
        compiler_params=limit(8),
        cost_estimate=cost(4 * adv_part.size, 2 * adv_part.size),
        name="sweep_up",
    )(token, table, adv_part, sums, extra, rims, *before)


def down_kernel(bit, n, block, co, load, other, lower, upper, low_ref, high_ref, u_hbm, u_ref, below_ref, above_ref,
                sems):
    steps = n // block
    couple(bit, lax.axis_index("gy"), load, other, lower, upper, below_ref, above_ref)
    below = below_ref[...].reshape(3, 32, 128)

    def copy(step):
        here = pl.ds(step * block, block)
        return pltpu.make_async_copy(u_ref.at[:, here], u_hbm.at[:, here], sems.at[step])

    def part(sum_ref, first):
        count = sum_ref.shape[1] // block

        def run(k, value):
            step = count - 1 - k
            for y in reversed(range(block)):
                i = step * block + y
                value = co[OWN, pl.ds(first + i, 1), :] * (sum_ref[:, i] + below) + co[NEXT, pl.ds(first + i, 1), :] * value
                u_ref[:, first + i] = value
            copy(first // block + step).start()
            return value

        return run

    value = above_ref[...].reshape(3, 32, 128)
    cut = low_ref.shape[1]
    value = lax.fori_loop(0, (n - cut) // block, part(high_ref, cut), value)
    lax.fori_loop(0, cut // block, part(low_ref, 0), value)

    def finish(step, _):
        copy(step).wait()
        return 0

    lax.fori_loop(0, steps, finish, 0)


def sweep_down(bit, table, load, other, around, sums, block):
    n = sums[0].shape[1] + sums[1].shape[1]
    shape = (3, n, 32, 128)
    return pl.pallas_call(
        functools.partial(down_kernel, bit, n, block),
        in_specs=[vmem()] + [vmem()] * 6,
        out_specs=pl.BlockSpec(memory_space=pltpu.HBM),
        out_shape=jax.ShapeDtypeStruct(shape, F32),
        scratch_shapes=[held(shape), held((96, 128)), held((96, 128)), pltpu.SemaphoreType.DMA((n // block,))],
        compiler_params=limit(12),
        cost_estimate=cost(12 * sums[0].size, 8 * sums[0].size),
        name="sweep_down",
    )(table, load, other, *around, *sums)


def shards(velocity, old_advection, lower_gap, upper_gap):
    n = velocity.shape[1]
    group = max(d for d in range(1, 9) if n % (2 * d) == 0)
    block = 2 * group
    nx, ny = lax.axis_size("gx"), lax.axis_size("gy")
    ring = [(i, (i + 1) % nx) for i in range(nx)]
    pairs = [(i, i ^ 1) for i in range(ny)]
    others = [(i, j) for k in range(1, ny - 1, 2) for i, j in ((k, k + 1), (k + 1, k))]

    vel, pair, left, right = pack(velocity, group)
    from_left = lax.ppermute(right, "gx", ring)
    from_right = lax.ppermute(left, "gx", [(j, i) for i, j in ring])
    table, wide, near, far = coefs(lower_gap, upper_gap, vel, group)
    near = lax.ppermute(near, "gy", pairs)
    far = lax.ppermute(far, "gy", others)
    adv_part, sums, b_sum = main_part(vel, pair, old_advection, table, group, block)
    *adv_edges, rims, load = edge_part(
        from_left, from_right, left, right, sums, b_sum, wide, near, far, vel, table, group
    )
    bits = [1 << t for t in range(ny.bit_length() - 1)]
    cut = group * (CUT * (n // group) // 24)
    extra = extra_part(*adv_edges)
    whole, around, token = load, [], extra
    for bit in bits:
        other = lax.ppermute(whole, "gy", [(i, i ^ bit) for i in range(ny)])
        if bit != bits[-1]:
            whole, *around = join_runs(bit, 2 * bit == bits[-1], token, whole, other, around)
        if bit == bits[0]:
            adv, low, end = sweep_up(0, cut, whole, table, adv_part, sums, extra, rims, group)
            token = end
    adv, high, _ = sweep_up(cut, n - cut, whole, table, adv_part, sums, extra, rims, group, (adv, end))
    down_block = max(d for d in range(group, 17, group) if cut % d == 0 and n % d == 0)
    return sweep_down(bits[-1], table, load, other, around, (low, high), down_block), adv


def solution(mesh):
    spec = P(None, "gy", None, "gx")
    return jax.shard_map(
        shards,
        mesh=mesh,
        in_specs=(spec, spec, P("gy"), P("gy")),
        out_specs=(spec, spec),
        check_vma=False,
    )
```
